128 devices in a mesh: batch: 8 (over x, core), seq: 16 (over y, z).
Axes of the slice: x: 4, y: 4, z: 4, core: 2. Of those that a mesh axis runs over, the one named last changes fastest.
Arguments:
- item_feats: bfloat16 [32768, 512], P(('batch', 'seq')), may hold values from -6 to 6
- item_weight: bfloat16 [512, 512], replicated, may hold values from -0.25 to 0.25
- send_rows: int32 [128, 256], P(('batch', 'seq')), may hold values from 0 to 255
- event_slot: int32 [49152], P(('batch', 'seq')), may hold values from 0 to 255
- user_blocks: int32 [8, 4], P('batch'), may hold values from 1 to 24, 48 in all within a row
- tail_len: int32 [8, 4], P('batch'), may hold values from 1 to 128
- block_order: int32 [8, 48], P('batch'), may hold values from 0 to 47, each once within a row
- gain_in: float32 [512], replicated, may hold values from 0.1 to 1.9
- gain_mid: float32 [512], replicated, may hold values from 0.1 to 1.9
- w_in: bfloat16 [512, 2048], replicated, may hold values from -0.22097087 to 0.22097087
- w_out: bfloat16 [512, 512], replicated, may hold values from -0.25 to 0.25
- cot_out: bfloat16 [49152, 512], P(('batch', 'seq')), may hold values from -6 to 6
Outputs:
- layer_out: bfloat16 [49152, 512], P(('batch', 'seq'))
- item_grad: float32 [32768, 512], P(('batch', 'seq'))
The draws below stay inside these ranges and needn't reach their ends.
Inputs may be any that keep to these rules, and one draw needn't show every extreme that they name: `user_blocks`: each batch index's 4 users fill its 48 blocks, none more than 24. `block_order`: each row holds every block once.
All inputs are finite; a program needn't handle non-finite values.
Results may differ from the reference program's by a relative error of at most 0.04.
Values may be sent and summed in bfloat16 or wider, within the bound.
A program may use at most 256 MiB of HBM per device.

```python
import math
import jax
import jax.numpy as jnp
import numpy as np
from jax import lax

D = 512
HEAD_DIM = 128
BLOCK = 128
USERS = 4
CAP = 2
ITEM_DEV = 256
ROWS = 384
BLK_GRP = 48
E_GRP = 6144
MAXB = 24
PEERS = 128
ITEMS = 32768
EVENTS = 49152
N_BATCH = 8
N_SEQ = 16


def draw_w_in(key, part):
    key = jax.random.fold_in(key, 11)
    subkeys = jax.random.split(key, 3)
    jitter = jax.random.normal(subkeys[0], (D, 4 * D), jnp.float32)
    shared = jax.random.normal(subkeys[2], (D, 2), jnp.float32)
    common = jnp.concatenate([jnp.zeros((D, 2 * D), jnp.float32), jnp.broadcast_to(shared[:, 0:1], (D, D)), jnp.broadcast_to(shared[:, 1:2], (D, D))], axis=1)
    weights = (jitter + 1.25 * common) * D ** (-0.5)
    bound_value = 5.0 * D ** (-0.5)
    return jnp.clip(weights, -bound_value, bound_value).astype(jnp.bfloat16)


def set_ends(values, own_key, least, top_value):
    longest = values.shape.index(max(values.shape))
    spots = []
    for shift in (0, 1):
        where = [jax.random.randint(jax.random.fold_in(own_key, axis), (), 0, length) for axis, length in enumerate(values.shape)]
        where[longest] = (where[longest] + shift) % values.shape[longest]
        spots.append(tuple(where))
    return values.at[spots[0]].set(least).at[spots[1]].set(top_value)


def shard_levels(own_key, shape, pieces, low, largest):
    level = 1.0
    for dim, shards_of in pieces:
        steps = jax.random.uniform(jax.random.fold_in(jax.random.fold_in(own_key, 6), dim), (shards_of,), jnp.float32, low / len(pieces), largest / len(pieces))
        level = level * jnp.repeat(jnp.exp(steps), shape[dim] // shards_of).reshape((-1,) + (1,) * (len(shape) - 1 - dim))
    return level


def split_up(amount, total, reach, skew):
    portions = [(1 << 20) // math.isqrt(rank ** skew) + 1 for rank in range(2, amount + 1)]
    rest, holding = total - reach - (amount - 1), [1] * (amount - 1)
    while rest > 0:
        movable = [i for i in range(amount - 1) if holding[i] < reach]
        mass, remaining = sum([portions[i] for i in movable]), rest
        for i in movable:
            addition = min(reach - holding[i], max(1, remaining * portions[i] // mass), rest)
            holding[i] = holding[i] + addition
            rest = rest - addition
    return np.array([reach] + holding)


def uneven(rng, count, total, most, skew):
    if count == 2:
        one = jax.random.randint(rng, (), max(1, total - most), min(most, total - 1) + 1)
        return jnp.stack([one, total - one])
    tallies = jnp.asarray(split_up(count, total, most, skew), jnp.int32)
    couples = (count - 1) // 2
    source_of, receiver = tallies[1:1 + 2 * couples:2], tallies[2:2 + 2 * couples:2]
    margin = jnp.minimum(source_of - 1, most - receiver)
    passed = jax.random.randint(jax.random.fold_in(rng, 1), (couples,), 0, 1 << 20) % (margin + 1)
    tallies = tallies.at[1:1 + 2 * couples:2].set(source_of - passed).at[2:2 + 2 * couples:2].set(receiver + passed)
    return tallies[jax.random.permutation(jax.random.fold_in(rng, 2), count)]


def scatter_about(stream_key, shape, scale, limit, cuts=(), held_as=jnp.bfloat16):
    drawn = scale * jax.random.normal(stream_key, shape, jnp.float32)
    if cuts:
        drawn = drawn * shard_levels(stream_key, shape, cuts, -0.22, 0.18)
    return jnp.clip(drawn, -limit, limit).astype(held_as)


def setup_inputs(seed: int = 0) -> dict:
    key_of = jax.random.split(jax.random.key(seed), 13)
    return {
        "item_feats": scatter_about(key_of[0], (ITEMS, D), 1.0, 6.0, ((0, 128),)),
        "item_weight": scatter_about(key_of[1], (D, D), D ** -0.5, 0.25),
        "send_rows": set_ends(jax.random.randint(key_of[2], (PEERS, PEERS * CAP), 0, ITEM_DEV), jax.random.fold_in(key_of[2], 1), 0, ITEM_DEV - 1).astype(jnp.int32),
        "event_slot": set_ends(jax.random.randint(key_of[3], (EVENTS,), 0, PEERS * CAP), jax.random.fold_in(key_of[3], 1), 0, (PEERS * CAP) - 1).astype(jnp.int32),
        "user_blocks": jax.vmap(lambda own: uneven(own, USERS, BLK_GRP, MAXB, 2))(jax.random.split(key_of[4], N_BATCH)).reshape((N_BATCH, USERS)).astype(jnp.int32),
        "tail_len": set_ends(jax.random.randint(key_of[5], (N_BATCH, USERS), 1, BLOCK + 1), jax.random.fold_in(key_of[5], 1), 1, BLOCK).astype(jnp.int32),
        "block_order": jax.vmap(lambda own: jax.random.permutation(own, BLK_GRP))(jax.random.split(key_of[6], N_BATCH)).reshape((N_BATCH, BLK_GRP)).astype(jnp.int32),
        "gain_in": jnp.clip(1.0 + 0.18 * jax.random.normal(key_of[7], (D,), jnp.float32), 0.1, 1.9),
        "gain_mid": jnp.clip(1.0 + 0.18 * jax.random.normal(key_of[8], (D,), jnp.float32), 0.1, 1.9),
        "w_in": draw_w_in(jax.random.fold_in(key_of[12], 71), 0),
        "w_out": scatter_about(key_of[10], (D, D), D ** -0.5, 0.25),
        "cot_out": scatter_about(key_of[11], (EVENTS, D), 1.0, 6.0, ((0, 128),)),
    }


def layer_norm(values, gain):
    mean = lax.optimization_barrier(jnp.mean(values, axis=-1, keepdims=True))
    centred = values - mean
    spread = lax.optimization_barrier(jnp.mean(centred * centred, axis=-1, keepdims=True))
    return centred * lax.rsqrt(spread + 1e-05) * gain

def norm_back(values, gain, upstream):
    mean = lax.optimization_barrier(jnp.mean(values, axis=-1, keepdims=True))
    centred = values - mean
    spread = lax.optimization_barrier(jnp.mean(centred * centred, axis=-1, keepdims=True))
    inverse = lax.rsqrt(spread + 1e-05)
    normal = centred * inverse
    scaled = upstream * gain
    return inverse * (scaled - lax.optimization_barrier(jnp.mean(scaled, axis=-1, keepdims=True)) - normal * lax.optimization_barrier(jnp.mean(scaled * normal, axis=-1, keepdims=True)))

def silu_slope(pre):
    sig = jax.nn.sigmoid(pre)
    return sig * (1.0 + pre * (1.0 - sig))

def event_meta(lengths_row, tails_row, order_row, block):
    users = lengths_row.shape[0]
    ends = jnp.cumsum(lengths_row).astype(jnp.int32)
    starts = (ends - lengths_row).astype(jnp.int32)
    user_of = lax.optimization_barrier(jnp.sum((order_row[:, None] >= ends[None, :]).astype(jnp.int32), axis=1)).astype(jnp.int32)
    onehot = (user_of[:, None] == jnp.arange(users, dtype=jnp.int32)[None, :]).astype(jnp.int32)
    start_of = lax.optimization_barrier(jnp.sum(onehot * starts[None, :], axis=1)).astype(jnp.int32)
    count_of = lax.optimization_barrier(jnp.sum(onehot * lengths_row[None, :], axis=1)).astype(jnp.int32)
    tail_of = lax.optimization_barrier(jnp.sum(onehot * tails_row[None, :], axis=1)).astype(jnp.int32)
    rank = order_row - start_of
    offsets = jnp.arange(block, dtype=jnp.int32)
    position = rank[:, None] * block + offsets[None, :]
    valid = (rank[:, None] < count_of[:, None] - 1) | (offsets[None, :] < tail_of[:, None])
    user = jnp.broadcast_to(user_of[:, None], (order_row.shape[0], block))
    return (user.reshape(-1), position.reshape(-1).astype(jnp.int32), valid.reshape(-1))

def visible_mask(user_q, pos_q, user_k, pos_k, valid_k):
    return (user_q[:, None] == user_k[None, :]) & (pos_k[None, :] <= pos_q[:, None]) & valid_k[None, :]

def attend(query, key, value, mask, head_dim):
    scale = head_dim ** (-0.5)
    outputs = []
    for head in range(query.shape[1] // head_dim):
        cols = slice(head * head_dim, (head + 1) * head_dim)
        scores = jnp.dot(query[:, cols], key[:, cols].T, preferred_element_type=jnp.float32) * scale
        weights = jnp.where(mask, scores * jax.nn.sigmoid(scores), 0.0).astype(jnp.bfloat16)
        outputs.append(jnp.dot(weights, value[:, cols], preferred_element_type=jnp.float32))
    return jnp.concatenate(outputs, axis=1)

def attend_back(query, key, value, d_mixed, mask, head_dim):
    scale = head_dim ** (-0.5)
    d_query, d_key, d_value = ([], [], [])
    for head in range(query.shape[1] // head_dim):
        cols = slice(head * head_dim, (head + 1) * head_dim)
        scores = jnp.dot(query[:, cols], key[:, cols].T, preferred_element_type=jnp.float32) * scale
        sig = jax.nn.sigmoid(scores)
        weights = jnp.where(mask, scores * sig, 0.0).astype(jnp.bfloat16)
        d_value.append(jnp.dot(weights.T, d_mixed[:, cols], preferred_element_type=jnp.float32))
        d_weights = jnp.dot(d_mixed[:, cols], value[:, cols].T, preferred_element_type=jnp.float32)
        d_scores = jnp.where(mask, d_weights * sig * (1.0 + scores * (1.0 - sig)), 0.0).astype(jnp.bfloat16)
        d_query.append(jnp.dot(d_scores, key[:, cols], preferred_element_type=jnp.float32) * scale)
        d_key.append(jnp.dot(d_scores.T, query[:, cols], preferred_element_type=jnp.float32) * scale)
    return (jnp.concatenate(d_query, axis=1), jnp.concatenate(d_key, axis=1), jnp.concatenate(d_value, axis=1))

def layer_group(tokens, cot, user, position, valid, gain_in, gain_mid, w_in, w_out):
    width = w_out.shape[0]
    x_full = tokens.astype(jnp.float32)
    normed = layer_norm(x_full, gain_in).astype(jnp.bfloat16)
    pre = jnp.dot(normed, w_in, preferred_element_type=jnp.float32)
    hidden = jax.nn.silu(pre).astype(jnp.bfloat16)
    gate = hidden[:, :width]
    value = hidden[:, width:2 * width]
    query = hidden[:, 2 * width:3 * width]
    key = hidden[:, 3 * width:]

    def slice_rows(array, index):
        return lax.dynamic_slice_in_dim(array, (index * ROWS).astype(jnp.int32), ROWS, 0)

    def mask_for(index):
        return visible_mask(slice_rows(user, index), slice_rows(position, index), user, position, valid)

    def forward_set(index):
        return attend(slice_rows(query, index), key, value, mask_for(index), HEAD_DIM)
    mixed = lax.map(forward_set, jnp.arange(N_SEQ, dtype=jnp.int32)).reshape(-1, width)
    normed_mid = layer_norm(mixed, gain_mid)
    gated = (normed_mid * gate.astype(jnp.float32)).astype(jnp.bfloat16)
    out = (x_full + jnp.dot(gated, w_out, preferred_element_type=jnp.float32)).astype(jnp.bfloat16)
    d_gated = jnp.dot(cot, w_out.T, preferred_element_type=jnp.float32).astype(jnp.bfloat16)
    d_gate = d_gated.astype(jnp.float32) * normed_mid
    d_mixed = norm_back(mixed, gain_mid, d_gated.astype(jnp.float32) * gate.astype(jnp.float32)).astype(jnp.bfloat16)

    def back_set(carry, index):
        d_query, d_key, d_value = attend_back(slice_rows(query, index), key, value, slice_rows(d_mixed, index), mask_for(index), HEAD_DIM)
        return ((carry[0] + d_key, carry[1] + d_value), d_query)
    zeros = jnp.zeros((tokens.shape[0], width), jnp.float32)
    sums, d_queries = lax.scan(back_set, (zeros, zeros), jnp.arange(N_SEQ, dtype=jnp.int32))
    d_hidden = jnp.concatenate([d_gate, sums[1], d_queries.reshape(-1, width), sums[0]], axis=1)
    d_pre = (d_hidden * silu_slope(pre)).astype(jnp.bfloat16)
    d_normed = jnp.dot(d_pre, w_in.T, preferred_element_type=jnp.float32)
    d_tokens = cot.astype(jnp.float32) + norm_back(x_full, gain_in, d_normed)
    return (out, d_tokens)

def reference(item_feats, item_weight, send_rows, event_slot, user_blocks, tail_len, block_order, gain_in, gain_mid, w_in, w_out, cot_out):
    item_pre = jnp.dot(item_feats, item_weight, preferred_element_type=jnp.float32)
    embedded = jax.nn.silu(item_pre).astype(jnp.bfloat16)
    events = jnp.arange(EVENTS, dtype=jnp.int32)
    reader = (events // ROWS).astype(jnp.int32)
    source = (event_slot // CAP).astype(jnp.int32)
    which = (event_slot % CAP).astype(jnp.int32)
    local = send_rows[source, reader * CAP + which]
    item_id = (source * ITEM_DEV + local).astype(jnp.int32)
    tokens = embedded[item_id]

    def group(inputs):
        group_tokens, group_cot, lengths_row, tails_row, order_row = inputs
        user, position, valid = event_meta(lengths_row, tails_row, order_row, BLOCK)
        return layer_group(group_tokens, group_cot, user, position, valid, gain_in, gain_mid, w_in, w_out)
    outs, d_tokens = lax.map(group, (tokens.reshape(N_BATCH, E_GRP, D), cot_out.reshape(N_BATCH, E_GRP, D), user_blocks, tail_len, block_order))
    d_embedded = jax.ops.segment_sum(d_tokens.reshape(EVENTS, D), item_id, num_segments=ITEMS)
    d_item = (d_embedded * silu_slope(item_pre)).astype(jnp.bfloat16)
    item_grad = jnp.dot(d_item, item_weight.T, preferred_element_type=jnp.float32)
    return (outs.reshape(EVENTS, D), item_grad)
```

```python
import jax
import jax.numpy as jnp
from jax import lax
from jax.experimental import pallas as pl
from jax.experimental.pallas import tpu as pltpu
from jax.sharding import PartitionSpec as P

WIDTH = 512
HEAD = 128
HEADS = 4
BLOCK = 128
BLOCKS = 48
SEQ = 16
GROUPS = 8
PIECE = 32
TILES = 12
HALF = 192
ROWS = 384
FAR = 1 << 20
SCALE = HEAD**-0.5
MESH = pl.DeviceIdType.MESH
F32 = jnp.float32
BF16 = jnp.bfloat16


def dot_nn(a, b):
    return jnp.dot(a, b, preferred_element_type=F32)


def dot_nt(a, b):
    return lax.dot_general(a, b, (((1,), (1,)), ((), ())), preferred_element_type=F32)


def dot_tn(a, b):
    return lax.dot_general(a, b, (((0,), (0,)), ((), ())), preferred_element_type=F32)


def silu(v):
    u = 0.5 * v
    return u + u * jnp.tanh(u)


def silu_slope(v):
    u = 0.5 * v
    t = jnp.tanh(u)
    a = 1.0 + t
    return 0.5 * (a + u * a * (1.0 - t))


def normalize(values):
    mean = jnp.mean(values, axis=-1, keepdims=True)
    centred = values - mean
    spread = jnp.mean(centred * centred, axis=-1, keepdims=True)
    inverse = lax.rsqrt(spread + 1e-05)
    return centred * inverse, inverse


def iota(shape, dim):
    return lax.broadcasted_iota(jnp.int32, shape, dim)


def place():
    b, s = lax.axis_index("batch"), lax.axis_index("seq")
    return b, s, b // 2, b % 2, s // 4, s % 4


def worker_at(w, x, c):
    head, half, core = w % 4, (w // 4) % 2, w // 8
    return head, half, core, x * 2 + core, (2 * c + half) * 4 + head


def copy_to(src, dst, send, recv, batch, seq):
    return pltpu.make_async_remote_copy(
        src_ref=src, dst_ref=dst, send_sem=send, recv_sem=recv, device_id=(batch, seq), device_id_type=MESH
    )


def arrived(ref, sem):
    pltpu.make_async_copy(ref, ref, sem).wait()


def rows_of(index, size):
    return pl.ds(pl.multiple_of(index * size, size), size)


def slot_onehot(event_slot):
    e = event_slot
    wanted = ((e >> 1) & 15) * 16 + (e >> 5) * 2 + (e & 1)
    return (iota((256, ROWS), 0) == wanted).astype(BF16)


def by_seq():
    i, j = iota((256, 256), 0), iota((256, 256), 1)
    return (j == ((i >> 1) & 7) * 32 + (i >> 4) * 2 + (i & 1)).astype(BF16)


def by_batch():
    i, j = iota((256, 256), 0), iota((256, 256), 1)
    return (j == ((i >> 1) & 15) * 16 + (i >> 5) * 2 + (i & 1)).astype(BF16)


def exchange_batch(src, dst, send, recv, b, s):
    copies = []
    for k in range(1, GROUPS):
        peer = lax.rem(b + k, GROUPS)
        copy = copy_to(src.at[rows_of(peer, 32)], dst.at[rows_of(b, 32)], send.at[k], recv.at[k], peer, s)
        copy.start()
        copies.append(copy)
    dst[rows_of(b, 32), :] = src[rows_of(b, 32), :]
    return copies


def exchange_seq(src, dst, send, recv, b, s):
    copies = []
    for k in range(1, SEQ):
        peer = lax.rem(s + k, SEQ)
        copy = copy_to(src.at[rows_of(peer, 16)], dst.at[rows_of(s, 16)], send.at[k], recv.at[k], b, peer)
        copy.start()
        copies.append(copy)
    dst[rows_of(s, 16), :] = src[rows_of(s, 16), :]
    return copies


def wait_all(copies):
    for copy in copies:
        copy.wait()


def send_kernel(
    feats, item_weight, send_rows, event_slot, user_blocks, tail_len, block_order, gain_in, gain_mid, w_in, w_out, cot,
    kv_out, qp_out, tokens_out, meta_out,
    out1, in1, out2, in2, kv, qp, meta_own, meta_other,
    send1, recv1, send2, recv2, kv_send, kv_recv, pass_send, pass_recv, qp_send, qp_recv, meta_send, meta_recv,
):
    b, s, x, c, y, z = place()
    partner = x * 2 + 1 - c
    mine = y // 2

    embedded = silu(dot_nn(feats[...], item_weight[...])).astype(BF16)
    wanted = (iota((256, 256), 0) == send_rows[...]).astype(BF16)
    out1[...] = dot_tn(wanted, embedded).astype(BF16)
    first = exchange_batch(out1, in1, send1, recv1, b, s)

    meta_own[...] = jnp.zeros_like(meta_own)
    meta_own[0:1, 0:48] = block_order[...]
    meta_own[1:2, 0:4] = user_blocks[...]
    meta_own[2:3, 0:4] = tail_len[...]
    meta_copy = copy_to(meta_own, meta_other, meta_send, meta_recv, partner, s)
    meta_copy.start()

    d_gated = dot_nt(cot[...], w_out[...]).astype(BF16)
    wait_all(first)
    out2[...] = dot_nn(by_seq(), in1[...]).astype(BF16)
    second = exchange_seq(out2, in2, send2, recv2, b, s)
    onehot = slot_onehot(event_slot[...])
    wait_all(second)
    tokens = dot_tn(onehot, in2[...])
    tokens_out[...] = tokens.astype(BF16)
    normed = (normalize(tokens)[0] * gain_in[...]).astype(BF16)

    for part, first_column in ((0, 1536), (1, 512)):
        lanes = slice(part * HEAD, part * HEAD + HEAD)
        made = silu(dot_nn(normed, w_in[:, first_column : first_column + WIDTH])).astype(BF16)
        for h in range(HEADS):
            kv[h, 0, :, lanes] = made[:HALF, h * HEAD : (h + 1) * HEAD]
            kv[h, 1, :, lanes] = made[HALF:, h * HEAD : (h + 1) * HEAD]

    def each_worker(act):
        @pl.loop(0, SEQ)
        def _(i):
            w = lax.rem(i + s, SEQ)
            head, half, core, to_batch, to_seq = worker_at(w, x, c)
            here = (to_batch == b) & (to_seq == s)
            act(w, head, half, core, to_batch, to_seq, here)

    def kv_copy(w, head, core, to_batch, to_seq):
        return copy_to(kv.at[head, core], kv_out.at[s, core], kv_send.at[w], kv_recv.at[s], to_batch, to_seq)

    def start_kv(w, head, half, core, to_batch, to_seq, here):
        @pl.when(here)
        def _():
            pltpu.make_async_copy(kv.at[head, core], kv_out.at[s, core], kv_recv.at[s]).start()

        @pl.when(jnp.logical_not(here))
        def _():
            kv_copy(w, head, core, to_batch, to_seq).start()

    each_worker(start_kv)

    query = silu(dot_nn(normed, w_in[:, 1024:1536])).astype(BF16)
    gate = silu(dot_nn(normed, w_in[:, 0:WIDTH])).astype(BF16)
    upstream = (d_gated.astype(F32) * gate.astype(F32) * gain_mid[...]).astype(BF16)
    for h in range(HEADS):
        cols = slice(h * HEAD, (h + 1) * HEAD)
        qp[h, :, :, :, 0:HEAD] = query[:, cols].reshape(3, 4, PIECE, HEAD)
        qp[h, :, :, :, HEAD : 2 * HEAD] = upstream[:, cols].reshape(3, 4, PIECE, HEAD)

    def qp_copy(w, head, half, core, to_batch, to_seq):
        return copy_to(
            qp.at[head, :, half * 2 + core], qp_out.at[s], qp_send.at[w], qp_recv.at[s], to_batch, to_seq
        )

    def start_qp(w, head, half, core, to_batch, to_seq, here):
        @pl.when(here)
        def _():
            pltpu.make_async_copy(qp.at[head, :, half * 2 + core], qp_out.at[s], qp_recv.at[s]).start()

        @pl.when(jnp.logical_not(here))
        def _():
            qp_copy(w, head, half, core, to_batch, to_seq).start()

    each_worker(start_qp)

    meta_copy.wait()
    row, lane = iota((8, 128), 0), iota((8, 128), 1)
    own = (jnp.zeros((8, 128), jnp.int32) + (mine == c).astype(jnp.int32)) == 1
    meta = jnp.where(own, meta_own[...], meta_other[...])
    meta_out[...] = jnp.where(row == 3, (y % 2) * 2 + c, meta)

    def pass_on(source):
        return copy_to(
            kv_out.at[source, c], kv_out.at[source, c], pass_send.at[source], pass_recv.at[source], partner, s
        )

    @pl.loop(0, SEQ)
    def _(i):
        source = lax.rem(s - i + SEQ, SEQ)
        arrived(kv_out.at[source, c], kv_recv.at[source])
        pass_on(source).start()

    def finish(w, head, half, core, to_batch, to_seq, here):
        @pl.when(jnp.logical_not(here))
        def _():
            kv_copy(w, head, core, to_batch, to_seq).wait_send()
            qp_copy(w, head, half, core, to_batch, to_seq).wait_send()

    each_worker(finish)

    @pl.loop(0, SEQ)
    def _(source):
        pass_on(source).wait_send()
        arrived(kv_out.at[source, 1 - c], pass_recv.at[source])
        arrived(qp_out.at[source], qp_recv.at[source])


def read_meta(meta, slot_of, start_of, limit_of):
    @pl.loop(0, BLOCKS)
    def _(i):
        slot_of[meta[0, i]] = i

    first = jnp.int32(0)
    for u in range(4):
        count = meta[1, u]

        @pl.loop(first, first + count)
        def _(n, first=first, count=count, u=u):
            start_of[n] = first
            limit_of[n] = jnp.where(n == first + count - 1, meta[2, u], BLOCK)

        first = first + count


def fetch(slot_of, kv_hbm, qp_hbm, kv, qp, kv_sem, qp_sem):
    @pl.loop(0, TILES)
    def _(t):
        for i in range(4):
            n = t * 4 + i
            slot = slot_of[n]
            pltpu.make_async_copy(qp_hbm.at[slot], qp.at[n], qp_sem.at[t]).start()
            pltpu.make_async_copy(kv_hbm.at[slot], kv.at[n], kv_sem.at[t]).start()


def wait_tile(t, kv, qp, kv_sem, qp_sem):
    four = pl.ds(t * 4, 4)
    arrived(qp.at[four], qp_sem.at[t])
    arrived(kv.at[four], kv_sem.at[t])


def pick4(index, values):
    return jnp.where(index == 0, values[0], jnp.where(index == 1, values[1], jnp.where(index == 2, values[2], values[3])))


def forward_kernel(
    meta, kv_hbm, qp_hbm, mixed_out, stats_out, kv, qp, slot_of, start_of, limit_of, kv_sem, qp_sem
):
    read_meta(meta, slot_of, start_of, limit_of)
    fetch(slot_of, kv_hbm, qp_hbm, kv, qp, kv_sem, qp_sem)
    quarter = meta[3, 0]

    @pl.loop(0, TILES)
    def _(t):
        wait_tile(t, kv, qp, kv_sem, qp_sem)
        both = qp[pl.ds(t * 4, 4)].reshape(BLOCK, 2 * HEAD)
        query, upstream = both[:, :HEAD], both[:, HEAD:].astype(F32)
        r = iota((BLOCK, 1), 0)
        at = (t * 4 + (r >> 5)) * BLOCK + quarter * PIECE + (r & 31)
        since = pick4(r >> 5, [start_of[t * 4 + i] for i in range(4)]) * BLOCK

        def chunk(j, total):
            both = kv[pl.ds(j * 4, 4)].reshape(4 * BLOCK, 2 * HEAD)
            key, value = both[:, :HEAD], both[:, HEAD:]
            u = dot_nt(query, key) * (0.5 * SCALE)
            weights = u + u * jnp.tanh(u)
            lane = iota((1, BLOCK), 1)
            where = jnp.concatenate(
                [
                    jnp.where(lane < limit_of[j * 4 + i], (j * 4 + i) * BLOCK + lane, FAR)
                    for i in range(4)
                ],
                axis=1,
            )
            weights = jnp.where((where <= at) & (where >= since), weights, 0.0).astype(BF16)
            return total + dot_nn(weights, value)

        mixed = lax.fori_loop(start_of[t * 4] // 4, t + 1, chunk, jnp.zeros((BLOCK, HEAD), F32))
        mixed_out[t] = mixed
        mean = jnp.mean(mixed, axis=1, keepdims=True)
        centred = mixed - mean
        lane = iota((BLOCK, HEAD), 1)
        stats = pick4(
            lane,
            [
                mean,
                jnp.sum(centred * centred, axis=1, keepdims=True),
                jnp.sum(upstream, axis=1, keepdims=True),
                jnp.sum(upstream * centred, axis=1, keepdims=True),
            ],
        )
        stats_out[t] = jnp.transpose(stats)[0:8, :]


def stats_kernel(stats, all_stats, held, send, recv):
    b, s, x, c, y, z = place()
    copies = []
    for k in range(1, HEADS):
        peer = lax.rem(z + k, HEADS)
        copy = copy_to(stats, held.at[z], send.at[k], recv.at[k], b, y * 4 + peer)
        copy.start()
        copies.append(copy)
    held[z] = stats[...]
    wait_all(copies)
    all_stats[...] = held[...]


def backward_kernel(
    meta, kv_hbm, qp_hbm, mixed_in, stats_in, mq_hbm, dkv_hbm,
    kv, qp, mq, dkv, dkv_out, slot_of, start_of, limit_of, kv_sem, qp_sem, mq_sem, dkv_sem,
):
    read_meta(meta, slot_of, start_of, limit_of)
    fetch(slot_of, kv_hbm, qp_hbm, kv, qp, kv_sem, qp_sem)
    quarter = meta[3, 0]

    @pl.loop(0, TILES)
    def _(t):
        dkv[pl.ds(t * 4 * BLOCK, 4 * BLOCK), :] = jnp.zeros((4 * BLOCK, 2 * HEAD), F32)

    @pl.loop(0, TILES)
    def _(t):
        wait_tile(t, kv, qp, kv_sem, qp_sem)
        both = qp[pl.ds(t * 4, 4)].reshape(BLOCK, 2 * HEAD)
        query, upstream = both[:, :HEAD], both[:, HEAD:].astype(F32)
        mixed = mixed_in[t]

        stats = [stats_in[h, t] for h in range(HEADS)]
        mean = sum(v[0:1] for v in stats) * 0.25
        spread = sum(v[1:2] + HEAD * (v[0:1] - mean) * (v[0:1] - mean) for v in stats) * (1.0 / WIDTH)
        inverse = lax.rsqrt(spread + 1e-05)
        slant = sum(v[2:3] for v in stats) * (1.0 / WIDTH)
        along = sum(v[3:4] + v[2:3] * (v[0:1] - mean) for v in stats) * (1.0 / WIDTH) * inverse
        r8 = iota((BLOCK, HEAD), 0)
        columns = jnp.transpose(pick4(r8, [mean, inverse, slant, along]))
        mean, inverse, slant, along = (columns[:, i : i + 1] for i in range(4))
        normal = (mixed - mean) * inverse
        d_mixed = (inverse * (upstream - slant - normal * along)).astype(BF16)

        r = iota((1, BLOCK), 1)
        at = (t * 4 + (r >> 5)) * BLOCK + quarter * PIECE + (r & 31)
        since = pick4(r >> 5, [start_of[t * 4 + i] for i in range(4)]) * BLOCK

        def chunk(j, total):
            both = kv[pl.ds(j * 4, 4)].reshape(4 * BLOCK, 2 * HEAD)
            key, value = both[:, :HEAD], both[:, HEAD:]
            u = dot_nt(key, query) * (0.5 * SCALE)
            th = jnp.tanh(u)
            a = 1.0 + th
            weights = u * a
            slope = a + weights * (1.0 - th)
            d_scores = dot_nt(value, d_mixed) * slope
            row = iota((BLOCK, 1), 0)
            where = jnp.concatenate(
                [
                    jnp.where(row < limit_of[j * 4 + i], (j * 4 + i) * BLOCK + row, FAR)
                    for i in range(4)
                ],
                axis=0,
            )
            seen = (where <= at) & (where >= since)
            weights = jnp.where(seen, weights, 0.0).astype(BF16)
            d_scores = jnp.where(seen, d_scores, 0.0).astype(BF16)
            keys = pl.ds(pl.multiple_of(j * 4 * BLOCK, 4 * BLOCK), 4 * BLOCK)
            dkv[keys, 0:HEAD] += dot_nn(d_scores, query)
            dkv[keys, HEAD : 2 * HEAD] += dot_nn(weights, d_mixed)
            return total + dot_tn(d_scores, key)

        d_query = lax.fori_loop(start_of[t * 4] // 4, t + 1, chunk, jnp.zeros((BLOCK, HEAD), F32))
        d_query = (d_query * (0.5 * SCALE)).astype(BF16)
        mq[pl.ds(t * 4, 4), :, 0:HEAD] = mixed.astype(BF16).reshape(4, PIECE, HEAD)
        mq[pl.ds(t * 4, 4), :, HEAD : 2 * HEAD] = d_query.reshape(4, PIECE, HEAD)
        for i in range(4):
            n = t * 4 + i
            pltpu.make_async_copy(mq.at[n], mq_hbm.at[slot_of[n]], mq_sem.at[n]).start()

    @pl.loop(0, BLOCKS)
    def _(n):
        keys = pl.ds(pl.multiple_of(n * BLOCK, BLOCK), BLOCK)
        dkv_out[n, :, 0:HEAD] = (dkv[keys, 0:HEAD] * (0.5 * SCALE)).astype(BF16)
        dkv_out[n, :, HEAD : 2 * HEAD] = dkv[keys, HEAD : 2 * HEAD].astype(BF16)
        pltpu.make_async_copy(dkv_out.at[n], dkv_hbm.at[slot_of[n]], dkv_sem.at[n]).start()

    @pl.loop(0, BLOCKS)
    def _(n):
        pltpu.make_async_copy(mq.at[n], mq_hbm.at[slot_of[n]], mq_sem.at[n]).wait()
        pltpu.make_async_copy(dkv_out.at[n], dkv_hbm.at[slot_of[n]], dkv_sem.at[n]).wait()


def return_kernel(
    feats, item_weight, send_rows, event_slot, gain_in, gain_mid, w_in, w_out, cot, tokens_in, mq_in, dkv_in,
    layer_out, item_grad,
    mq, dkv, own, part, pre, d_pre, out2, in2, out1, in1,
    own_sem, part_send, part_recv, mq_send, mq_recv, dkv_send, dkv_recv, send2, recv2, send1, recv1,
):
    b, s, x, c, y, z = place()
    partner = x * 2 + 1 - c
    mine = y // 2
    half = y % 2
    to_batch = x * 2 + mine
    me = z + 4 * half + 8 * c

    def group_order(k):
        return lax.rem(k + z, 4)

    def own_copy(g):
        return pltpu.make_async_copy(dkv_in.at[pl.ds(g * 4, 4), c], own.at[pl.ds(g * 4, 4)], own_sem.at[g])

    def part_copy(g):
        return copy_to(
            dkv_in.at[pl.ds(g * 4, 4), 1 - c], part.at[pl.ds(g * 4, 4)], part_send.at[g], part_recv.at[g], partner, s
        )

    @pl.loop(0, 4)
    def _(k):
        g = group_order(k)
        own_copy(g).start()
        part_copy(g).start()

    def is_here(source):
        return (to_batch == b) & (source == s)

    def mq_copy(source):
        return copy_to(
            mq_in.at[source], mq.at[z, :, half * 2 + c], mq_send.at[source], mq_recv.at[me], to_batch, source
        )

    def dkv_copy(source):
        return copy_to(
            own.at[source], dkv.at[z, half, c], dkv_send.at[source], dkv_recv.at[me], to_batch, source
        )

    @pl.loop(0, SEQ)
    def _(i):
        source = lax.rem(i + s, SEQ)

        @pl.when(is_here(source))
        def _():
            pltpu.make_async_copy(mq_in.at[source], mq.at[z, :, half * 2 + c], mq_recv.at[me]).start()

        @pl.when(jnp.logical_not(is_here(source)))
        def _():
            mq_copy(source).start()

    @pl.loop(0, 4)
    def _(k):
        g = group_order(k)
        own_copy(g).wait()
        arrived(part.at[pl.ds(g * 4, 4)], part_recv.at[g])

        @pl.loop(0, 4)
        def _(i):
            source = g * 4 + lax.rem(i + y, 4)
            own[source] = (own[source].astype(F32) + part[source].astype(F32)).astype(BF16)

            @pl.when(is_here(source))
            def _():
                pltpu.make_async_copy(own.at[source], dkv.at[z, half, c], dkv_recv.at[me]).start()

            @pl.when(jnp.logical_not(is_here(source)))
            def _():
                dkv_copy(source).start()

    tokens = tokens_in[...].astype(F32)
    normal, inverse = normalize(tokens)
    normed = (normal * gain_in[...]).astype(BF16)
    for k in range(4):
        cols = slice(k * WIDTH, (k + 1) * WIDTH)
        pre[:, cols] = dot_nn(normed, w_in[:, cols])
    gate = silu(pre[:, 0:WIDTH]).astype(BF16).astype(F32)
    d_gated = dot_nt(cot[...], w_out[...]).astype(BF16).astype(F32)
    onehot = slot_onehot(event_slot[...])
    item_pre = dot_nn(feats[...], item_weight[...])
    item_slope = silu_slope(item_pre)

    @pl.loop(0, SEQ)
    def _(w):
        arrived(mq.at[w % 4, :, ((w // 4) % 2) * 2 + w // 8], mq_recv.at[w])

    mixed = jnp.concatenate([mq[h, :, :, :, 0:HEAD].reshape(ROWS, HEAD) for h in range(HEADS)], axis=1)
    normed_mid = normalize(mixed.astype(F32))[0] * gain_mid[...]
    gated = (normed_mid * gate).astype(BF16)
    layer_out[...] = (tokens + dot_nn(gated, w_out[...])).astype(BF16)
    d_pre[...] = (d_gated * normed_mid * silu_slope(pre[:, 0:WIDTH])).astype(BF16)
    d_normed = dot_nt(d_pre[...], w_in[:, 0:WIDTH])
    d_query = jnp.concatenate(
        [mq[h, :, :, :, HEAD : 2 * HEAD].reshape(ROWS, HEAD) for h in range(HEADS)], axis=1
    )
    d_pre[...] = (d_query.astype(F32) * silu_slope(pre[:, 1024:1536])).astype(BF16)
    d_normed += dot_nt(d_pre[...], w_in[:, 1024:1536])

    @pl.loop(0, SEQ)
    def _(w):
        arrived(dkv.at[w % 4, (w // 4) % 2, w // 8], dkv_recv.at[w])

    for lanes, first_column in ((0, 1536), (HEAD, 512)):
        grad = jnp.concatenate(
            [
                dkv[h, 0, :, :, lanes : lanes + HEAD].reshape(ROWS, HEAD).astype(F32)
                + dkv[h, 1, :, :, lanes : lanes + HEAD].reshape(ROWS, HEAD).astype(F32)
                for h in range(HEADS)
            ],
            axis=1,
        )
        d_pre[...] = (grad * silu_slope(pre[:, first_column : first_column + WIDTH])).astype(BF16)
        d_normed += dot_nt(d_pre[...], w_in[:, first_column : first_column + WIDTH])

    scaled = d_normed * gain_in[...]
    d_tokens = cot[...].astype(F32) + inverse * (
        scaled
        - jnp.mean(scaled, axis=-1, keepdims=True)
        - normal * jnp.mean(scaled * normal, axis=-1, keepdims=True)
    )
    out2[...] = dot_nn(onehot, d_tokens.astype(BF16)).astype(BF16)
    wait_all(exchange_seq(out2, in2, send2, recv2, b, s))
    out1[...] = dot_nn(by_batch(), in2[...]).astype(BF16)
    last = exchange_batch(out1, in1, send1, recv1, b, s)
    wanted = (iota((256, 256), 0) == send_rows[...]).astype(BF16)
    wait_all(last)
    d_embedded = dot_nn(wanted, in1[...])
    d_item = (d_embedded * item_slope).astype(BF16)
    item_grad[...] = dot_nt(d_item, item_weight[...])

    @pl.loop(0, 4)
    def _(g):
        part_copy(g).wait_send()

    @pl.loop(0, SEQ)
    def _(source):
        @pl.when(jnp.logical_not(is_here(source)))
        def _():
            mq_copy(source).wait_send()
            dkv_copy(source).wait_send()


def spec(space):
    return pl.BlockSpec(memory_space=space)


VMEM, SMEM, ANY = pltpu.VMEM, pltpu.SMEM, pl.ANY
DMA = pltpu.SemaphoreType.DMA


def shape(dims, dtype):
    return jax.ShapeDtypeStruct(dims, dtype)


def params(remote):
    return pltpu.CompilerParams(vmem_limit_bytes=56 << 20, has_side_effects=remote)


def per_device(
    item_feats, item_weight, send_rows, event_slot, user_blocks, tail_len, block_order, gain_in, gain_mid, w_in, w_out,
    cot_out,
):
    event_slot = event_slot.reshape(1, ROWS)
    gain_in, gain_mid = gain_in.reshape(1, WIDTH), gain_mid.reshape(1, WIDTH)
    kv, qp, tokens, meta = pl.pallas_call(
        send_kernel,
        out_shape=(
            shape((SEQ, 2, HALF, 2 * HEAD), BF16),
            shape((SEQ, 3, PIECE, 2 * HEAD), BF16),
            shape((ROWS, WIDTH), BF16),
            shape((8, 128), jnp.int32),
        ),
        in_specs=[spec(VMEM)] * 12,
        out_specs=(spec(ANY), spec(ANY), spec(VMEM), spec(VMEM)),
        scratch_shapes=[VMEM((256, WIDTH), BF16)] * 4
        + [
            VMEM((HEADS, 2, HALF, 2 * HEAD), BF16),
            VMEM((HEADS, 3, 4, PIECE, 2 * HEAD), BF16),
            VMEM((8, 128), jnp.int32),
            VMEM((8, 128), jnp.int32),
            DMA((GROUPS,)),
            DMA((GROUPS,)),
            DMA((SEQ,)),
            DMA((SEQ,)),
        ]
        + [DMA((SEQ,))] * 6
        + [DMA, DMA],
        compiler_params=params(True),
        name="send",
    )(
        item_feats, item_weight, send_rows, event_slot, user_blocks, tail_len, block_order, gain_in, gain_mid, w_in,
        w_out, cot_out,
    )
    kv = kv.reshape(BLOCKS, BLOCK, 2 * HEAD)
    qp = qp.reshape(BLOCKS, PIECE, 2 * HEAD)
    tables = [SMEM((BLOCKS,), jnp.int32)] * 3
    held = [VMEM((BLOCKS, BLOCK, 2 * HEAD), BF16), VMEM((BLOCKS, PIECE, 2 * HEAD), BF16)]
    mixed, stats = pl.pallas_call(
        forward_kernel,
        out_shape=(shape((TILES, BLOCK, HEAD), F32), shape((TILES, 8, BLOCK), F32)),
        in_specs=[spec(SMEM), spec(ANY), spec(ANY)],
        out_specs=(spec(VMEM), spec(VMEM)),
        scratch_shapes=held + tables + [DMA((TILES,))] * 2,
        compiler_params=params(False),
        name="forward",
    )(meta, kv, qp)
    stats = pl.pallas_call(
        stats_kernel,
        out_shape=shape((HEADS, TILES, 8, BLOCK), F32),
        in_specs=[spec(VMEM)],
        out_specs=spec(VMEM),
        scratch_shapes=[VMEM((HEADS, TILES, 8, BLOCK), F32), DMA((HEADS,)), DMA((HEADS,))],
        compiler_params=params(True),
        name="stats",
    )(stats)
    mq, dkv = pl.pallas_call(
        backward_kernel,
        out_shape=(shape((BLOCKS, PIECE, 2 * HEAD), BF16), shape((BLOCKS, BLOCK, 2 * HEAD), BF16)),
        in_specs=[spec(SMEM), spec(ANY), spec(ANY), spec(VMEM), spec(VMEM)],
        out_specs=(spec(ANY), spec(ANY)),
        scratch_shapes=held
        + [
            VMEM((BLOCKS, PIECE, 2 * HEAD), BF16),
            VMEM((BLOCKS * BLOCK, 2 * HEAD), F32),
            VMEM((BLOCKS, BLOCK, 2 * HEAD), BF16),
        ]
        + tables
        + [DMA((TILES,))] * 2
        + [DMA((BLOCKS,))] * 2,
        compiler_params=params(False),
        name="backward",
    )(meta, kv, qp, mixed, stats)
    mq = mq.reshape(SEQ, 3, PIECE, 2 * HEAD)
    dkv = dkv.reshape(SEQ, 2, HALF, 2 * HEAD)
    return pl.pallas_call(
        return_kernel,
        out_shape=(shape((ROWS, WIDTH), BF16), shape((256, WIDTH), F32)),
        in_specs=[spec(VMEM)] * 10 + [spec(ANY)] * 2,
        out_specs=(spec(VMEM), spec(VMEM)),
        scratch_shapes=[
            VMEM((HEADS, 3, 4, PIECE, 2 * HEAD), BF16),
            VMEM((HEADS, 2, 2, HALF, 2 * HEAD), BF16),
            VMEM((SEQ, HALF, 2 * HEAD), BF16),
            VMEM((SEQ, HALF, 2 * HEAD), BF16),
            VMEM((ROWS, 4 * WIDTH), F32),
            VMEM((ROWS, WIDTH), BF16),
        ]
        + [VMEM((256, WIDTH), BF16)] * 4
        + [DMA((4,))] * 3
        + [DMA((SEQ,))] * 6
        + [DMA((GROUPS,))] * 2,
        compiler_params=params(True),
        name="give_back",
    )(
        item_feats, item_weight, send_rows, event_slot, gain_in, gain_mid, w_in, w_out, cot_out, tokens, mq, dkv,
    )


def solution(mesh):
    rows = P(("batch", "seq"), None)
    return jax.shard_map(
        per_device,
        mesh=mesh,
        in_specs=(
            rows,
            P(),
            rows,
            P(("batch", "seq")),
            P("batch", None),
            P("batch", None),
            P("batch", None),
            P(),
            P(),
            P(),
            P(),
            rows,
        ),
        out_specs=(rows, rows),
        check_vma=False,
    )
```

```python
import jax
import jax.numpy as jnp
from jax import lax
from jax.experimental import pallas as pl
from jax.experimental.pallas import tpu as pltpu
from jax.sharding import PartitionSpec as P

WIDTH = 512
HEAD = 128
HEADS = 4
BLOCK = 128
BLOCKS = 48
SEQ = 16
GROUPS = 8
PIECE = 32
TILES = 12
HALF = 192
ROWS = 384
FAR = 1 << 20
AT_ONCE = 4
BACK_AT_ONCE = 4
SCALE = HEAD**-0.5
MESH = pl.DeviceIdType.MESH
F32 = jnp.float32
BF16 = jnp.bfloat16


def dot_nn(a, b):
    return jnp.dot(a, b, preferred_element_type=F32)


def dot_nt(a, b):
    return lax.dot_general(a, b, (((1,), (1,)), ((), ())), preferred_element_type=F32)


def dot_tn(a, b):
    return lax.dot_general(a, b, (((0,), (0,)), ((), ())), preferred_element_type=F32)


def silu(v):
    u = 0.5 * v
    return u + u * jnp.tanh(u)


def silu_slope(v):
    u = 0.5 * v
    t = jnp.tanh(u)
    a = 1.0 + t
    return 0.5 * (a + u * a * (1.0 - t))


def normalize(values):
    mean = jnp.mean(values, axis=-1, keepdims=True)
    centred = values - mean
    spread = jnp.mean(centred * centred, axis=-1, keepdims=True)
    inverse = lax.rsqrt(spread + 1e-05)
    return centred * inverse, inverse


def iota(shape, dim):
    return lax.broadcasted_iota(jnp.int32, shape, dim)


def place():
    b, s = lax.axis_index("batch"), lax.axis_index("seq")
    return b, s, b // 2, b % 2, s // 4, s % 4


def worker_at(w, x, c):
    head, half, core = w % 4, (w // 4) % 2, w // 8
    return head, half, core, x * 2 + core, (2 * c + half) * 4 + head


def copy_to(src, dst, send, recv, batch, seq):
    return pltpu.make_async_remote_copy(
        src_ref=src, dst_ref=dst, send_sem=send, recv_sem=recv, device_id=(batch, seq), device_id_type=MESH
    )


def arrived(ref, sem):
    pltpu.make_async_copy(ref, ref, sem).wait()


def rows_of(index, size):
    return pl.ds(pl.multiple_of(index * size, size), size)


def slot_onehot(event_slot):
    e = event_slot
    wanted = ((e >> 1) & 15) * 16 + (e >> 5) * 2 + (e & 1)
    return (iota((256, ROWS), 0) == wanted).astype(BF16)


def by_seq():
    i, j = iota((256, 256), 0), iota((256, 256), 1)
    return (j == ((i >> 1) & 7) * 32 + (i >> 4) * 2 + (i & 1)).astype(BF16)


def by_batch():
    i, j = iota((256, 256), 0), iota((256, 256), 1)
    return (j == ((i >> 1) & 15) * 16 + (i >> 5) * 2 + (i & 1)).astype(BF16)


def exchange_batch(src, dst, send, recv, b, s):
    copies = []
    for k in range(1, GROUPS):
        peer = lax.rem(b + k, GROUPS)
        copy = copy_to(src.at[rows_of(peer, 32)], dst.at[rows_of(b, 32)], send.at[k], recv.at[k], peer, s)
        copy.start()
        copies.append(copy)
    dst[rows_of(b, 32), :] = src[rows_of(b, 32), :]
    return copies


def exchange_seq(src, dst, send, recv, b, s):
    copies = []
    for k in range(1, SEQ):
        peer = lax.rem(s + k, SEQ)
        copy = copy_to(src.at[rows_of(peer, 16)], dst.at[rows_of(s, 16)], send.at[k], recv.at[k], b, peer)
        copy.start()
        copies.append(copy)
    dst[rows_of(s, 16), :] = src[rows_of(s, 16), :]
    return copies


def signal(barrier, batch, seq):
    pl.semaphore_signal(barrier, inc=1, device_id=(batch, seq), device_id_type=MESH)


def greet(b, s, partner):
    barrier = pltpu.get_barrier_semaphore()
    for k in range(1, GROUPS):
        signal(barrier, lax.rem(b + k, GROUPS), s)

    @pl.loop(1, SEQ)
    def _(k):
        peer = lax.rem(s + k, SEQ)
        signal(barrier, b, peer)
        signal(barrier, partner, peer)


def greeted():
    pl.semaphore_wait(pltpu.get_barrier_semaphore(), GROUPS - 1 + 2 * (SEQ - 1))


def wait_all(copies):
    for copy in copies:
        copy.wait()


def send_kernel(
    feats, item_weight, send_rows, event_slot, user_blocks, tail_len, block_order, gain_in, gain_mid, w_in, w_out, cot,
    kv_out, qp_out, tokens_out, meta_out,
    out1, in1, out2, in2, kv, qp, meta_own, meta_other,
    send1, recv1, send2, recv2, kv_send, kv_recv, pass_send, pass_recv, qp_send, qp_recv, meta_send, meta_recv,
):
    b, s, x, c, y, z = place()
    partner = x * 2 + 1 - c
    mine = y // 2
    greet(b, s, partner)

    embedded = silu(dot_nn(feats[...], item_weight[...])).astype(BF16)
    wanted = (iota((256, 256), 0) == send_rows[...]).astype(BF16)
    out1[...] = dot_tn(wanted, embedded).astype(BF16)
    greeted()
    first = exchange_batch(out1, in1, send1, recv1, b, s)

    meta_own[...] = jnp.zeros_like(meta_own)
    meta_own[0:1, 0:48] = block_order[...]
    meta_own[1:2, 0:4] = user_blocks[...]
    meta_own[2:3, 0:4] = tail_len[...]
    meta_copy = copy_to(meta_own, meta_other, meta_send, meta_recv, partner, s)
    meta_copy.start()

    d_gated = dot_nt(cot[...], w_out[...]).astype(BF16)
    wait_all(first)
    out2[...] = dot_nn(by_seq(), in1[...]).astype(BF16)
    second = exchange_seq(out2, in2, send2, recv2, b, s)
    onehot = slot_onehot(event_slot[...])
    wait_all(second)
    tokens = dot_tn(onehot, in2[...])
    tokens_out[...] = tokens.astype(BF16)
    normed = (normalize(tokens)[0] * gain_in[...]).astype(BF16)

    for part, first_column in ((0, 1536), (1, 512)):
        lanes = slice(part * HEAD, part * HEAD + HEAD)
        made = silu(dot_nn(normed, w_in[:, first_column : first_column + WIDTH])).astype(BF16)
        for h in range(HEADS):
            kv[h, 0, :, lanes] = made[:HALF, h * HEAD : (h + 1) * HEAD]
            kv[h, 1, :, lanes] = made[HALF:, h * HEAD : (h + 1) * HEAD]

    def each_worker(act):
        @pl.loop(0, SEQ)
        def _(i):
            w = lax.rem(i + s, SEQ)
            head, half, core, to_batch, to_seq = worker_at(w, x, c)
            here = (to_batch == b) & (to_seq == s)
            act(w, head, half, core, to_batch, to_seq, here)

    def kv_copy(w, head, core, to_batch, to_seq):
        return copy_to(kv.at[head, core], kv_out.at[s, core], kv_send.at[w], kv_recv.at[s], to_batch, to_seq)

    def start_kv(w, head, half, core, to_batch, to_seq, here):
        @pl.when(here)
        def _():
            pltpu.make_async_copy(kv.at[head, core], kv_out.at[s, core], kv_recv.at[s]).start()

        @pl.when(jnp.logical_not(here))
        def _():
            kv_copy(w, head, core, to_batch, to_seq).start()

    each_worker(start_kv)

    query = silu(dot_nn(normed, w_in[:, 1024:1536])).astype(BF16)
    gate = silu(dot_nn(normed, w_in[:, 0:WIDTH])).astype(BF16)
    upstream = (d_gated.astype(F32) * gate.astype(F32) * gain_mid[...]).astype(BF16)
    for h in range(HEADS):
        cols = slice(h * HEAD, (h + 1) * HEAD)
        qp[h, :, :, :, 0:HEAD] = query[:, cols].reshape(3, 4, PIECE, HEAD)
        qp[h, :, :, :, HEAD : 2 * HEAD] = upstream[:, cols].reshape(3, 4, PIECE, HEAD)

    def qp_copy(w, head, half, core, to_batch, to_seq):
        return copy_to(
            qp.at[head, :, half * 2 + core], qp_out.at[s], qp_send.at[w], qp_recv.at[s], to_batch, to_seq
        )

    def start_qp(w, head, half, core, to_batch, to_seq, here):
        @pl.when(here)
        def _():
            pltpu.make_async_copy(qp.at[head, :, half * 2 + core], qp_out.at[s], qp_recv.at[s]).start()

        @pl.when(jnp.logical_not(here))
        def _():
            qp_copy(w, head, half, core, to_batch, to_seq).start()

    each_worker(start_qp)

    meta_copy.wait()
    own = (jnp.zeros((8, 128), jnp.int32) + (mine == c).astype(jnp.int32)) == 1
    meta_out[...] = tables_of(jnp.where(own, meta_own[...], meta_other[...]), (y % 2) * 2 + c)

    def pass_on(source):
        return copy_to(
            kv_out.at[source, c], kv_out.at[source, c], pass_send.at[source], pass_recv.at[source], partner, s
        )

    @pl.loop(0, SEQ)
    def _(i):
        source = lax.rem(s - i + SEQ, SEQ)
        arrived(kv_out.at[source, c], kv_recv.at[source])
        pass_on(source).start()

    def finish(w, head, half, core, to_batch, to_seq, here):
        @pl.when(jnp.logical_not(here))
        def _():
            kv_copy(w, head, core, to_batch, to_seq).wait_send()
            qp_copy(w, head, half, core, to_batch, to_seq).wait_send()

    each_worker(finish)

    @pl.loop(0, SEQ)
    def _(source):
        pass_on(source).wait_send()
        arrived(kv_out.at[source, 1 - c], pass_recv.at[source])
        arrived(qp_out.at[source], qp_recv.at[source])


def tables_of(meta, quarter):
    slot, lane = iota((128, 128), 0), iota((1, 128), 1)
    held = jnp.transpose(jnp.broadcast_to(meta[0:1, :].astype(F32), (128, 128)))
    slot_of = jnp.where((held == iota((128, 128), 1).astype(F32)) & (slot < BLOCKS), slot.astype(F32), 0.0)
    slot_of = jnp.sum(slot_of, axis=0, keepdims=True).astype(jnp.int32)
    first = jnp.zeros((1, 1), jnp.int32)
    start_of = jnp.zeros((1, 128), jnp.int32)
    limit_of = jnp.full((1, 128), BLOCK, jnp.int32)
    for u in range(4):
        start_of = jnp.where(lane >= first, first, start_of)
        first = first + meta[1:2, u : u + 1]
        limit_of = jnp.where(lane == first - 1, meta[2:3, u : u + 1], limit_of)
    start_of = jnp.where(lane < BLOCKS, start_of, FAR)
    row = iota((8, 128), 0)
    return pick4(row, [slot_of, start_of, limit_of, jnp.zeros((1, 128), jnp.int32) + quarter])


def pick4(index, values):
    return jnp.where(index == 0, values[0], jnp.where(index == 1, values[1], jnp.where(index == 2, values[2], values[3])))


def first_chunk(meta, t):
    return jnp.minimum(meta[1, 4 * t] // 4, TILES - 1)


def walk(meta, t, j, count):
    pairs = []
    for _ in range(count):
        pairs.append((t, j))
        more = j < jnp.minimum(t, TILES - 1)
        after = jnp.minimum(t + 1, TILES)
        j = jnp.where(more, j + 1, first_chunk(meta, after))
        t = jnp.where(more, t, after)
    return pairs, t, j


def pairs_in_all(meta):
    return sum(t + 1 - meta[1, 4 * t] // 4 for t in range(TILES))


def four(ref, meta, n):
    return jnp.concatenate([ref[meta[0, 4 * n + i]] for i in range(4)], axis=0)


def query_bounds(meta, t, r):
    at = (t * 4 + (r >> 5)) * BLOCK + meta[3, 0] * PIECE + (r & 31)
    return at, pick4(r >> 5, [meta[1, t * 4 + i] for i in range(4)]) * BLOCK


def key_places(meta, j, dim):
    size = (1, BLOCK) if dim else (BLOCK, 1)
    e = iota(size, dim)
    return jnp.concatenate(
        [jnp.where(e < meta[2, j * 4 + i], (j * 4 + i) * BLOCK + e, FAR) for i in range(4)], axis=dim
    )


def forward_kernel(meta, kv, qp, mixed_out, stats_out, total):
    @pl.loop(0, TILES + 1)
    def _(t):
        total[t] = jnp.zeros((BLOCK, HEAD), F32)

    def step(_, state):
        pairs, t, j = walk(meta, *state, AT_ONCE)
        keyvals = [four(kv, meta, j) for _, j in pairs]
        us = [
            dot_nt(four(qp, meta, t)[:, :HEAD], keyval[:, :HEAD]) * (0.5 * SCALE)
            for (t, _), keyval in zip(pairs, keyvals)
        ]
        weights = []
        for (t_, j_), u in zip(pairs, us):
            at, since = query_bounds(meta, t_, iota((BLOCK, 1), 0))
            where = key_places(meta, j_, 1)
            w = u + u * jnp.tanh(u)
            weights.append(jnp.where((where <= at) & (where >= since), w, 0.0).astype(BF16))
        for (t_, _), w, keyval in zip(pairs, weights, keyvals):
            total[t_] += dot_nn(w, keyval[:, HEAD:])
        return t, j

    lax.fori_loop(0, (pairs_in_all(meta) + AT_ONCE - 1) // AT_ONCE, step, (jnp.int32(0), jnp.int32(0)))

    @pl.loop(0, TILES, unroll=4)
    def _(t):
        mixed = total[t]
        upstream = four(qp, meta, t)[:, HEAD:].astype(F32)
        mixed_out[t] = mixed
        mean = jnp.mean(mixed, axis=1, keepdims=True)
        centred = mixed - mean
        stats = pick4(
            iota((BLOCK, HEAD), 1),
            [
                mean,
                jnp.sum(centred * centred, axis=1, keepdims=True),
                jnp.sum(upstream, axis=1, keepdims=True),
                jnp.sum(upstream * centred, axis=1, keepdims=True),
            ],
        )
        stats_out[t] = jnp.transpose(stats)[0:8, :]


def stats_kernel(stats, all_stats, held, send, recv):
    b, s, x, c, y, z = place()
    barrier = pltpu.get_barrier_semaphore()
    for k in range(1, HEADS):
        signal(barrier, b, y * 4 + lax.rem(z + k, HEADS))
    pl.semaphore_wait(barrier, HEADS - 1)
    copies = []
    for k in range(1, HEADS):
        peer = lax.rem(z + k, HEADS)
        copy = copy_to(stats, held.at[z], send.at[k], recv.at[k], b, y * 4 + peer)
        copy.start()
        copies.append(copy)
    held[z] = stats[...]
    wait_all(copies)
    all_stats[...] = held[...]


def backward_kernel(meta, kv, qp, mixed_in, stats_in, mq_out, dkv_out, d_mixed, d_query, dkv):
    @pl.loop(0, TILES)
    def _(t):
        dkv[pl.ds(t * 4 * BLOCK, 4 * BLOCK), :] = jnp.zeros((4 * BLOCK, 2 * HEAD), F32)

    d_mixed[TILES] = jnp.zeros((BLOCK, HEAD), BF16)

    @pl.loop(0, TILES, unroll=4)
    def _(t):
        d_query[t] = jnp.zeros((BLOCK, HEAD), F32)
        mixed = mixed_in[t]
        upstream = four(qp, meta, t)[:, HEAD:].astype(F32)
        stats = [stats_in[h, t] for h in range(HEADS)]
        mean = sum(v[0:1] for v in stats) * 0.25
        spread = sum(v[1:2] + HEAD * (v[0:1] - mean) * (v[0:1] - mean) for v in stats) * (1.0 / WIDTH)
        inverse = lax.rsqrt(spread + 1e-05)
        slant = sum(v[2:3] for v in stats) * (1.0 / WIDTH)
        along = sum(v[3:4] + v[2:3] * (v[0:1] - mean) for v in stats) * (1.0 / WIDTH) * inverse
        columns = jnp.transpose(pick4(iota((BLOCK, HEAD), 0), [mean, inverse, slant, along]))
        mean, inverse, slant, along = (columns[:, i : i + 1] for i in range(4))
        normal = (mixed - mean) * inverse
        d_mixed[t] = (inverse * (upstream - slant - normal * along)).astype(BF16)

    def step(_, state):
        pairs, t, j = walk(meta, *state, BACK_AT_ONCE)
        keyvals = [four(kv, meta, j) for _, j in pairs]
        queries = [four(qp, meta, t)[:, :HEAD] for t, _ in pairs]
        d_mixeds = [d_mixed[t] for t, _ in pairs]
        us = [dot_nt(keyval[:, :HEAD], query) * (0.5 * SCALE) for keyval, query in zip(keyvals, queries)]
        d_weights = [dot_nt(keyval[:, HEAD:], dm) for keyval, dm in zip(keyvals, d_mixeds)]
        made = []
        for (t_, j_), u, dw in zip(pairs, us, d_weights):
            th = jnp.tanh(u)
            a = 1.0 + th
            w = u * a
            ds = dw * (a + w * (1.0 - th))
            at, since = query_bounds(meta, t_, iota((1, BLOCK), 1))
            where = key_places(meta, j_, 0)
            seen = (where <= at) & (where >= since)
            made.append((jnp.where(seen, w, 0.0).astype(BF16), jnp.where(seen, ds, 0.0).astype(BF16)))
        for (t_, j_), keyval, query, dm, (w, ds) in zip(pairs, keyvals, queries, d_mixeds, made):
            keys = pl.ds(pl.multiple_of(j_ * 4 * BLOCK, 4 * BLOCK), 4 * BLOCK)
            dkv[keys, 0:HEAD] += dot_nn(ds, query)
            dkv[keys, HEAD : 2 * HEAD] += dot_nn(w, dm)
            d_query[t_] += dot_tn(ds, keyval[:, :HEAD])
        return t, j

    lax.fori_loop(0, (pairs_in_all(meta) + BACK_AT_ONCE - 1) // BACK_AT_ONCE, step, (jnp.int32(0), jnp.int32(0)))

    @pl.loop(0, TILES)
    def _(t):
        mixed = mixed_in[t].astype(BF16)
        dq = (d_query[t] * (0.5 * SCALE)).astype(BF16)
        for i in range(4):
            n = t * 4 + i
            slot = meta[0, n]
            rows = slice(i * PIECE, (i + 1) * PIECE)
            mq_out[slot, :, 0:HEAD] = mixed[rows]
            mq_out[slot, :, HEAD : 2 * HEAD] = dq[rows]
            keys = pl.ds(pl.multiple_of(n * BLOCK, BLOCK), BLOCK)
            dkv_out[slot, :, 0:HEAD] = (dkv[keys, 0:HEAD] * (0.5 * SCALE)).astype(BF16)
            dkv_out[slot, :, HEAD : 2 * HEAD] = dkv[keys, HEAD : 2 * HEAD].astype(BF16)


def return_kernel(
    feats, item_weight, send_rows, event_slot, gain_in, gain_mid, w_in, w_out, cot, tokens_in, mq_in, dkv_in,
    layer_out, item_grad,
    mq, dkv, own, part, pre, d_pre, out2, in2, out1, in1,
    own_sem, part_send, part_recv, mq_send, mq_recv, dkv_send, dkv_recv, send2, recv2, send1, recv1,
):
    b, s, x, c, y, z = place()
    partner = x * 2 + 1 - c
    mine = y // 2
    half = y % 2
    to_batch = x * 2 + mine
    me = z + 4 * half + 8 * c
    greet(b, s, partner)
    greeted()

    def group_order(k):
        return lax.rem(k + z, 4)

    def own_copy(g):
        return pltpu.make_async_copy(dkv_in.at[pl.ds(g * 4, 4), c], own.at[pl.ds(g * 4, 4)], own_sem.at[g])

    def part_copy(g):
        return copy_to(
            dkv_in.at[pl.ds(g * 4, 4), 1 - c], part.at[pl.ds(g * 4, 4)], part_send.at[g], part_recv.at[g], partner, s
        )

    @pl.loop(0, 4)
    def _(k):
        g = group_order(k)
        own_copy(g).start()
        part_copy(g).start()

    def is_here(source):
        return (to_batch == b) & (source == s)

    def mq_copy(source):
        return copy_to(
            mq_in.at[source], mq.at[z, :, half * 2 + c], mq_send.at[source], mq_recv.at[me], to_batch, source
        )

    def dkv_copy(source):
        return copy_to(
            own.at[source], dkv.at[z, half, c], dkv_send.at[source], dkv_recv.at[me], to_batch, source
        )

    @pl.loop(0, SEQ)
    def _(i):
        source = lax.rem(i + s, SEQ)

        @pl.when(is_here(source))
        def _():
            pltpu.make_async_copy(mq_in.at[source], mq.at[z, :, half * 2 + c], mq_recv.at[me]).start()

        @pl.when(jnp.logical_not(is_here(source)))
        def _():
            mq_copy(source).start()

    @pl.loop(0, 4)
    def _(k):
        g = group_order(k)
        own_copy(g).wait()
        arrived(part.at[pl.ds(g * 4, 4)], part_recv.at[g])

        @pl.loop(0, 4)
        def _(i):
            source = g * 4 + lax.rem(i + y, 4)
            own[source] = (own[source].astype(F32) + part[source].astype(F32)).astype(BF16)

            @pl.when(is_here(source))
            def _():
                pltpu.make_async_copy(own.at[source], dkv.at[z, half, c], dkv_recv.at[me]).start()

            @pl.when(jnp.logical_not(is_here(source)))
            def _():
                dkv_copy(source).start()

    tokens = tokens_in[...].astype(F32)
    normal, inverse = normalize(tokens)
    normed = (normal * gain_in[...]).astype(BF16)
    for k in range(4):
        cols = slice(k * WIDTH, (k + 1) * WIDTH)
        pre[:, cols] = dot_nn(normed, w_in[:, cols])
    gate = silu(pre[:, 0:WIDTH]).astype(BF16).astype(F32)
    d_gated = dot_nt(cot[...], w_out[...]).astype(BF16).astype(F32)
    onehot = slot_onehot(event_slot[...])
    item_pre = dot_nn(feats[...], item_weight[...])
    item_slope = silu_slope(item_pre)

    @pl.loop(0, SEQ)
    def _(w):
        arrived(mq.at[w % 4, :, ((w // 4) % 2) * 2 + w // 8], mq_recv.at[w])

    mixed = jnp.concatenate([mq[h, :, :, :, 0:HEAD].reshape(ROWS, HEAD) for h in range(HEADS)], axis=1)
    normed_mid = normalize(mixed.astype(F32))[0] * gain_mid[...]
    gated = (normed_mid * gate).astype(BF16)
    layer_out[...] = (tokens + dot_nn(gated, w_out[...])).astype(BF16)
    d_pre[...] = (d_gated * normed_mid * silu_slope(pre[:, 0:WIDTH])).astype(BF16)
    d_normed = dot_nt(d_pre[...], w_in[:, 0:WIDTH])
    d_query = jnp.concatenate(
        [mq[h, :, :, :, HEAD : 2 * HEAD].reshape(ROWS, HEAD) for h in range(HEADS)], axis=1
    )
    d_pre[...] = (d_query.astype(F32) * silu_slope(pre[:, 1024:1536])).astype(BF16)
    d_normed += dot_nt(d_pre[...], w_in[:, 1024:1536])

    @pl.loop(0, SEQ)
    def _(w):
        arrived(dkv.at[w % 4, (w // 4) % 2, w // 8], dkv_recv.at[w])

    for lanes, first_column in ((0, 1536), (HEAD, 512)):
        grad = jnp.concatenate(
            [
                dkv[h, 0, :, :, lanes : lanes + HEAD].reshape(ROWS, HEAD).astype(F32)
                + dkv[h, 1, :, :, lanes : lanes + HEAD].reshape(ROWS, HEAD).astype(F32)
                for h in range(HEADS)
            ],
            axis=1,
        )
        d_pre[...] = (grad * silu_slope(pre[:, first_column : first_column + WIDTH])).astype(BF16)
        d_normed += dot_nt(d_pre[...], w_in[:, first_column : first_column + WIDTH])

    scaled = d_normed * gain_in[...]
    d_tokens = cot[...].astype(F32) + inverse * (
        scaled
        - jnp.mean(scaled, axis=-1, keepdims=True)
        - normal * jnp.mean(scaled * normal, axis=-1, keepdims=True)
    )
    out2[...] = dot_nn(onehot, d_tokens.astype(BF16)).astype(BF16)
    wait_all(exchange_seq(out2, in2, send2, recv2, b, s))
    out1[...] = dot_nn(by_batch(), in2[...]).astype(BF16)
    last = exchange_batch(out1, in1, send1, recv1, b, s)
    wanted = (iota((256, 256), 0) == send_rows[...]).astype(BF16)
    wait_all(last)
    d_embedded = dot_nn(wanted, in1[...])
    d_item = (d_embedded * item_slope).astype(BF16)
    item_grad[...] = dot_nt(d_item, item_weight[...])

    @pl.loop(0, 4)
    def _(g):
        part_copy(g).wait_send()

    @pl.loop(0, SEQ)
    def _(source):
        @pl.when(jnp.logical_not(is_here(source)))
        def _():
            mq_copy(source).wait_send()
            dkv_copy(source).wait_send()


def spec(space):
    return pl.BlockSpec(memory_space=space)


VMEM, SMEM, ANY = pltpu.VMEM, pltpu.SMEM, pl.ANY
DMA = pltpu.SemaphoreType.DMA


def shape(dims, dtype):
    return jax.ShapeDtypeStruct(dims, dtype)


def params(remote=None):
    return pltpu.CompilerParams(
        vmem_limit_bytes=56 << 20, has_side_effects=remote is not None, collective_id=remote
    )


def forward_call(meta, kv, qp):
    return pl.pallas_call(
        forward_kernel,
        out_shape=(shape((TILES, BLOCK, HEAD), F32), shape((TILES, 8, BLOCK), F32)),
        in_specs=[spec(SMEM), spec(VMEM), spec(VMEM)],
        out_specs=(spec(VMEM), spec(VMEM)),
        scratch_shapes=[VMEM((TILES + 1, BLOCK, HEAD), F32)],
        compiler_params=params(),
        name="forward",
    )(meta, kv, qp)


def backward_call(meta, kv, qp, mixed, stats):
    return pl.pallas_call(
        backward_kernel,
        out_shape=(shape((BLOCKS, PIECE, 2 * HEAD), BF16), shape((BLOCKS, BLOCK, 2 * HEAD), BF16)),
        in_specs=[spec(SMEM), spec(VMEM), spec(VMEM), spec(VMEM), spec(VMEM)],
        out_specs=(spec(VMEM), spec(VMEM)),
        scratch_shapes=[
            VMEM((TILES + 1, BLOCK, HEAD), BF16),
            VMEM((TILES + 1, BLOCK, HEAD), F32),
            VMEM((BLOCKS * BLOCK, 2 * HEAD), F32),
        ],
        compiler_params=params(),
        name="backward",
    )(meta, kv, qp, mixed, stats)


def per_device(
    item_feats, item_weight, send_rows, event_slot, user_blocks, tail_len, block_order, gain_in, gain_mid, w_in, w_out,
    cot_out,
):
    event_slot = event_slot.reshape(1, ROWS)
    gain_in, gain_mid = gain_in.reshape(1, WIDTH), gain_mid.reshape(1, WIDTH)
    kv, qp, tokens, meta = pl.pallas_call(
        send_kernel,
        out_shape=(
            shape((SEQ, 2, HALF, 2 * HEAD), BF16),
            shape((SEQ, 3, PIECE, 2 * HEAD), BF16),
            shape((ROWS, WIDTH), BF16),
            shape((8, 128), jnp.int32),
        ),
        in_specs=[spec(VMEM)] * 12,
        out_specs=(spec(ANY), spec(ANY), spec(VMEM), spec(VMEM)),
        scratch_shapes=[VMEM((256, WIDTH), BF16)] * 4
        + [
            VMEM((HEADS, 2, HALF, 2 * HEAD), BF16),
            VMEM((HEADS, 3, 4, PIECE, 2 * HEAD), BF16),
            VMEM((8, 128), jnp.int32),
            VMEM((8, 128), jnp.int32),
            DMA((GROUPS,)),
            DMA((GROUPS,)),
            DMA((SEQ,)),
            DMA((SEQ,)),
        ]
        + [DMA((SEQ,))] * 6
        + [DMA, DMA],
        compiler_params=params(0),
        name="send",
    )(
        item_feats, item_weight, send_rows, event_slot, user_blocks, tail_len, block_order, gain_in, gain_mid, w_in,
        w_out, cot_out,
    )
    kv = kv.reshape(BLOCKS, BLOCK, 2 * HEAD)
    qp = qp.reshape(BLOCKS, PIECE, 2 * HEAD)
    mixed, stats = forward_call(meta, kv, qp)
    stats = pl.pallas_call(
        stats_kernel,
        out_shape=shape((HEADS, TILES, 8, BLOCK), F32),
        in_specs=[spec(VMEM)],
        out_specs=spec(VMEM),
        scratch_shapes=[VMEM((HEADS, TILES, 8, BLOCK), F32), DMA((HEADS,)), DMA((HEADS,))],
        compiler_params=params(1),
        name="stats",
    )(stats)
    mq, dkv = backward_call(meta, kv, qp, mixed, stats)
    mq = mq.reshape(SEQ, 3, PIECE, 2 * HEAD)
    dkv = dkv.reshape(SEQ, 2, HALF, 2 * HEAD)
    return pl.pallas_call(
        return_kernel,
        out_shape=(shape((ROWS, WIDTH), BF16), shape((256, WIDTH), F32)),
        in_specs=[spec(VMEM)] * 10 + [spec(ANY)] * 2,
        out_specs=(spec(VMEM), spec(VMEM)),
        scratch_shapes=[
            VMEM((HEADS, 3, 4, PIECE, 2 * HEAD), BF16),
            VMEM((HEADS, 2, 2, HALF, 2 * HEAD), BF16),
            VMEM((SEQ, HALF, 2 * HEAD), BF16),
            VMEM((SEQ, HALF, 2 * HEAD), BF16),
            VMEM((ROWS, 4 * WIDTH), F32),
            VMEM((ROWS, WIDTH), BF16),
        ]
        + [VMEM((256, WIDTH), BF16)] * 4
        + [DMA((4,))] * 3
        + [DMA((SEQ,))] * 6
        + [DMA((GROUPS,))] * 2,
        compiler_params=params(2),
        name="give_back",
    )(
        item_feats, item_weight, send_rows, event_slot, gain_in, gain_mid, w_in, w_out, cot_out, tokens, mq, dkv,
    )


def solution(mesh):
    rows = P(("batch", "seq"), None)
    return jax.shard_map(
        per_device,
        mesh=mesh,
        in_specs=(
            rows,
            P(),
            rows,
            P(("batch", "seq")),
            P("batch", None),
            P("batch", None),
            P("batch", None),
            P(),
            P(),
            P(),
            P(),
            rows,
        ),
        out_specs=(rows, rows),
        check_vma=False,
    )
```

```python
import jax
import jax.numpy as jnp
from jax import lax
from jax.experimental import pallas as pl
from jax.experimental.pallas import tpu as pltpu
from jax.sharding import PartitionSpec as P

WIDTH = 512
HEAD = 128
HEADS = 4
BLOCK = 128
BLOCKS = 48
SEQ = 16
GROUPS = 8
PIECE = 32
TILES = 12
SLOTS = 256
HALF = 128
ROWS = 384
FAR = 1 << 20
AT_ONCE = 4
BACK_AT_ONCE = 4
SCALE = HEAD**-0.5
MESH = pl.DeviceIdType.MESH
F32 = jnp.float32
BF16 = jnp.bfloat16


def dot_nn(a, b):
    return jnp.dot(a, b, preferred_element_type=F32)


def dot_nt(a, b):
    return lax.dot_general(a, b, (((1,), (1,)), ((), ())), preferred_element_type=F32)


def dot_tn(a, b):
    return lax.dot_general(a, b, (((0,), (0,)), ((), ())), preferred_element_type=F32)


def silu(v):
    u = 0.5 * v
    return u + u * jnp.tanh(u)


def silu_slope(v):
    u = 0.5 * v
    t = jnp.tanh(u)
    a = 1.0 + t
    return 0.5 * (a + u * a * (1.0 - t))


def normalize(values):
    mean = jnp.mean(values, axis=-1, keepdims=True)
    centred = values - mean
    spread = jnp.mean(centred * centred, axis=-1, keepdims=True)
    inverse = lax.rsqrt(spread + 1e-05)
    return centred * inverse, inverse


def iota(shape, dim):
    return lax.broadcasted_iota(jnp.int32, shape, dim)


def place():
    b, s = lax.axis_index("batch"), lax.axis_index("seq")
    return b, s, b // 2, b % 2, s // 4, s % 4


def worker_at(w, x, c):
    head, half, core = w % 4, (w // 4) % 2, w // 8
    return head, half, core, x * 2 + core, (2 * c + half) * 4 + head


def copy_to(src, dst, send, recv, batch, seq):
    return pltpu.make_async_remote_copy(
        src_ref=src, dst_ref=dst, send_sem=send, recv_sem=recv, device_id=(batch, seq), device_id_type=MESH
    )


def arrived(ref, sem):
    pltpu.make_async_copy(ref, ref, sem).wait()


def rows_of(index, size):
    return pl.ds(pl.multiple_of(index * size, size), size)


def slot_rows(event_slot):
    e = event_slot
    return ((e >> 1) & 15) * 16 + (e >> 5) * 2 + (e & 1)


def slot_onehot(wanted):
    return (iota((SLOTS, wanted.shape[1]), 0) == wanted).astype(BF16)


def by_seq():
    i, j = iota((256, 256), 0), iota((256, 256), 1)
    return (j == ((i >> 1) & 7) * 32 + (i >> 4) * 2 + (i & 1)).astype(BF16)


def by_batch():
    i, j = iota((256, 256), 0), iota((256, 256), 1)
    return (j == ((i >> 1) & 15) * 16 + (i >> 5) * 2 + (i & 1)).astype(BF16)


def exchange_batch(src, dst, send, recv, b, s):
    copies = []
    for k in range(1, GROUPS):
        peer = lax.rem(b + k, GROUPS)
        copy = copy_to(src.at[rows_of(peer, 32)], dst.at[rows_of(b, 32)], send.at[k], recv.at[k], peer, s)
        copy.start()
        copies.append(copy)
    dst[rows_of(b, 32), :] = src[rows_of(b, 32), :]
    return copies


def exchange_seq(src, dst, send, recv, b, s):
    copies = []
    for k in range(1, SEQ):
        peer = lax.rem(s + k, SEQ)
        copy = copy_to(src.at[rows_of(peer, 16)], dst.at[rows_of(s, 16)], send.at[k], recv.at[k], b, peer)
        copy.start()
        copies.append(copy)
    dst[rows_of(s, 16), :] = src[rows_of(s, 16), :]
    return copies


def signal(barrier, batch, seq):
    pl.semaphore_signal(barrier, inc=1, device_id=(batch, seq), device_id_type=MESH)


def greet(b, s, partner):
    barrier = pltpu.get_barrier_semaphore()
    for k in range(1, GROUPS):
        signal(barrier, lax.rem(b + k, GROUPS), s)

    @pl.loop(1, SEQ)
    def _(k):
        peer = lax.rem(s + k, SEQ)
        signal(barrier, b, peer)
        signal(barrier, partner, peer)


def greeted():
    pl.semaphore_wait(pltpu.get_barrier_semaphore(), GROUPS - 1 + 2 * (SEQ - 1))


def wait_all(copies):
    for copy in copies:
        copy.wait()


def send_kernel(
    feats, item_weight, send_rows, event_slot, user_blocks, tail_len, block_order, gain_in, gain_mid,
    w_in_hbm, w_out_hbm, cot_hbm,
    kv_out, qp_out, slots_out, ids_out, meta_out,
    w_in, w_out, cot, out1, in1, out2, in2, kv, qp, ids, ids_in,
    load_sem, send1, recv1, send2, recv2, kv_send, kv_recv, pass_send, pass_recv, qp_send, qp_recv, ids_send, ids_recv,
):
    b, s, x, c, y, z = place()
    partner = x * 2 + 1 - c
    greet(b, s, partner)
    loads = [
        pltpu.make_async_copy(src, dst, load_sem.at[k])
        for k, (src, dst) in enumerate(((w_out_hbm, w_out), (cot_hbm, cot), (w_in_hbm, w_in)))
    ]
    for load in loads:
        load.start()

    embedded = silu(dot_nn(feats[...], item_weight[...])).astype(BF16)
    wanted = (iota((256, 256), 0) == send_rows[...]).astype(BF16)
    out1[...] = dot_tn(wanted, embedded).astype(BF16)
    slot_of_event = slot_rows(event_slot[...].reshape(1, ROWS))
    ids[...] = jnp.zeros_like(ids)
    for k in range(3):
        ids[k : k + 1, :] = slot_of_event[:, k * BLOCK : (k + 1) * BLOCK]
    ids[3:4, 0:BLOCKS] = block_order[...]
    ids[4:5, 0:4] = user_blocks[...]
    ids[5:6, 0:4] = tail_len[...]
    greeted()
    first = exchange_batch(out1, in1, send1, recv1, b, s)

    def each_worker(act):
        @pl.loop(0, SEQ)
        def _(i):
            w = lax.rem(i + s, SEQ)
            head, half, core, to_batch, to_seq = worker_at(w, x, c)
            here = (to_batch == b) & (to_seq == s)
            act(w, head, half, core, to_batch, to_seq, here)

    def start(here, src, dst, recv, remote):
        @pl.when(here)
        def _():
            pltpu.make_async_copy(src, dst, recv).start()

        @pl.when(jnp.logical_not(here))
        def _():
            remote.start()

    def ids_copy(w, to_batch, to_seq):
        return copy_to(ids, ids_in.at[s], ids_send.at[w], ids_recv.at[s], to_batch, to_seq)

    def start_ids(w, head, half, core, to_batch, to_seq, here):
        start(here, ids, ids_in.at[s], ids_recv.at[s], ids_copy(w, to_batch, to_seq))

    each_worker(start_ids)

    loads[0].wait()
    loads[1].wait()
    d_gated = dot_nt(cot[...], w_out[...]).astype(BF16)
    wait_all(first)
    out2[...] = dot_nn(by_seq(), in1[...]).astype(BF16)
    second = exchange_seq(out2, in2, send2, recv2, b, s)
    onehot = slot_onehot(slot_of_event)
    loads[2].wait()
    wait_all(second)
    slots_out[...] = in2[...]
    normed = (normalize(in2[...].astype(F32))[0] * gain_in[...]).astype(BF16)

    for part, first_column in ((0, 1536), (1, 512)):
        lanes = slice(part * HEAD, part * HEAD + HEAD)
        made = silu(dot_nn(normed, w_in[:, first_column : first_column + WIDTH])).astype(BF16)
        for h in range(HEADS):
            kv[h, 0, :, lanes] = made[:HALF, h * HEAD : (h + 1) * HEAD]
            kv[h, 1, :, lanes] = made[HALF:, h * HEAD : (h + 1) * HEAD]

    def kv_copy(w, head, core, to_batch, to_seq):
        return copy_to(kv.at[head, core], kv_out.at[s, core], kv_send.at[w], kv_recv.at[s], to_batch, to_seq)

    def start_kv(w, head, half, core, to_batch, to_seq, here):
        start(
            here, kv.at[head, core], kv_out.at[s, core], kv_recv.at[s], kv_copy(w, head, core, to_batch, to_seq)
        )

    each_worker(start_kv)

    query = silu(dot_nn(normed, w_in[:, 1024:1536])).astype(BF16)
    query = dot_tn(onehot, query).astype(BF16)
    gate = silu(dot_nn(normed, w_in[:, 0:WIDTH])).astype(BF16)
    gate = dot_tn(onehot, gate)
    upstream = (d_gated.astype(F32) * gate * gain_mid[...]).astype(BF16)
    for h in range(HEADS):
        cols = slice(h * HEAD, (h + 1) * HEAD)
        qp[h, :, :, :, 0:HEAD] = query[:, cols].reshape(3, 4, PIECE, HEAD)
        qp[h, :, :, :, HEAD : 2 * HEAD] = upstream[:, cols].reshape(3, 4, PIECE, HEAD)

    def qp_copy(w, head, half, core, to_batch, to_seq):
        return copy_to(
            qp.at[head, :, half * 2 + core], qp_out.at[s], qp_send.at[w], qp_recv.at[s], to_batch, to_seq
        )

    def start_qp(w, head, half, core, to_batch, to_seq, here):
        start(
            here, qp.at[head, :, half * 2 + core], qp_out.at[s], qp_recv.at[s],
            qp_copy(w, head, half, core, to_batch, to_seq),
        )

    each_worker(start_qp)

    @pl.loop(0, SEQ)
    def _(source):
        arrived(ids_in.at[source], ids_recv.at[source])

    ids_out[...] = ids_in[...]
    meta_out[...] = tables_of(ids_in[s], (y % 2) * 2 + c)

    def pass_on(source):
        return copy_to(
            kv_out.at[source, c], kv_out.at[source, c], pass_send.at[source], pass_recv.at[source], partner, s
        )

    @pl.loop(0, SEQ)
    def _(i):
        source = lax.rem(s - i + SEQ, SEQ)
        arrived(kv_out.at[source, c], kv_recv.at[source])
        pass_on(source).start()

    def finish(w, head, half, core, to_batch, to_seq, here):
        @pl.when(jnp.logical_not(here))
        def _():
            ids_copy(w, to_batch, to_seq).wait_send()
            kv_copy(w, head, core, to_batch, to_seq).wait_send()
            qp_copy(w, head, half, core, to_batch, to_seq).wait_send()

    each_worker(finish)

    @pl.loop(0, SEQ)
    def _(source):
        pass_on(source).wait_send()
        arrived(kv_out.at[source, 1 - c], pass_recv.at[source])
        arrived(qp_out.at[source], qp_recv.at[source])


def tables_of(meta, quarter):
    slot, lane = iota((128, 128), 0), iota((1, 128), 1)
    held = jnp.transpose(jnp.broadcast_to(meta[3:4, :].astype(F32), (128, 128)))
    slot_of = jnp.where((held == iota((128, 128), 1).astype(F32)) & (slot < BLOCKS), slot.astype(F32), 0.0)
    slot_of = jnp.sum(slot_of, axis=0, keepdims=True).astype(jnp.int32)
    first = jnp.zeros((1, 1), jnp.int32)
    start_of = jnp.zeros((1, 128), jnp.int32)
    limit_of = jnp.full((1, 128), BLOCK, jnp.int32)
    for u in range(4):
        start_of = jnp.where(lane >= first, first, start_of)
        first = first + meta[4:5, u : u + 1]
        limit_of = jnp.where(lane == first - 1, meta[5:6, u : u + 1], limit_of)
    start_of = jnp.where(lane < BLOCKS, start_of, FAR)
    row = iota((8, 128), 0)
    picked = pick4(row, [slot_of, start_of, limit_of, jnp.zeros((1, 128), jnp.int32) + quarter])
    return jnp.where(row == 4, meta[3:4, :], picked)


def pick4(index, values):
    return jnp.where(index == 0, values[0], jnp.where(index == 1, values[1], jnp.where(index == 2, values[2], values[3])))


def first_chunk(meta, t):
    return jnp.minimum(meta[1, 4 * t] // 4, TILES - 1)


def walk(meta, t, j, count):
    pairs = []
    for _ in range(count):
        pairs.append((t, j))
        more = j < jnp.minimum(t, TILES - 1)
        after = jnp.minimum(t + 1, TILES)
        j = jnp.where(more, j + 1, first_chunk(meta, after))
        t = jnp.where(more, t, after)
    return pairs, t, j


def pairs_in_all(meta):
    return sum(t + 1 - meta[1, 4 * t] // 4 for t in range(TILES))


def four(ref, meta, n):
    return jnp.concatenate([ref[meta[0, 4 * n + i]] for i in range(4)], axis=0)


def query_bounds(meta, t, r):
    at = (t * 4 + (r >> 5)) * BLOCK + meta[3, 0] * PIECE + (r & 31)
    return at, pick4(r >> 5, [meta[1, t * 4 + i] for i in range(4)]) * BLOCK


def chunk_of(kv, j):
    return kv[pl.ds(j * 4, 4)].reshape(4 * BLOCK, 2 * HEAD)


def key_places(meta, j, dim):
    size = (1, BLOCK) if dim else (BLOCK, 1)
    e = iota(size, dim)
    return jnp.concatenate(
        [jnp.where(e < meta[2, j * 4 + i], (j * 4 + i) * BLOCK + e, FAR) for i in range(4)], axis=dim
    )


def forward_kernel(meta, ids, kv_slots, qp, kv_out, mixed_out, stats_out, kv, total, kv_sem):
    @pl.loop(0, SEQ, unroll=4)
    def _(s):
        rows = jnp.concatenate([ids[s].astype(F32), jnp.zeros((120, 128), F32)], axis=0)
        columns = jnp.transpose(rows)
        for k in range(3):
            onehot = (iota((BLOCK, SLOTS), 1).astype(F32) == columns[:, k : k + 1]).astype(BF16)
            kv[meta[4, s * 3 + k]] = dot_nn(onehot, kv_slots[s]).astype(BF16)

    save = pltpu.make_async_copy(kv, kv_out, kv_sem)
    save.start()

    @pl.loop(0, TILES + 1)
    def _(t):
        total[t] = jnp.zeros((BLOCK, HEAD), F32)

    def step(_, state):
        pairs, t, j = walk(meta, *state, AT_ONCE)
        keyvals = [chunk_of(kv, j) for _, j in pairs]
        us = [
            dot_nt(four(qp, meta, t)[:, :HEAD], keyval[:, :HEAD]) * (0.5 * SCALE)
            for (t, _), keyval in zip(pairs, keyvals)
        ]
        weights = []
        for (t_, j_), u in zip(pairs, us):
            at, since = query_bounds(meta, t_, iota((BLOCK, 1), 0))
            where = key_places(meta, j_, 1)
            w = u + u * jnp.tanh(u)
            weights.append(jnp.where((where <= at) & (where >= since), w, 0.0).astype(BF16))
        for (t_, _), w, keyval in zip(pairs, weights, keyvals):
            total[t_] += dot_nn(w, keyval[:, HEAD:])
        return t, j

    lax.fori_loop(0, (pairs_in_all(meta) + AT_ONCE - 1) // AT_ONCE, step, (jnp.int32(0), jnp.int32(0)))

    @pl.loop(0, TILES, unroll=4)
    def _(t):
        mixed = total[t]
        upstream = four(qp, meta, t)[:, HEAD:].astype(F32)
        mixed_out[t] = mixed
        mean = jnp.mean(mixed, axis=1, keepdims=True)
        centred = mixed - mean
        stats = pick4(
            iota((BLOCK, HEAD), 1),
            [
                mean,
                jnp.sum(centred * centred, axis=1, keepdims=True),
                jnp.sum(upstream, axis=1, keepdims=True),
                jnp.sum(upstream * centred, axis=1, keepdims=True),
            ],
        )
        stats_out[t] = jnp.transpose(stats)[0:8, :]

    save.wait()


def stats_kernel(stats, all_stats, held, send, recv):
    b, s, x, c, y, z = place()
    barrier = pltpu.get_barrier_semaphore()
    for k in range(1, HEADS):
        signal(barrier, b, y * 4 + lax.rem(z + k, HEADS))
    pl.semaphore_wait(barrier, HEADS - 1)
    copies = []
    for k in range(1, HEADS):
        peer = lax.rem(z + k, HEADS)
        copy = copy_to(stats, held.at[z], send.at[k], recv.at[k], b, y * 4 + peer)
        copy.start()
        copies.append(copy)
    held[z] = stats[...]
    wait_all(copies)
    all_stats[...] = held[...]


def backward_kernel(meta, ids, kv, qp, mixed_in, stats_in, mq_out, dkv_out, d_mixed, d_query, dkv):
    @pl.loop(0, TILES)
    def _(t):
        dkv[pl.ds(t * 4 * BLOCK, 4 * BLOCK), :] = jnp.zeros((4 * BLOCK, 2 * HEAD), F32)

    d_mixed[TILES] = jnp.zeros((BLOCK, HEAD), BF16)

    @pl.loop(0, TILES, unroll=4)
    def _(t):
        d_query[t] = jnp.zeros((BLOCK, HEAD), F32)
        mixed = mixed_in[t]
        upstream = four(qp, meta, t)[:, HEAD:].astype(F32)
        stats = [stats_in[h, t] for h in range(HEADS)]
        mean = sum(v[0:1] for v in stats) * 0.25
        spread = sum(v[1:2] + HEAD * (v[0:1] - mean) * (v[0:1] - mean) for v in stats) * (1.0 / WIDTH)
        inverse = lax.rsqrt(spread + 1e-05)
        slant = sum(v[2:3] for v in stats) * (1.0 / WIDTH)
        along = sum(v[3:4] + v[2:3] * (v[0:1] - mean) for v in stats) * (1.0 / WIDTH) * inverse
        columns = jnp.transpose(pick4(iota((BLOCK, HEAD), 0), [mean, inverse, slant, along]))
        mean, inverse, slant, along = (columns[:, i : i + 1] for i in range(4))
        normal = (mixed - mean) * inverse
        d_mixed[t] = (inverse * (upstream - slant - normal * along)).astype(BF16)

    def step(_, state):
        pairs, t, j = walk(meta, *state, BACK_AT_ONCE)
        keyvals = [chunk_of(kv, j) for _, j in pairs]
        queries = [four(qp, meta, t)[:, :HEAD] for t, _ in pairs]
        d_mixeds = [d_mixed[t] for t, _ in pairs]
        us = [dot_nt(keyval[:, :HEAD], query) * (0.5 * SCALE) for keyval, query in zip(keyvals, queries)]
        d_weights = [dot_nt(keyval[:, HEAD:], dm) for keyval, dm in zip(keyvals, d_mixeds)]
        made = []
        for (t_, j_), u, dw in zip(pairs, us, d_weights):
            th = jnp.tanh(u)
            a = 1.0 + th
            w = u * a
            ds = dw * (a + w * (1.0 - th))
            at, since = query_bounds(meta, t_, iota((1, BLOCK), 1))
            where = key_places(meta, j_, 0)
            seen = (where <= at) & (where >= since)
            made.append((jnp.where(seen, w, 0.0).astype(BF16), jnp.where(seen, ds, 0.0).astype(BF16)))
        for (t_, j_), keyval, query, dm, (w, ds) in zip(pairs, keyvals, queries, d_mixeds, made):
            keys = pl.ds(pl.multiple_of(j_ * 4 * BLOCK, 4 * BLOCK), 4 * BLOCK)
            dkv[keys, 0:HEAD] += dot_nn(ds, query)
            dkv[keys, HEAD : 2 * HEAD] += dot_nn(w, dm)
            d_query[t_] += dot_tn(ds, keyval[:, :HEAD])
        return t, j

    lax.fori_loop(0, (pairs_in_all(meta) + BACK_AT_ONCE - 1) // BACK_AT_ONCE, step, (jnp.int32(0), jnp.int32(0)))

    @pl.loop(0, TILES)
    def _(t):
        mixed = mixed_in[t].astype(BF16)
        dq = (d_query[t] * (0.5 * SCALE)).astype(BF16)
        for i in range(4):
            n = t * 4 + i
            slot = meta[0, n]
            rows = slice(i * PIECE, (i + 1) * PIECE)
            mq_out[slot, :, 0:HEAD] = mixed[rows]
            mq_out[slot, :, HEAD : 2 * HEAD] = dq[rows]

    @pl.loop(0, SEQ, unroll=4)
    def _(s):
        total = jnp.zeros((SLOTS, 2 * HEAD), F32)
        for k in range(3):
            keys = pl.ds(pl.multiple_of(meta[4, s * 3 + k] * BLOCK, BLOCK), BLOCK)
            total += dot_nn(slot_onehot(ids[s, k : k + 1, :]), dkv[keys, :].astype(BF16))
        dkv_out[s, :, 0:HEAD] = (total[:, 0:HEAD] * (0.5 * SCALE)).astype(BF16)
        dkv_out[s, :, HEAD : 2 * HEAD] = total[:, HEAD : 2 * HEAD].astype(BF16)


def return_kernel(
    send_rows, event_slot, gain_in, gain_mid, slots_in,
    feats_hbm, item_weight_hbm, w_in_hbm, w_out_hbm, cot_hbm, mq_in, dkv_in,
    layer_out, d_item_out,
    feats, item_weight, w_in, w_out, cot, mq, dkv, own, part, pre, d_pre, out2, in2, out1, in1,
    load_sem, own_sem, part_send, part_recv, mq_send, mq_recv, dkv_send, dkv_recv, send2, recv2, send1, recv1,
):
    b, s, x, c, y, z = place()
    partner = x * 2 + 1 - c
    mine = y // 2
    half = y % 2
    to_batch = x * 2 + mine
    me = z + 4 * half + 8 * c
    greet(b, s, partner)
    loads = [
        pltpu.make_async_copy(src, dst, load_sem.at[k])
        for k, (src, dst) in enumerate(
            (
                (w_in_hbm, w_in),
                (w_out_hbm, w_out),
                (cot_hbm, cot),
                (feats_hbm, feats),
                (item_weight_hbm, item_weight),
            )
        )
    ]
    greeted()

    def group_order(k):
        return lax.rem(k + z, 4)

    def own_copy(g):
        return pltpu.make_async_copy(dkv_in.at[pl.ds(g * 4, 4), c], own.at[pl.ds(g * 4, 4)], own_sem.at[g])

    def part_copy(g):
        return copy_to(
            dkv_in.at[pl.ds(g * 4, 4), 1 - c], part.at[pl.ds(g * 4, 4)], part_send.at[g], part_recv.at[g], partner, s
        )

    @pl.loop(0, 4)
    def _(k):
        g = group_order(k)
        own_copy(g).start()
        part_copy(g).start()

    def is_here(source):
        return (to_batch == b) & (source == s)

    def mq_copy(source):
        return copy_to(
            mq_in.at[source], mq.at[z, :, half * 2 + c], mq_send.at[source], mq_recv.at[me], to_batch, source
        )

    def dkv_copy(source):
        return copy_to(
            own.at[source], dkv.at[z, half, c], dkv_send.at[source], dkv_recv.at[me], to_batch, source
        )

    @pl.loop(0, SEQ)
    def _(i):
        source = lax.rem(i + s, SEQ)

        @pl.when(is_here(source))
        def _():
            pltpu.make_async_copy(mq_in.at[source], mq.at[z, :, half * 2 + c], mq_recv.at[me]).start()

        @pl.when(jnp.logical_not(is_here(source)))
        def _():
            mq_copy(source).start()

    @pl.loop(0, 4)
    def _(k):
        g = group_order(k)
        own_copy(g).wait()
        arrived(part.at[pl.ds(g * 4, 4)], part_recv.at[g])

        @pl.loop(0, 4)
        def _(i):
            source = g * 4 + lax.rem(i + y, 4)
            own[source] = (own[source].astype(F32) + part[source].astype(F32)).astype(BF16)

            @pl.when(is_here(source))
            def _():
                pltpu.make_async_copy(own.at[source], dkv.at[z, half, c], dkv_recv.at[me]).start()

            @pl.when(jnp.logical_not(is_here(source)))
            def _():
                dkv_copy(source).start()

    for load in loads:
        load.start()
    onehot = slot_onehot(slot_rows(event_slot[...].reshape(1, ROWS)))
    normal, inverse = normalize(slots_in[...].astype(F32))
    normed = (normal * gain_in[...]).astype(BF16)
    loads[0].wait()
    for k in range(4):
        cols = slice(k * WIDTH, (k + 1) * WIDTH)
        pre[:, cols] = dot_nn(normed, w_in[:, cols])
    tokens = dot_tn(onehot, slots_in[...])
    gate = dot_tn(onehot, silu(pre[:, 0:WIDTH]).astype(BF16))
    loads[1].wait()
    loads[2].wait()
    d_gated = dot_nt(cot[...], w_out[...]).astype(BF16).astype(F32)
    slot_cot = dot_nn(onehot, cot[...])
    loads[3].wait()
    loads[4].wait()
    item_slope = silu_slope(dot_nn(feats[...], item_weight[...]))

    @pl.loop(0, SEQ)
    def _(w):
        arrived(mq.at[w % 4, :, ((w // 4) % 2) * 2 + w // 8], mq_recv.at[w])

    mixed = jnp.concatenate([mq[h, :, :, :, 0:HEAD].reshape(ROWS, HEAD) for h in range(HEADS)], axis=1)
    normed_mid = normalize(mixed.astype(F32))[0] * gain_mid[...]
    gated = (normed_mid * gate).astype(BF16)
    layer_out[...] = (tokens + dot_nn(gated, w_out[...])).astype(BF16)
    d_gate = dot_nn(onehot, (d_gated * normed_mid).astype(BF16))
    d_pre[...] = (d_gate * silu_slope(pre[:, 0:WIDTH])).astype(BF16)
    d_normed = dot_nt(d_pre[...], w_in[:, 0:WIDTH])
    d_query = jnp.concatenate(
        [mq[h, :, :, :, HEAD : 2 * HEAD].reshape(ROWS, HEAD) for h in range(HEADS)], axis=1
    )
    d_pre[...] = (dot_nn(onehot, d_query) * silu_slope(pre[:, 1024:1536])).astype(BF16)
    d_normed += dot_nt(d_pre[...], w_in[:, 1024:1536])
    for first_column in (512, 1536):
        cols = slice(first_column, first_column + WIDTH)
        pre[:, cols] = silu_slope(pre[:, cols])

    @pl.loop(0, SEQ)
    def _(w):
        arrived(dkv.at[w % 4, (w // 4) % 2, w // 8], dkv_recv.at[w])

    for lanes, first_column in ((0, 1536), (HEAD, 512)):
        cols = slice(first_column, first_column + WIDTH)
        grad = jnp.concatenate(
            [
                dkv[h, 0, :, :, lanes : lanes + HEAD].reshape(SLOTS, HEAD).astype(F32)
                + dkv[h, 1, :, :, lanes : lanes + HEAD].reshape(SLOTS, HEAD).astype(F32)
                for h in range(HEADS)
            ],
            axis=1,
        )
        d_pre[...] = (grad * pre[:, cols]).astype(BF16)
        d_normed += dot_nt(d_pre[...], w_in[:, cols])

    scaled = d_normed * gain_in[...]
    d_slots = slot_cot + inverse * (
        scaled
        - jnp.mean(scaled, axis=-1, keepdims=True)
        - normal * jnp.mean(scaled * normal, axis=-1, keepdims=True)
    )
    out2[...] = d_slots.astype(BF16)
    wait_all(exchange_seq(out2, in2, send2, recv2, b, s))
    out1[...] = dot_nn(by_batch(), in2[...]).astype(BF16)
    last = exchange_batch(out1, in1, send1, recv1, b, s)
    wanted = (iota((256, 256), 0) == send_rows[...]).astype(BF16)
    wait_all(last)
    d_embedded = dot_nn(wanted, in1[...])
    d_item_out[...] = (d_embedded * item_slope).astype(BF16)

    @pl.loop(0, 4)
    def _(g):
        part_copy(g).wait_send()

    @pl.loop(0, SEQ)
    def _(source):
        @pl.when(jnp.logical_not(is_here(source)))
        def _():
            mq_copy(source).wait_send()
            dkv_copy(source).wait_send()


def result_kernel(layer, d_item, item_weight, layer_out, item_grad):
    layer_out[...] = layer[...]
    item_grad[...] = dot_nt(d_item[...], item_weight[...])


def spec(space):
    return pl.BlockSpec(memory_space=space)


VMEM, SMEM, ANY = pltpu.VMEM, pltpu.SMEM, pl.ANY
DMA = pltpu.SemaphoreType.DMA


def shape(dims, dtype):
    return jax.ShapeDtypeStruct(dims, dtype)


def params(remote=None):
    return pltpu.CompilerParams(
        vmem_limit_bytes=56 << 20, has_side_effects=remote is not None, collective_id=remote
    )


def forward_call(meta, ids, kv, qp):
    return pl.pallas_call(
        forward_kernel,
        out_shape=(
            shape((BLOCKS, BLOCK, 2 * HEAD), BF16),
            shape((TILES, BLOCK, HEAD), F32),
            shape((TILES, 8, BLOCK), F32),
        ),
        in_specs=[spec(SMEM), spec(VMEM), spec(VMEM), spec(VMEM)],
        out_specs=(spec(ANY), spec(VMEM), spec(VMEM)),
        scratch_shapes=[VMEM((BLOCKS, BLOCK, 2 * HEAD), BF16), VMEM((TILES + 1, BLOCK, HEAD), F32), DMA],
        compiler_params=params(),
        name="forward",
    )(meta, ids, kv, qp)


def backward_call(meta, ids, kv, qp, mixed, stats):
    return pl.pallas_call(
        backward_kernel,
        out_shape=(shape((BLOCKS, PIECE, 2 * HEAD), BF16), shape((SEQ, SLOTS, 2 * HEAD), BF16)),
        in_specs=[spec(SMEM)] + [spec(VMEM)] * 5,
        out_specs=(spec(VMEM), spec(VMEM)),
        scratch_shapes=[
            VMEM((TILES + 1, BLOCK, HEAD), BF16),
            VMEM((TILES + 1, BLOCK, HEAD), F32),
            VMEM((BLOCKS * BLOCK, 2 * HEAD), F32),
        ],
        compiler_params=params(),
        name="backward",
    )(meta, ids, kv, qp, mixed, stats)


def per_device(
    item_feats, item_weight, send_rows, event_slot, user_blocks, tail_len, block_order, gain_in, gain_mid, w_in, w_out,
    cot_out,
):
    gain_in, gain_mid = gain_in.reshape(1, WIDTH), gain_mid.reshape(1, WIDTH)
    kv, qp, slots, ids, meta = pl.pallas_call(
        send_kernel,
        out_shape=(
            shape((SEQ, 2, HALF, 2 * HEAD), BF16),
            shape((SEQ, 3, PIECE, 2 * HEAD), BF16),
            shape((SLOTS, WIDTH), BF16),
            shape((SEQ, 8, 128), jnp.int32),
            shape((8, 128), jnp.int32),
        ),
        in_specs=[spec(VMEM)] * 9 + [spec(ANY)] * 3,
        out_specs=(spec(ANY), spec(ANY), spec(VMEM), spec(VMEM), spec(VMEM)),
        scratch_shapes=[VMEM((WIDTH, 4 * WIDTH), BF16), VMEM((WIDTH, WIDTH), BF16), VMEM((ROWS, WIDTH), BF16)]
        + [VMEM((256, WIDTH), BF16)] * 4
        + [
            VMEM((HEADS, 2, HALF, 2 * HEAD), BF16),
            VMEM((HEADS, 3, 4, PIECE, 2 * HEAD), BF16),
            VMEM((8, 128), jnp.int32),
            VMEM((SEQ, 8, 128), jnp.int32),
            DMA((3,)),
            DMA((GROUPS,)),
            DMA((GROUPS,)),
        ]
        + [DMA((SEQ,))] * 10,
        compiler_params=params(0),
        name="send",
    )(
        item_feats, item_weight, send_rows, event_slot, user_blocks, tail_len, block_order, gain_in, gain_mid, w_in,
        w_out, cot_out,
    )
    kv = kv.reshape(SEQ, SLOTS, 2 * HEAD)
    qp = qp.reshape(BLOCKS, PIECE, 2 * HEAD)
    kv, mixed, stats = forward_call(meta, ids, kv, qp)
    stats = pl.pallas_call(
        stats_kernel,
        out_shape=shape((HEADS, TILES, 8, BLOCK), F32),
        in_specs=[spec(VMEM)],
        out_specs=spec(VMEM),
        scratch_shapes=[VMEM((HEADS, TILES, 8, BLOCK), F32), DMA((HEADS,)), DMA((HEADS,))],
        compiler_params=params(1),
        name="stats",
    )(stats)
    mq, dkv = backward_call(meta, ids, kv, qp, mixed, stats)
    mq = mq.reshape(SEQ, 3, PIECE, 2 * HEAD)
    dkv = dkv.reshape(SEQ, 2, HALF, 2 * HEAD)
    layer, d_item = pl.pallas_call(
        return_kernel,
        out_shape=(shape((ROWS, WIDTH), BF16), shape((256, WIDTH), BF16)),
        in_specs=[spec(VMEM)] * 5 + [spec(ANY)] * 7,
        out_specs=(spec(VMEM), spec(VMEM)),
        scratch_shapes=[
            VMEM((256, WIDTH), BF16),
            VMEM((WIDTH, WIDTH), BF16),
            VMEM((WIDTH, 4 * WIDTH), BF16),
            VMEM((WIDTH, WIDTH), BF16),
            VMEM((ROWS, WIDTH), BF16),
            VMEM((HEADS, 3, 4, PIECE, 2 * HEAD), BF16),
            VMEM((HEADS, 2, 2, HALF, 2 * HEAD), BF16),
            VMEM((SEQ, HALF, 2 * HEAD), BF16),
            VMEM((SEQ, HALF, 2 * HEAD), BF16),
            VMEM((SLOTS, 4 * WIDTH), F32),
            VMEM((SLOTS, WIDTH), BF16),
        ]
        + [VMEM((256, WIDTH), BF16)] * 4
        + [DMA((5,))]
        + [DMA((4,))] * 3
        + [DMA((SEQ,))] * 6
        + [DMA((GROUPS,))] * 2,
        compiler_params=params(2),
        name="give_back",
    )(
        send_rows, event_slot, gain_in, gain_mid, slots, item_feats, item_weight, w_in, w_out, cot_out, mq, dkv,
    )
    return pl.pallas_call(
        result_kernel,
        out_shape=(shape((ROWS, WIDTH), BF16), shape((256, WIDTH), F32)),
        in_specs=[spec(VMEM)] * 3,
        out_specs=(spec(VMEM), spec(VMEM)),
        compiler_params=params(),
        name="results",
    )(layer, d_item, item_weight)


def solution(mesh):
    rows = P(("batch", "seq"), None)
    return jax.shard_map(
        per_device,
        mesh=mesh,
        in_specs=(
            rows,
            P(),
            rows,
            P(("batch", "seq")),
            P("batch", None),
            P("batch", None),
            P("batch", None),
            P(),
            P(),
            P(),
            P(),
            rows,
        ),
        out_specs=(rows, rows),
        check_vma=False,
    )
```

```python
import jax
import jax.numpy as jnp
from jax import lax
from jax.experimental import pallas as pl
from jax.experimental.pallas import tpu as pltpu
from jax.sharding import PartitionSpec as P

WIDTH = 512
HEAD = 128
HEADS = 4
BLOCK = 128
BLOCKS = 48
SEQ = 16
GROUPS = 8
PIECE = 32
TILES = 12
SLOTS = 256
HALF = 128
ROWS = 384
FAR = 30000
NO_BLOCK = 200
AT_ONCE = 4
BACK_AT_ONCE = 4
SCALE = HEAD**-0.5
MESH = pl.DeviceIdType.MESH
F32 = jnp.float32
BF16 = jnp.bfloat16


def dot_nn(a, b):
    return jnp.dot(a, b, preferred_element_type=F32)


def dot_nt(a, b):
    return lax.dot_general(a, b, (((1,), (1,)), ((), ())), preferred_element_type=F32)


def dot_tn(a, b):
    return lax.dot_general(a, b, (((0,), (0,)), ((), ())), preferred_element_type=F32)


def silu(v):
    u = 0.5 * v
    return u + u * jnp.tanh(u)


def silu_slope(v):
    u = 0.5 * v
    t = jnp.tanh(u)
    a = 1.0 + t
    return 0.5 * (a + u * a * (1.0 - t))


def normalize(values):
    mean = jnp.mean(values, axis=-1, keepdims=True)
    centred = values - mean
    spread = jnp.mean(centred * centred, axis=-1, keepdims=True)
    inverse = lax.rsqrt(spread + 1e-05)
    return centred * inverse, inverse


def iota(shape, dim):
    return lax.broadcasted_iota(jnp.int32, shape, dim)


def place():
    b, s = lax.axis_index("batch"), lax.axis_index("seq")
    return b, s, b // 2, b % 2, s // 4, s % 4


def worker_at(w, x, c):
    head, half, core = w % 4, (w // 4) % 2, w // 8
    return head, half, core, x * 2 + core, (2 * c + half) * 4 + head


def copy_to(src, dst, send, recv, batch, seq):
    return pltpu.make_async_remote_copy(
        src_ref=src, dst_ref=dst, send_sem=send, recv_sem=recv, device_id=(batch, seq), device_id_type=MESH
    )


def arrived(ref, sem):
    pltpu.make_async_copy(ref, ref, sem).wait()


def rows_of(index, size):
    return pl.ds(pl.multiple_of(index * size, size), size)


def slot_rows(event_slot):
    e = event_slot
    return ((e >> 1) & 15) * 16 + (e >> 5) * 2 + (e & 1)


def slot_onehot(wanted):
    return (iota((SLOTS, wanted.shape[1]), 0) == wanted).astype(BF16)


def by_seq():
    i, j = iota((256, 256), 0), iota((256, 256), 1)
    return (j == ((i >> 1) & 7) * 32 + (i >> 4) * 2 + (i & 1)).astype(BF16)


def by_batch():
    i, j = iota((256, 256), 0), iota((256, 256), 1)
    return (j == ((i >> 1) & 15) * 16 + (i >> 5) * 2 + (i & 1)).astype(BF16)


def exchange_batch(src, dst, send, recv, b, s):
    copies = []
    for k in range(1, GROUPS):
        peer = lax.rem(b + k, GROUPS)
        copy = copy_to(src.at[rows_of(peer, 32)], dst.at[rows_of(b, 32)], send.at[k], recv.at[k], peer, s)
        copy.start()
        copies.append(copy)
    dst[rows_of(b, 32), :] = src[rows_of(b, 32), :]
    return copies


def exchange_seq(src, dst, send, recv, b, s):
    copies = []
    for k in range(1, SEQ):
        peer = lax.rem(s + k, SEQ)
        copy = copy_to(src.at[rows_of(peer, 16)], dst.at[rows_of(s, 16)], send.at[k], recv.at[k], b, peer)
        copy.start()
        copies.append(copy)
    dst[rows_of(s, 16), :] = src[rows_of(s, 16), :]
    return copies


def signal(barrier, batch, seq):
    pl.semaphore_signal(barrier, inc=1, device_id=(batch, seq), device_id_type=MESH)


def greet(b, s, partner):
    barrier = pltpu.get_barrier_semaphore()
    for k in range(1, GROUPS):
        signal(barrier, lax.rem(b + k, GROUPS), s)

    @pl.loop(1, SEQ)
    def _(k):
        peer = lax.rem(s + k, SEQ)
        signal(barrier, b, peer)
        signal(barrier, partner, peer)


def greeted():
    pl.semaphore_wait(pltpu.get_barrier_semaphore(), GROUPS - 1 + 2 * (SEQ - 1))


def wait_all(copies):
    for copy in copies:
        copy.wait()


def send_kernel(
    feats, item_weight, send_rows, event_slot, user_blocks, tail_len, block_order, gain_in, gain_mid,
    w_in_hbm, w_out_hbm, cot_hbm,
    kv_out, qp_out, slots_out, ids_out, meta_out,
    w_in, w_out, cot, out1, in1, out2, in2, kv, qp, ids, ids_in, kv_in, kv_events,
    load_sem, save_sem, send1, recv1, send2, recv2, kv_send, kv_recv, pass_send, pass_recv, qp_send, qp_recv, ids_send, ids_recv,
):
    b, s, x, c, y, z = place()
    partner = x * 2 + 1 - c
    greet(b, s, partner)
    loads = [
        pltpu.make_async_copy(src, dst, load_sem.at[k])
        for k, (src, dst) in enumerate(((w_out_hbm, w_out), (cot_hbm, cot), (w_in_hbm, w_in)))
    ]
    for load in loads:
        load.start()

    embedded = silu(dot_nn(feats[...], item_weight[...])).astype(BF16)
    wanted = (iota((256, 256), 0) == send_rows[...]).astype(BF16)
    out1[...] = dot_tn(wanted, embedded).astype(BF16)
    slot_of_event = slot_rows(event_slot[...].reshape(1, ROWS))
    ids[...] = jnp.zeros_like(ids)
    for k in range(3):
        ids[k : k + 1, :] = slot_of_event[:, k * BLOCK : (k + 1) * BLOCK]
    ids[3:4, 0:BLOCKS] = block_order[...]
    ids[4:5, 0:4] = user_blocks[...]
    ids[5:6, 0:4] = tail_len[...]
    greeted()
    first = exchange_batch(out1, in1, send1, recv1, b, s)

    def each_worker(act):
        @pl.loop(0, SEQ)
        def _(i):
            w = lax.rem(i + s, SEQ)
            head, half, core, to_batch, to_seq = worker_at(w, x, c)
            here = (to_batch == b) & (to_seq == s)
            act(w, head, half, core, to_batch, to_seq, here)

    def start(here, src, dst, recv, remote):
        @pl.when(here)
        def _():
            pltpu.make_async_copy(src, dst, recv).start()

        @pl.when(jnp.logical_not(here))
        def _():
            remote.start()

    def ids_copy(w, to_batch, to_seq):
        return copy_to(ids, ids_in.at[s], ids_send.at[w], ids_recv.at[s], to_batch, to_seq)

    def start_ids(w, head, half, core, to_batch, to_seq, here):
        start(here, ids, ids_in.at[s], ids_recv.at[s], ids_copy(w, to_batch, to_seq))

    each_worker(start_ids)

    loads[0].wait()
    loads[1].wait()
    d_gated = dot_nt(cot[...], w_out[...]).astype(BF16)
    wait_all(first)
    out2[...] = dot_nn(by_seq(), in1[...]).astype(BF16)
    second = exchange_seq(out2, in2, send2, recv2, b, s)
    onehot = slot_onehot(slot_of_event)
    loads[2].wait()
    wait_all(second)
    slots_out[...] = in2[...]
    normed = (normalize(in2[...].astype(F32))[0] * gain_in[...]).astype(BF16)

    for part, first_column in ((0, 1536), (1, 512)):
        lanes = slice(part * HEAD, part * HEAD + HEAD)
        made = silu(dot_nn(normed, w_in[:, first_column : first_column + WIDTH])).astype(BF16)
        for h in range(HEADS):
            kv[h, 0, :, lanes] = made[:HALF, h * HEAD : (h + 1) * HEAD]
            kv[h, 1, :, lanes] = made[HALF:, h * HEAD : (h + 1) * HEAD]

    def kv_copy(w, head, core, to_batch, to_seq):
        return copy_to(kv.at[head, core], kv_in.at[s, core], kv_send.at[w], kv_recv.at[s], to_batch, to_seq)

    def start_kv(w, head, half, core, to_batch, to_seq, here):
        start(
            here, kv.at[head, core], kv_in.at[s, core], kv_recv.at[s], kv_copy(w, head, core, to_batch, to_seq)
        )

    each_worker(start_kv)

    query = (silu(dot_nn(normed, w_in[:, 1024:1536])) * (0.5 * SCALE)).astype(BF16)
    query = dot_tn(onehot, query).astype(BF16)
    gate = silu(dot_nn(normed, w_in[:, 0:WIDTH])).astype(BF16)
    gate = dot_tn(onehot, gate)
    upstream = (d_gated.astype(F32) * gate * gain_mid[...]).astype(BF16)
    for h in range(HEADS):
        cols = slice(h * HEAD, (h + 1) * HEAD)
        qp[h, :, :, :, 0:HEAD] = query[:, cols].reshape(3, 4, PIECE, HEAD)
        qp[h, :, :, :, HEAD : 2 * HEAD] = upstream[:, cols].reshape(3, 4, PIECE, HEAD)

    def qp_copy(w, head, half, core, to_batch, to_seq):
        return copy_to(
            qp.at[head, :, half * 2 + core], qp_out.at[s], qp_send.at[w], qp_recv.at[s], to_batch, to_seq
        )

    def start_qp(w, head, half, core, to_batch, to_seq, here):
        start(
            here, qp.at[head, :, half * 2 + core], qp_out.at[s], qp_recv.at[s],
            qp_copy(w, head, half, core, to_batch, to_seq),
        )

    each_worker(start_qp)

    @pl.loop(0, SEQ)
    def _(source):
        arrived(ids_in.at[source], ids_recv.at[source])

    ids_out[...] = ids_in[...]
    meta_out[...] = tables_of(ids_in[s], (y % 2) * 2 + c)

    def pass_on(source):
        return copy_to(
            kv_in.at[source, c], kv_in.at[source, c], pass_send.at[source], pass_recv.at[source], partner, s
        )

    def save(source):
        return pltpu.make_async_copy(kv_events.at[source], kv_out.at[source], save_sem.at[source])

    @pl.loop(0, SEQ + 2)
    def _(i):
        @pl.when(i < SEQ)
        def _():
            source = lax.rem(s - i + SEQ, SEQ)
            arrived(kv_in.at[source, c], kv_recv.at[source])
            pass_on(source).start()

        @pl.when(i >= 2)
        def _():
            source = lax.rem(s - i + 2 + SEQ, SEQ)
            arrived(kv_in.at[source, 1 - c], pass_recv.at[source])
            rows = jnp.concatenate([ids_in[source].astype(F32), jnp.zeros((120, 128), F32)], axis=0)
            columns = jnp.transpose(rows)
            lane = iota((BLOCK, SLOTS), 1).astype(F32)
            read = jnp.concatenate([(lane == columns[:, k : k + 1]).astype(BF16) for k in range(3)], axis=0)
            slots = kv_in[source].reshape(SLOTS, 2 * HEAD)
            kv_events[source] = dot_nn(read, slots).astype(BF16).reshape(3, BLOCK, 2 * HEAD)
            save(source).start()

    def finish(w, head, half, core, to_batch, to_seq, here):
        @pl.when(jnp.logical_not(here))
        def _():
            ids_copy(w, to_batch, to_seq).wait_send()
            kv_copy(w, head, core, to_batch, to_seq).wait_send()
            qp_copy(w, head, half, core, to_batch, to_seq).wait_send()

    each_worker(finish)

    @pl.loop(0, SEQ)
    def _(source):
        pass_on(source).wait_send()
        arrived(qp_out.at[source], qp_recv.at[source])
        save(source).wait()


def tables_of(meta, quarter):
    slot, lane = iota((128, 128), 0), iota((1, 128), 1)
    held = jnp.transpose(jnp.broadcast_to(meta[3:4, :].astype(F32), (128, 128)))
    slot_of = jnp.where((held == iota((128, 128), 1).astype(F32)) & (slot < BLOCKS), slot.astype(F32), 0.0)
    slot_of = jnp.sum(slot_of, axis=0, keepdims=True).astype(jnp.int32)
    first = jnp.zeros((1, 1), jnp.int32)
    start_of = jnp.zeros((1, 128), jnp.int32)
    limit_of = jnp.full((1, 128), BLOCK, jnp.int32)
    for u in range(4):
        start_of = jnp.where(lane >= first, first, start_of)
        first = first + meta[4:5, u : u + 1]
        limit_of = jnp.where(lane == first - 1, meta[5:6, u : u + 1], limit_of)
    start_of = jnp.where(lane < BLOCKS, start_of, NO_BLOCK)
    row = iota((8, 128), 0)
    picked = pick4(row, [slot_of, start_of, limit_of, jnp.zeros((1, 128), jnp.int32) + quarter])
    return jnp.where(row == 4, meta[3:4, :], picked)


def pick4(index, values):
    return jnp.where(index == 0, values[0], jnp.where(index == 1, values[1], jnp.where(index == 2, values[2], values[3])))


def first_chunk(meta, t):
    return jnp.minimum(meta[1, 4 * t] // 4, TILES - 1)


def walk(meta, t, j, count):
    pairs = []
    for _ in range(count):
        pairs.append((t, j))
        more = j < jnp.minimum(t, TILES - 1)
        after = jnp.minimum(t + 1, TILES)
        j = jnp.where(more, j + 1, first_chunk(meta, after))
        t = jnp.where(more, t, after)
    return pairs, t, j


def pairs_in_all(meta):
    return sum(t + 1 - meta[1, 4 * t] // 4 for t in range(TILES))


def four(ref, meta, n):
    return jnp.concatenate([ref[meta[0, 4 * n + i]] for i in range(4)], axis=0)


def visible(meta, t, j):
    r, lane = iota((BLOCK, 1), 0), iota((1, BLOCK), 1)
    at = (t * 4 + (r >> 5)) * BLOCK + meta[3, 0] * PIECE + (r & 31)
    since = pick4(r >> 5, [meta[1, t * 4 + i] for i in range(4)]) * BLOCK
    where = jnp.concatenate(
        [jnp.where(lane < meta[2, j * 4 + i], (j * 4 + i) * BLOCK + lane, FAR) for i in range(4)], axis=1
    )
    where, at, since = (v.astype(jnp.int16) for v in (where, at, since))
    return (where <= at) & (where >= since)


def forward_kernel(meta, kv, qp, mixed_out, stats_out, total):
    @pl.loop(0, TILES + 1)
    def _(t):
        total[t] = jnp.zeros((BLOCK, HEAD), F32)

    def step(_, state):
        pairs, t, j = walk(meta, *state, AT_ONCE)
        keyvals = [four(kv, meta, j) for _, j in pairs]
        us = [dot_nt(four(qp, meta, t)[:, :HEAD], keyval[:, :HEAD]) for (t, _), keyval in zip(pairs, keyvals)]
        weights = []
        for (t_, j_), u in zip(pairs, us):
            w = u.astype(BF16) * (1.0 + jnp.tanh(u)).astype(BF16)
            weights.append(jnp.where(visible(meta, t_, j_), w, jnp.zeros_like(w)))
        for (t_, _), w, keyval in zip(pairs, weights, keyvals):
            total[t_] += dot_nn(w, keyval[:, HEAD:])
        return t, j

    lax.fori_loop(0, (pairs_in_all(meta) + AT_ONCE - 1) // AT_ONCE, step, (jnp.int32(0), jnp.int32(0)))

    @pl.loop(0, TILES, unroll=4)
    def _(t):
        mixed = total[t]
        upstream = four(qp, meta, t)[:, HEAD:].astype(F32)
        mixed_out[t] = mixed
        mean = jnp.mean(mixed, axis=1, keepdims=True)
        centred = mixed - mean
        stats = pick4(
            iota((BLOCK, HEAD), 1),
            [
                mean,
                jnp.sum(centred * centred, axis=1, keepdims=True),
                jnp.sum(upstream, axis=1, keepdims=True),
                jnp.sum(upstream * centred, axis=1, keepdims=True),
            ],
        )
        stats_out[t] = jnp.transpose(stats)[0:8, :]


def stats_kernel(stats, all_stats, held, send, recv):
    b, s, x, c, y, z = place()
    barrier = pltpu.get_barrier_semaphore()
    for k in range(1, HEADS):
        signal(barrier, b, y * 4 + lax.rem(z + k, HEADS))
    pl.semaphore_wait(barrier, HEADS - 1)
    copies = []
    for k in range(1, HEADS):
        peer = lax.rem(z + k, HEADS)
        copy = copy_to(stats, held.at[z], send.at[k], recv.at[k], b, y * 4 + peer)
        copy.start()
        copies.append(copy)
    held[z] = stats[...]
    wait_all(copies)
    all_stats[...] = held[...]


def backward_kernel(
    meta, ids, qp, mixed_in, stats_in, kv_hbm, mq_hbm, dkv_hbm,
    kv, mq, dkv_slots, d_mixed, query_t, d_mixed_t, d_query, dkv, kv_sem, mq_sem, dkv_sem,
):
    load = pltpu.make_async_copy(kv_hbm, kv, kv_sem)
    load.start()
    d_mixed[TILES] = jnp.zeros((BLOCK, HEAD), BF16)
    d_mixed_t[TILES] = jnp.zeros((BLOCK, HEAD), BF16)
    query_t[TILES] = jnp.zeros((BLOCK, HEAD), BF16)

    @pl.loop(0, TILES, unroll=4)
    def _(t):
        d_query[t] = jnp.zeros((BLOCK, HEAD), F32)
        dkv[pl.ds(t * 4, 4)] = jnp.zeros((4, 2 * HEAD, BLOCK), F32)
        mixed = mixed_in[t]
        both = four(qp, meta, t)
        upstream = both[:, HEAD:].astype(F32)
        stats = [stats_in[h, t] for h in range(HEADS)]
        mean = sum(v[0:1] for v in stats) * 0.25
        spread = sum(v[1:2] + HEAD * (v[0:1] - mean) * (v[0:1] - mean) for v in stats) * (1.0 / WIDTH)
        inverse = lax.rsqrt(spread + 1e-05)
        slant = sum(v[2:3] for v in stats) * (1.0 / WIDTH)
        along = sum(v[3:4] + v[2:3] * (v[0:1] - mean) for v in stats) * (1.0 / WIDTH) * inverse
        columns = jnp.transpose(pick4(iota((BLOCK, HEAD), 0), [mean, inverse, slant, along]))
        mean, inverse, slant, along = (columns[:, i : i + 1] for i in range(4))
        normal = (mixed - mean) * inverse
        made = (inverse * (upstream - slant - normal * along)).astype(BF16)
        d_mixed[t] = made
        d_mixed_t[t] = jnp.transpose(made)
        query_t[t] = jnp.transpose(both[:, :HEAD])
        mixed = mixed.astype(BF16)
        for i in range(4):
            mq[meta[0, t * 4 + i], :, 0:HEAD] = mixed[i * PIECE : (i + 1) * PIECE]

    load.wait()

    def step(_, state):
        pairs, t, j = walk(meta, *state, BACK_AT_ONCE)
        keyvals = [four(kv, meta, j) for _, j in pairs]
        us = [dot_nt(four(qp, meta, t)[:, :HEAD], keyval[:, :HEAD]) for (t, _), keyval in zip(pairs, keyvals)]
        d_weights = [dot_nt(d_mixed[t], keyval[:, HEAD:]) for (t, _), keyval in zip(pairs, keyvals)]
        made = []
        for (t_, j_), u, dw in zip(pairs, us, d_weights):
            th = jnp.tanh(u)
            a = (1.0 + th).astype(BF16)
            w = u.astype(BF16) * a
            ds = dw.astype(BF16) * (a + w * (1.0 - th).astype(BF16))
            seen = visible(meta, t_, j_)
            made.append((jnp.where(seen, w, jnp.zeros_like(w)), jnp.where(seen, ds, jnp.zeros_like(ds))))
        for (t_, j_), keyval, (w, ds) in zip(pairs, keyvals, made):
            d_key = dot_nn(query_t[t_], ds)
            d_value = dot_nn(d_mixed_t[t_], w)
            for i in range(4):
                dkv[j_ * 4 + i, 0:HEAD] += d_key[:, i * BLOCK : (i + 1) * BLOCK]
                dkv[j_ * 4 + i, HEAD : 2 * HEAD] += d_value[:, i * BLOCK : (i + 1) * BLOCK]
            d_query[t_] += dot_nn(ds, keyval[:, :HEAD])
        return t, j

    lax.fori_loop(0, (pairs_in_all(meta) + BACK_AT_ONCE - 1) // BACK_AT_ONCE, step, (jnp.int32(0), jnp.int32(0)))

    @pl.loop(0, TILES)
    def _(t):
        dq = (d_query[t] * (0.5 * SCALE)).astype(BF16)
        for i in range(4):
            mq[meta[0, t * 4 + i], :, HEAD : 2 * HEAD] = dq[i * PIECE : (i + 1) * PIECE]

    mq_save = pltpu.make_async_copy(mq, mq_hbm, mq_sem)
    mq_save.start()

    def save(s):
        return pltpu.make_async_copy(dkv_slots.at[s], dkv_hbm.at[s], dkv_sem.at[s])

    @pl.loop(0, SEQ, unroll=4)
    def _(s):
        total = sum(
            dot_nt(slot_onehot(ids[s, k : k + 1, :]), dkv[meta[4, s * 3 + k]].astype(BF16)) for k in range(3)
        )
        dkv_slots[s] = total.astype(BF16)
        save(s).start()

    mq_save.wait()

    @pl.loop(0, SEQ)
    def _(s):
        save(s).wait()


def return_kernel(
    send_rows, event_slot, gain_in, gain_mid, slots_in,
    feats_hbm, item_weight_hbm, w_in_hbm, w_out_hbm, cot_hbm, mq_in, dkv_in,
    layer_out, d_item_out,
    feats, item_weight, w_in, w_out, cot, mq, dkv, own, part, pre, d_pre, out2, in2, out1, in1,
    load_sem, own_sem, part_send, part_recv, mq_send, mq_recv, dkv_send, dkv_recv, send2, recv2, send1, recv1,
):
    b, s, x, c, y, z = place()
    partner = x * 2 + 1 - c
    mine = y // 2
    half = y % 2
    to_batch = x * 2 + mine
    me = z + 4 * half + 8 * c
    greet(b, s, partner)
    loads = [
        pltpu.make_async_copy(src, dst, load_sem.at[k])
        for k, (src, dst) in enumerate(
            (
                (w_in_hbm, w_in),
                (w_out_hbm, w_out),
                (cot_hbm, cot),
                (feats_hbm, feats),
                (item_weight_hbm, item_weight),
            )
        )
    ]
    greeted()

    def group_order(k):
        return lax.rem(k + z, 4)

    def own_copy(g):
        return pltpu.make_async_copy(dkv_in.at[pl.ds(g * 4, 4), c], own.at[pl.ds(g * 4, 4)], own_sem.at[g])

    def part_copy(g):
        return copy_to(
            dkv_in.at[pl.ds(g * 4, 4), 1 - c], part.at[pl.ds(g * 4, 4)], part_send.at[g], part_recv.at[g], partner, s
        )

    @pl.loop(0, 4)
    def _(k):
        g = group_order(k)
        own_copy(g).start()
        part_copy(g).start()

    def is_here(source):
        return (to_batch == b) & (source == s)

    def mq_copy(source):
        return copy_to(
            mq_in.at[source], mq.at[z, :, half * 2 + c], mq_send.at[source], mq_recv.at[me], to_batch, source
        )

    def dkv_copy(source):
        return copy_to(
            own.at[source], dkv.at[z, half, c], dkv_send.at[source], dkv_recv.at[me], to_batch, source
        )

    @pl.loop(0, SEQ)
    def _(i):
        source = lax.rem(i + s, SEQ)

        @pl.when(is_here(source))
        def _():
            pltpu.make_async_copy(mq_in.at[source], mq.at[z, :, half * 2 + c], mq_recv.at[me]).start()

        @pl.when(jnp.logical_not(is_here(source)))
        def _():
            mq_copy(source).start()

    @pl.loop(0, 4)
    def _(k):
        g = group_order(k)
        own_copy(g).wait()
        arrived(part.at[pl.ds(g * 4, 4)], part_recv.at[g])

        @pl.loop(0, 4)
        def _(i):
            source = g * 4 + lax.rem(i + y, 4)
            own[source] = (own[source].astype(F32) + part[source].astype(F32)).astype(BF16)

            @pl.when(is_here(source))
            def _():
                pltpu.make_async_copy(own.at[source], dkv.at[z, half, c], dkv_recv.at[me]).start()

            @pl.when(jnp.logical_not(is_here(source)))
            def _():
                dkv_copy(source).start()

    for load in loads:
        load.start()
    onehot = slot_onehot(slot_rows(event_slot[...].reshape(1, ROWS)))
    normal, inverse = normalize(slots_in[...].astype(F32))
    normed = (normal * gain_in[...]).astype(BF16)
    loads[0].wait()
    for k in range(4):
        cols = slice(k * WIDTH, (k + 1) * WIDTH)
        pre[:, cols] = dot_nn(normed, w_in[:, cols])
    tokens = dot_tn(onehot, slots_in[...])
    gate = dot_tn(onehot, silu(pre[:, 0:WIDTH]).astype(BF16))
    loads[1].wait()
    loads[2].wait()
    d_gated = dot_nt(cot[...], w_out[...]).astype(BF16).astype(F32)
    slot_cot = dot_nn(onehot, cot[...])
    loads[3].wait()
    loads[4].wait()
    item_slope = silu_slope(dot_nn(feats[...], item_weight[...]))

    @pl.loop(0, SEQ)
    def _(w):
        arrived(mq.at[w % 4, :, ((w // 4) % 2) * 2 + w // 8], mq_recv.at[w])

    mixed = jnp.concatenate([mq[h, :, :, :, 0:HEAD].reshape(ROWS, HEAD) for h in range(HEADS)], axis=1)
    normed_mid = normalize(mixed.astype(F32))[0] * gain_mid[...]
    gated = (normed_mid * gate).astype(BF16)
    layer_out[...] = (tokens + dot_nn(gated, w_out[...])).astype(BF16)
    d_gate = dot_nn(onehot, (d_gated * normed_mid).astype(BF16))
    d_pre[...] = (d_gate * silu_slope(pre[:, 0:WIDTH])).astype(BF16)
    d_normed = dot_nt(d_pre[...], w_in[:, 0:WIDTH])
    d_query = jnp.concatenate(
        [mq[h, :, :, :, HEAD : 2 * HEAD].reshape(ROWS, HEAD) for h in range(HEADS)], axis=1
    )
    d_pre[...] = (dot_nn(onehot, d_query) * silu_slope(pre[:, 1024:1536])).astype(BF16)
    d_normed += dot_nt(d_pre[...], w_in[:, 1024:1536])
    for first_column in (512, 1536):
        cols = slice(first_column, first_column + WIDTH)
        pre[:, cols] = silu_slope(pre[:, cols])

    @pl.loop(0, SEQ)
    def _(w):
        arrived(dkv.at[w % 4, (w // 4) % 2, w // 8], dkv_recv.at[w])

    for lanes, first_column in ((0, 1536), (HEAD, 512)):
        cols = slice(first_column, first_column + WIDTH)
        grad = jnp.concatenate(
            [
                dkv[h, 0, :, :, lanes : lanes + HEAD].reshape(SLOTS, HEAD).astype(F32)
                + dkv[h, 1, :, :, lanes : lanes + HEAD].reshape(SLOTS, HEAD).astype(F32)
                for h in range(HEADS)
            ],
            axis=1,
        )
        d_pre[...] = (grad * pre[:, cols]).astype(BF16)
        d_normed += dot_nt(d_pre[...], w_in[:, cols])

    scaled = d_normed * gain_in[...]
    d_slots = slot_cot + inverse * (
        scaled
        - jnp.mean(scaled, axis=-1, keepdims=True)
        - normal * jnp.mean(scaled * normal, axis=-1, keepdims=True)
    )
    out2[...] = d_slots.astype(BF16)
    wait_all(exchange_seq(out2, in2, send2, recv2, b, s))
    out1[...] = dot_nn(by_batch(), in2[...]).astype(BF16)
    last = exchange_batch(out1, in1, send1, recv1, b, s)
    wanted = (iota((256, 256), 0) == send_rows[...]).astype(BF16)
    wait_all(last)
    d_embedded = dot_nn(wanted, in1[...])
    d_item_out[...] = (d_embedded * item_slope).astype(BF16)

    @pl.loop(0, 4)
    def _(g):
        part_copy(g).wait_send()

    @pl.loop(0, SEQ)
    def _(source):
        @pl.when(jnp.logical_not(is_here(source)))
        def _():
            mq_copy(source).wait_send()
            dkv_copy(source).wait_send()


def result_kernel(layer, d_item, item_weight, layer_out, item_grad):
    layer_out[...] = layer[...]
    item_grad[...] = dot_nt(d_item[...], item_weight[...])


def spec(space):
    return pl.BlockSpec(memory_space=space)


VMEM, SMEM, ANY = pltpu.VMEM, pltpu.SMEM, pl.ANY
DMA = pltpu.SemaphoreType.DMA


def shape(dims, dtype):
    return jax.ShapeDtypeStruct(dims, dtype)


def params(remote=None):
    return pltpu.CompilerParams(
        vmem_limit_bytes=56 << 20, has_side_effects=remote is not None, collective_id=remote
    )


def forward_call(meta, kv, qp):
    return pl.pallas_call(
        forward_kernel,
        out_shape=(shape((TILES, BLOCK, HEAD), F32), shape((TILES, 8, BLOCK), F32)),
        in_specs=[spec(SMEM), spec(VMEM), spec(VMEM)],
        out_specs=(spec(VMEM), spec(VMEM)),
        scratch_shapes=[VMEM((TILES + 1, BLOCK, HEAD), F32)],
        compiler_params=params(),
        name="forward",
    )(meta, kv, qp)


def backward_call(meta, ids, kv, qp, mixed, stats):
    return pl.pallas_call(
        backward_kernel,
        out_shape=(shape((BLOCKS, PIECE, 2 * HEAD), BF16), shape((SEQ, SLOTS, 2 * HEAD), BF16)),
        in_specs=[spec(SMEM)] + [spec(VMEM)] * 4 + [spec(ANY)],
        out_specs=(spec(ANY), spec(ANY)),
        scratch_shapes=[
            VMEM((BLOCKS, BLOCK, 2 * HEAD), BF16),
            VMEM((BLOCKS, PIECE, 2 * HEAD), BF16),
            VMEM((SEQ, SLOTS, 2 * HEAD), BF16),
            VMEM((TILES + 1, BLOCK, HEAD), BF16),
            VMEM((TILES + 1, HEAD, BLOCK), BF16),
            VMEM((TILES + 1, HEAD, BLOCK), BF16),
            VMEM((TILES + 1, BLOCK, HEAD), F32),
            VMEM((BLOCKS, 2 * HEAD, BLOCK), F32),
            DMA,
            DMA,
            DMA((SEQ,)),
        ],
        compiler_params=params(),
        name="backward",
    )(meta, ids, qp, mixed, stats, kv)


def per_device(
    item_feats, item_weight, send_rows, event_slot, user_blocks, tail_len, block_order, gain_in, gain_mid, w_in, w_out,
    cot_out,
):
    gain_in, gain_mid = gain_in.reshape(1, WIDTH), gain_mid.reshape(1, WIDTH)
    kv, qp, slots, ids, meta = pl.pallas_call(
        send_kernel,
        out_shape=(
            shape((SEQ, 3, BLOCK, 2 * HEAD), BF16),
            shape((SEQ, 3, PIECE, 2 * HEAD), BF16),
            shape((SLOTS, WIDTH), BF16),
            shape((SEQ, 8, 128), jnp.int32),
            shape((8, 128), jnp.int32),
        ),
        in_specs=[spec(VMEM)] * 9 + [spec(ANY)] * 3,
        out_specs=(spec(ANY), spec(ANY), spec(VMEM), spec(VMEM), spec(VMEM)),
        scratch_shapes=[VMEM((WIDTH, 4 * WIDTH), BF16), VMEM((WIDTH, WIDTH), BF16), VMEM((ROWS, WIDTH), BF16)]
        + [VMEM((256, WIDTH), BF16)] * 4
        + [
            VMEM((HEADS, 2, HALF, 2 * HEAD), BF16),
            VMEM((HEADS, 3, 4, PIECE, 2 * HEAD), BF16),
            VMEM((8, 128), jnp.int32),
            VMEM((SEQ, 8, 128), jnp.int32),
            VMEM((SEQ, 2, HALF, 2 * HEAD), BF16),
            VMEM((SEQ, 3, BLOCK, 2 * HEAD), BF16),
            DMA((3,)),
            DMA((SEQ,)),
            DMA((GROUPS,)),
            DMA((GROUPS,)),
        ]
        + [DMA((SEQ,))] * 10,
        compiler_params=params(0),
        name="send",
    )(
        item_feats, item_weight, send_rows, event_slot, user_blocks, tail_len, block_order, gain_in, gain_mid, w_in,
        w_out, cot_out,
    )
    kv = kv.reshape(BLOCKS, BLOCK, 2 * HEAD)
    qp = qp.reshape(BLOCKS, PIECE, 2 * HEAD)
    mixed, stats = forward_call(meta, kv, qp)
    stats = pl.pallas_call(
        stats_kernel,
        out_shape=shape((HEADS, TILES, 8, BLOCK), F32),
        in_specs=[spec(VMEM)],
        out_specs=spec(VMEM),
        scratch_shapes=[VMEM((HEADS, TILES, 8, BLOCK), F32), DMA((HEADS,)), DMA((HEADS,))],
        compiler_params=params(1),
        name="stats",
    )(stats)
    mq, dkv = backward_call(meta, ids, kv, qp, mixed, stats)
    mq = mq.reshape(SEQ, 3, PIECE, 2 * HEAD)
    dkv = dkv.reshape(SEQ, 2, HALF, 2 * HEAD)
    layer, d_item = pl.pallas_call(
        return_kernel,
        out_shape=(shape((ROWS, WIDTH), BF16), shape((256, WIDTH), BF16)),
        in_specs=[spec(VMEM)] * 5 + [spec(ANY)] * 7,
        out_specs=(spec(VMEM), spec(VMEM)),
        scratch_shapes=[
            VMEM((256, WIDTH), BF16),
            VMEM((WIDTH, WIDTH), BF16),
            VMEM((WIDTH, 4 * WIDTH), BF16),
            VMEM((WIDTH, WIDTH), BF16),
            VMEM((ROWS, WIDTH), BF16),
            VMEM((HEADS, 3, 4, PIECE, 2 * HEAD), BF16),
            VMEM((HEADS, 2, 2, HALF, 2 * HEAD), BF16),
            VMEM((SEQ, HALF, 2 * HEAD), BF16),
            VMEM((SEQ, HALF, 2 * HEAD), BF16),
            VMEM((SLOTS, 4 * WIDTH), F32),
            VMEM((SLOTS, WIDTH), BF16),
        ]
        + [VMEM((256, WIDTH), BF16)] * 4
        + [DMA((5,))]
        + [DMA((4,))] * 3
        + [DMA((SEQ,))] * 6
        + [DMA((GROUPS,))] * 2,
        compiler_params=params(2),
        name="give_back",
    )(
        send_rows, event_slot, gain_in, gain_mid, slots, item_feats, item_weight, w_in, w_out, cot_out, mq, dkv,
    )
    return pl.pallas_call(
        result_kernel,
        out_shape=(shape((ROWS, WIDTH), BF16), shape((256, WIDTH), F32)),
        in_specs=[spec(VMEM)] * 3,
        out_specs=(spec(VMEM), spec(VMEM)),
        compiler_params=params(),
        name="results",
    )(layer, d_item, item_weight)


def solution(mesh):
    rows = P(("batch", "seq"), None)
    return jax.shard_map(
        per_device,
        mesh=mesh,
        in_specs=(
            rows,
            P(),
            rows,
            P(("batch", "seq")),
            P("batch", None),
            P("batch", None),
            P("batch", None),
            P(),
            P(),
            P(),
            P(),
            rows,
        ),
        out_specs=(rows, rows),
        check_vma=False,
    )
```

```python
import jax
import jax.numpy as jnp
from jax import lax
from jax.experimental import pallas as pl
from jax.experimental.pallas import tpu as pltpu
from jax.sharding import PartitionSpec as P

WIDTH = 512
HEAD = 128
HEADS = 4
BLOCK = 128
BLOCKS = 48
SEQ = 16
GROUPS = 8
PIECE = 32
TILES = 12
SLOTS = 256
HALF = 128
ROWS = 384
FAR = 30000
NO_BLOCK = 200
AT_ONCE = 4
MOST_PAIRS = 48
MOST_CHUNKS = 7
BACK_AT_ONCE = 4
SCALE = HEAD**-0.5
MESH = pl.DeviceIdType.MESH
F32 = jnp.float32
BF16 = jnp.bfloat16


def dot_nn(a, b):
    return jnp.dot(a, b, preferred_element_type=F32)


def dot_nt(a, b):
    return lax.dot_general(a, b, (((1,), (1,)), ((), ())), preferred_element_type=F32)


def dot_tn(a, b):
    return lax.dot_general(a, b, (((0,), (0,)), ((), ())), preferred_element_type=F32)


def silu(v):
    u = 0.5 * v
    return u + u * jnp.tanh(u)


def silu_slope(v):
    u = 0.5 * v
    t = jnp.tanh(u)
    a = 1.0 + t
    return 0.5 * (a + u * a * (1.0 - t))


def normalize(values):
    mean = jnp.mean(values, axis=-1, keepdims=True)
    centred = values - mean
    spread = jnp.mean(centred * centred, axis=-1, keepdims=True)
    inverse = lax.rsqrt(spread + 1e-05)
    return centred * inverse, inverse


def iota(shape, dim):
    return lax.broadcasted_iota(jnp.int32, shape, dim)


def place():
    b, s = lax.axis_index("batch"), lax.axis_index("seq")
    return b, s, b // 2, b % 2, s // 4, s % 4


def worker_at(w, x, c):
    head, half, core = w % 4, (w // 4) % 2, w // 8
    return head, half, core, x * 2 + core, (2 * c + half) * 4 + head


def copy_to(src, dst, send, recv, batch, seq):
    return pltpu.make_async_remote_copy(
        src_ref=src, dst_ref=dst, send_sem=send, recv_sem=recv, device_id=(batch, seq), device_id_type=MESH
    )


def arrived(ref, sem):
    pltpu.make_async_copy(ref, ref, sem).wait()


def rows_of(index, size):
    return pl.ds(pl.multiple_of(index * size, size), size)


def slot_rows(event_slot):
    e = event_slot
    return ((e >> 1) & 15) * 16 + (e >> 5) * 2 + (e & 1)


def slot_onehot(wanted):
    return (iota((SLOTS, wanted.shape[1]), 0) == wanted).astype(BF16)


def by_seq():
    i, j = iota((256, 256), 0), iota((256, 256), 1)
    return (j == ((i >> 1) & 7) * 32 + (i >> 4) * 2 + (i & 1)).astype(BF16)


def by_batch():
    i, j = iota((256, 256), 0), iota((256, 256), 1)
    return (j == ((i >> 1) & 15) * 16 + (i >> 5) * 2 + (i & 1)).astype(BF16)


def exchange_batch(src, dst, send, recv, b, s):
    copies = []
    for k in range(1, GROUPS):
        peer = lax.rem(b + k, GROUPS)
        copy = copy_to(src.at[rows_of(peer, 32)], dst.at[rows_of(b, 32)], send.at[k], recv.at[k], peer, s)
        copy.start()
        copies.append(copy)
    dst[rows_of(b, 32), :] = src[rows_of(b, 32), :]
    return copies


def exchange_seq(src, dst, send, recv, b, s):
    copies = []
    for k in range(1, SEQ):
        peer = lax.rem(s + k, SEQ)
        copy = copy_to(src.at[rows_of(peer, 16)], dst.at[rows_of(s, 16)], send.at[k], recv.at[k], b, peer)
        copy.start()
        copies.append(copy)
    dst[rows_of(s, 16), :] = src[rows_of(s, 16), :]
    return copies


def signal(barrier, batch, seq):
    pl.semaphore_signal(barrier, inc=1, device_id=(batch, seq), device_id_type=MESH)


def greet(b, s, partner):
    barrier = pltpu.get_barrier_semaphore()
    for k in range(1, GROUPS):
        signal(barrier, lax.rem(b + k, GROUPS), s)

    @pl.loop(1, SEQ)
    def _(k):
        peer = lax.rem(s + k, SEQ)
        signal(barrier, b, peer)
        signal(barrier, partner, peer)


def greeted():
    pl.semaphore_wait(pltpu.get_barrier_semaphore(), GROUPS - 1 + 2 * (SEQ - 1))


def wait_all(copies):
    for copy in copies:
        copy.wait()


def send_kernel(
    feats, item_weight, send_rows, event_slot, user_blocks, tail_len, block_order, gain_in, gain_mid,
    w_in_hbm, w_out_hbm, cot_hbm,
    kv_out, q_out, p_out, slots_out, ids_out, meta_out, mixed_out, stats_out,
    w_in, w_out, cot, out1, in1, out2, in2, kv, q, p, ids, ids_in, kv_in, kv_events, q_in, p_in, tables, products, stats,
    load_sem, save_sem, out_sem, table_sem, send1, recv1, send2, recv2, kv_send, kv_recv, pass_send, pass_recv,
    q_send, q_recv, p_send, p_recv, ids_send, ids_recv, stats_send, stats_recv,
):
    b, s, x, c, y, z = place()
    partner = x * 2 + 1 - c
    greet(b, s, partner)
    loads = [
        pltpu.make_async_copy(src, dst, load_sem.at[k])
        for k, (src, dst) in enumerate(((w_out_hbm, w_out), (cot_hbm, cot), (w_in_hbm, w_in)))
    ]
    for load in loads:
        load.start()

    embedded = silu(dot_nn(feats[...], item_weight[...])).astype(BF16)
    wanted = (iota((256, 256), 0) == send_rows[...]).astype(BF16)
    out1[...] = dot_tn(wanted, embedded).astype(BF16)
    slot_of_event = slot_rows(event_slot[...].reshape(1, ROWS))
    ids[...] = jnp.zeros_like(ids)
    for k in range(3):
        ids[k : k + 1, :] = slot_of_event[:, k * BLOCK : (k + 1) * BLOCK]
    ids[3:4, 0:BLOCKS] = block_order[...]
    ids[4:5, 0:4] = user_blocks[...]
    ids[5:6, 0:4] = tail_len[...]
    greeted()
    first = exchange_batch(out1, in1, send1, recv1, b, s)

    def each_worker(act):
        @pl.loop(0, SEQ)
        def _(i):
            w = lax.rem(i + s, SEQ)
            head, half, core, to_batch, to_seq = worker_at(w, x, c)
            here = (to_batch == b) & (to_seq == s)
            act(w, head, half, core, to_batch, to_seq, here)

    def start(here, src, dst, recv, remote):
        @pl.when(here)
        def _():
            pltpu.make_async_copy(src, dst, recv).start()

        @pl.when(jnp.logical_not(here))
        def _():
            remote.start()

    def ids_copy(w, to_batch, to_seq):
        return copy_to(ids, ids_in.at[s], ids_send.at[w], ids_recv.at[s], to_batch, to_seq)

    def start_ids(w, head, half, core, to_batch, to_seq, here):
        start(here, ids, ids_in.at[s], ids_recv.at[s], ids_copy(w, to_batch, to_seq))

    each_worker(start_ids)

    loads[0].wait()
    loads[1].wait()
    d_gated = dot_nt(cot[...], w_out[...]).astype(BF16)
    wait_all(first)
    out2[...] = dot_nn(by_seq(), in1[...]).astype(BF16)
    second = exchange_seq(out2, in2, send2, recv2, b, s)
    onehot = slot_onehot(slot_of_event)
    loads[2].wait()
    wait_all(second)
    slots_out[...] = in2[...]
    normed = (normalize(in2[...].astype(F32))[0] * gain_in[...]).astype(BF16)

    for part, first_column in ((0, 1536), (1, 512)):
        lanes = slice(part * HEAD, part * HEAD + HEAD)
        made = silu(dot_nn(normed, w_in[:, first_column : first_column + WIDTH])).astype(BF16)
        for h in range(HEADS):
            kv[h, 0, :, lanes] = made[:HALF, h * HEAD : (h + 1) * HEAD]
            kv[h, 1, :, lanes] = made[HALF:, h * HEAD : (h + 1) * HEAD]

    def kv_copy(w, head, core, to_batch, to_seq):
        return copy_to(kv.at[head, core], kv_in.at[s, core], kv_send.at[w], kv_recv.at[s], to_batch, to_seq)

    def start_kv(w, head, half, core, to_batch, to_seq, here):
        start(
            here, kv.at[head, core], kv_in.at[s, core], kv_recv.at[s], kv_copy(w, head, core, to_batch, to_seq)
        )

    each_worker(start_kv)

    query = (silu(dot_nn(normed, w_in[:, 1024:1536])) * (0.5 * SCALE)).astype(BF16)
    query = dot_tn(onehot, query).astype(BF16)
    for h in range(HEADS):
        q[h] = query[:, h * HEAD : (h + 1) * HEAD].reshape(3, 4, PIECE, HEAD)

    def piece_copy(src, dst, send, recv, w, head, half, core, to_batch, to_seq):
        three = pl.ds(s * 3, 3)
        return copy_to(
            src.at[head, :, half * 2 + core], dst.at[three], send.at[w], recv.at[s], to_batch, to_seq
        )

    def start_piece(src, dst, send, recv):
        def act(w, head, half, core, to_batch, to_seq, here):
            start(
                here, src.at[head, :, half * 2 + core], dst.at[pl.ds(s * 3, 3)], recv.at[s],
                piece_copy(src, dst, send, recv, w, head, half, core, to_batch, to_seq),
            )

        each_worker(act)

    start_piece(q, q_in, q_send, q_recv)
    gate = silu(dot_nn(normed, w_in[:, 0:WIDTH])).astype(BF16)
    gate = dot_tn(onehot, gate)
    upstream = (d_gated.astype(F32) * gate * gain_mid[...]).astype(BF16)
    for h in range(HEADS):
        p[h] = upstream[:, h * HEAD : (h + 1) * HEAD].reshape(3, 4, PIECE, HEAD)
    start_piece(p, p_in, p_send, p_recv)

    @pl.loop(0, SEQ)
    def _(source):
        arrived(ids_in.at[source], ids_recv.at[source])

    ids_out[...] = ids_in[...]
    meta_out[...] = tables_of(ids_in[s], (y % 2) * 2 + c)
    table_copy = pltpu.make_async_copy(meta_out, tables, table_sem)
    table_copy.start()

    def pass_on(source):
        return copy_to(
            kv_in.at[source, c], kv_in.at[source, c], pass_send.at[source], pass_recv.at[source], partner, s
        )

    def save(source):
        three = pl.ds(source * 3, 3)
        return pltpu.make_async_copy(kv_events.at[three], kv_out.at[three], save_sem.at[source])

    @pl.loop(0, SEQ + 2)
    def _(i):
        @pl.when(i < SEQ)
        def _():
            source = lax.rem(s - i + SEQ, SEQ)
            arrived(kv_in.at[source, c], kv_recv.at[source])
            pass_on(source).start()

        @pl.when(i >= 2)
        def _():
            source = lax.rem(s - i + 2 + SEQ, SEQ)
            arrived(kv_in.at[source, 1 - c], pass_recv.at[source])
            rows = jnp.concatenate([ids_in[source].astype(F32), jnp.zeros((120, 128), F32)], axis=0)
            columns = jnp.transpose(rows)
            lane = iota((BLOCK, SLOTS), 1).astype(F32)
            read = jnp.concatenate([(lane == columns[:, k : k + 1]).astype(BF16) for k in range(3)], axis=0)
            slots = kv_in[source].reshape(SLOTS, 2 * HEAD)
            made = dot_nn(read, slots).astype(BF16).reshape(3, BLOCK, 2 * HEAD)
            kv_events[pl.ds(source * 3, 3)] = made
            save(source).start()

    table_copy.wait()

    @pl.loop(0, SEQ)
    def _(source):
        arrived(q_in.at[pl.ds(source * 3, 3)], q_recv.at[source])

    def step(k, state):
        pairs, t, j = walk(tables, *state, AT_ONCE)
        keyvals = [four(kv_events, tables, j) for _, j in pairs]
        us = [dot_nt(four(q_in, tables, t), keyval[:, :HEAD]) for (t, _), keyval in zip(pairs, keyvals)]
        weights = []
        for (t_, j_), u in zip(pairs, us):
            w = u.astype(BF16) * (1.0 + jnp.tanh(u)).astype(BF16)
            weights.append(jnp.where(visible(tables, t_, j_), w, jnp.zeros_like(w)))
        for n, (w, keyval) in enumerate(zip(weights, keyvals)):
            products[k * AT_ONCE + n] = dot_nn(w, keyval[:, HEAD:])
        return t, j

    lax.fori_loop(0, MOST_PAIRS // AT_ONCE, step, (jnp.int32(0), jnp.int32(0)))

    @pl.loop(0, SEQ)
    def _(source):
        arrived(p_in.at[pl.ds(source * 3, 3)], p_recv.at[source])

    outs = [
        pltpu.make_async_copy(src, dst, out_sem.at[k]) for k, (src, dst) in enumerate(((q_in, q_out), (p_in, p_out)))
    ]
    for out in outs:
        out.start()

    first_pair = jnp.int32(0)
    for t in range(TILES):
        count = t + 1 - tables[1, 4 * t] // 4
        mixed = products[jnp.minimum(first_pair, MOST_PAIRS - 1)]
        for k in range(1, min(t + 1, MOST_CHUNKS)):
            more = products[jnp.minimum(first_pair + k, MOST_PAIRS - 1)]
            mixed = mixed + jnp.where(k < count, more, jnp.zeros_like(more))
        first_pair = first_pair + count
        upstream = four(p_in, tables, t).astype(F32)
        mixed_out[t] = mixed
        mean = jnp.mean(mixed, axis=1, keepdims=True)
        centred = mixed - mean
        sums = pick4(
            iota((BLOCK, HEAD), 1) & 3,
            [
                mean,
                jnp.sum(centred * centred, axis=1, keepdims=True),
                jnp.sum(upstream, axis=1, keepdims=True),
                jnp.sum(upstream * centred, axis=1, keepdims=True),
            ],
        )
        rows = slice(4 * (t % 2), 4 * (t % 2) + 4)
        stats[z, t // 2, rows, :] = jnp.transpose(sums)[rows, :]

    copies = []
    for k in range(1, HEADS):
        peer = lax.rem(z + k, HEADS)
        copy = copy_to(stats.at[z], stats.at[z], stats_send.at[k], stats_recv.at[k], b, y * 4 + peer)
        copy.start()
        copies.append(copy)

    def finish(w, head, half, core, to_batch, to_seq, here):
        @pl.when(jnp.logical_not(here))
        def _():
            ids_copy(w, to_batch, to_seq).wait_send()
            kv_copy(w, head, core, to_batch, to_seq).wait_send()
            piece_copy(q, q_in, q_send, q_recv, w, head, half, core, to_batch, to_seq).wait_send()
            piece_copy(p, p_in, p_send, p_recv, w, head, half, core, to_batch, to_seq).wait_send()

    each_worker(finish)

    @pl.loop(0, SEQ)
    def _(source):
        pass_on(source).wait_send()
        save(source).wait()

    for out in outs:
        out.wait()
    wait_all(copies)
    stats_out[...] = stats[...]


def tables_of(meta, quarter):
    slot, lane = iota((128, 128), 0), iota((1, 128), 1)
    held = jnp.transpose(jnp.broadcast_to(meta[3:4, :], (128, 128)))
    slot_of = jnp.where((held == iota((128, 128), 1)) & (slot < BLOCKS), slot, 0)
    slot_of = jnp.minimum(jnp.sum(slot_of, axis=0, keepdims=True), BLOCKS - 1)
    first = jnp.zeros((1, 1), jnp.int32)
    start_of = jnp.zeros((1, 128), jnp.int32)
    limit_of = jnp.full((1, 128), BLOCK, jnp.int32)
    for u in range(4):
        start_of = jnp.where(lane >= first, first, start_of)
        first = first + meta[4:5, u : u + 1]
        limit_of = jnp.where(lane == first - 1, meta[5:6, u : u + 1], limit_of)
    start_of = jnp.where(lane < BLOCKS, start_of, NO_BLOCK)
    row = iota((8, 128), 0)
    picked = pick4(row, [slot_of, start_of, limit_of, jnp.zeros((1, 128), jnp.int32) + quarter])
    return jnp.where(row == 4, meta[3:4, :], picked)


def pick4(index, values):
    return jnp.where(index == 0, values[0], jnp.where(index == 1, values[1], jnp.where(index == 2, values[2], values[3])))


def first_chunk(meta, t):
    return jnp.clip(meta[1, 4 * t] // 4, 0, TILES - 1)


def walk(meta, t, j, count):
    pairs = []
    for _ in range(count):
        pairs.append((t, j))
        more = j < jnp.minimum(t, TILES - 1)
        after = jnp.minimum(t + 1, TILES)
        j = jnp.where(more, j + 1, first_chunk(meta, after))
        t = jnp.where(more, t, after)
    return pairs, t, j


def pairs_in_all(meta):
    return sum(t + 1 - meta[1, 4 * t] // 4 for t in range(TILES))


def four(ref, meta, n):
    return jnp.concatenate([ref[meta[0, 4 * n + i]] for i in range(4)], axis=0)


def visible(meta, t, j):
    r, lane = iota((BLOCK, 1), 0), iota((1, BLOCK), 1)
    at = (t * 4 + (r >> 5)) * BLOCK + meta[3, 0] * PIECE + (r & 31)
    since = pick4(r >> 5, [meta[1, t * 4 + i] for i in range(4)]) * BLOCK
    where = jnp.concatenate(
        [jnp.where(lane < meta[2, j * 4 + i], (j * 4 + i) * BLOCK + lane, FAR) for i in range(4)], axis=1
    )
    where, at, since = (v.astype(jnp.int16) for v in (where, at, since))
    return (where <= at) & (where >= since)


def backward_kernel(
    meta, ids, q, p, mixed_in, stats_in, kv_hbm, mq_hbm, dkv_hbm,
    kv, mq, dkv_slots, d_mixed, query_t, d_mixed_t, d_query, dkv, kv_sem, mq_sem, dkv_sem,
):
    load = pltpu.make_async_copy(kv_hbm, kv, kv_sem)
    load.start()
    d_mixed[TILES] = jnp.zeros((BLOCK, HEAD), BF16)
    d_mixed_t[TILES] = jnp.zeros((BLOCK, HEAD), BF16)
    query_t[TILES] = jnp.zeros((BLOCK, HEAD), BF16)

    def prepare(t, stats):
        d_query[t] = jnp.zeros((BLOCK, HEAD), F32)
        dkv[pl.ds(t * 4, 4)] = jnp.zeros((4, 2 * HEAD, BLOCK), F32)
        mixed = mixed_in[t]
        upstream = four(p, meta, t).astype(F32)
        mean = sum(v[0:1] for v in stats) * 0.25
        spread = sum(v[1:2] + HEAD * (v[0:1] - mean) * (v[0:1] - mean) for v in stats) * (1.0 / WIDTH)
        inverse = lax.rsqrt(spread + 1e-05)
        slant = sum(v[2:3] for v in stats) * (1.0 / WIDTH)
        along = sum(v[3:4] + v[2:3] * (v[0:1] - mean) for v in stats) * (1.0 / WIDTH) * inverse
        columns = jnp.transpose(pick4(iota((BLOCK, HEAD), 0), [mean, inverse, slant, along]))
        mean, inverse, slant, along = (columns[:, i : i + 1] for i in range(4))
        normal = (mixed - mean) * inverse
        made = (inverse * (upstream - slant - normal * along)).astype(BF16)
        d_mixed[t] = made
        d_mixed_t[t] = jnp.transpose(made)
        query_t[t] = jnp.transpose(four(q, meta, t))
        mixed = mixed.astype(BF16)
        for i in range(4):
            mq[meta[0, t * 4 + i], :, 0:HEAD] = mixed[i * PIECE : (i + 1) * PIECE]

    @pl.loop(0, TILES // 2, unroll=2)
    def _(pair):
        both = [stats_in[h, pair] for h in range(HEADS)]
        prepare(pair * 2, [v[0:4] for v in both])
        prepare(pair * 2 + 1, [v[4:8] for v in both])

    load.wait()

    def step(_, state):
        pairs, t, j = walk(meta, *state, BACK_AT_ONCE)
        keyvals = [four(kv, meta, j) for _, j in pairs]
        us = [dot_nt(four(q, meta, t), keyval[:, :HEAD]) for (t, _), keyval in zip(pairs, keyvals)]
        d_weights = [dot_nt(d_mixed[t], keyval[:, HEAD:]) for (t, _), keyval in zip(pairs, keyvals)]
        made = []
        for (t_, j_), u, dw in zip(pairs, us, d_weights):
            th = jnp.tanh(u)
            a = (1.0 + th).astype(BF16)
            w = u.astype(BF16) * a
            ds = dw.astype(BF16) * (a + w * (1.0 - th).astype(BF16))
            seen = visible(meta, t_, j_)
            made.append((jnp.where(seen, w, jnp.zeros_like(w)), jnp.where(seen, ds, jnp.zeros_like(ds))))
        for (t_, j_), keyval, (w, ds) in zip(pairs, keyvals, made):
            d_key = dot_nn(query_t[t_], ds)
            d_value = dot_nn(d_mixed_t[t_], w)
            for i in range(4):
                dkv[j_ * 4 + i, 0:HEAD] += d_key[:, i * BLOCK : (i + 1) * BLOCK]
                dkv[j_ * 4 + i, HEAD : 2 * HEAD] += d_value[:, i * BLOCK : (i + 1) * BLOCK]
            d_query[t_] += dot_nn(ds, keyval[:, :HEAD])
        return t, j

    lax.fori_loop(0, (pairs_in_all(meta) + BACK_AT_ONCE - 1) // BACK_AT_ONCE, step, (jnp.int32(0), jnp.int32(0)))

    @pl.loop(0, TILES)
    def _(t):
        dq = (d_query[t] * (0.5 * SCALE)).astype(BF16)
        for i in range(4):
            mq[meta[0, t * 4 + i], :, HEAD : 2 * HEAD] = dq[i * PIECE : (i + 1) * PIECE]

    mq_save = pltpu.make_async_copy(mq, mq_hbm, mq_sem)
    mq_save.start()

    def save(s):
        return pltpu.make_async_copy(dkv_slots.at[s], dkv_hbm.at[s], dkv_sem.at[s])

    @pl.loop(0, SEQ, unroll=8)
    def _(s):
        wanted = jnp.concatenate([ids[s, k : k + 1, :] for k in range(3)], axis=1)
        grads = jnp.concatenate([dkv[meta[4, s * 3 + k]].astype(BF16) for k in range(3)], axis=1)
        dkv_slots[s] = dot_nt(slot_onehot(wanted), grads).astype(BF16)
        save(s).start()

    mq_save.wait()

    @pl.loop(0, SEQ)
    def _(s):
        save(s).wait()


def return_kernel(
    send_rows, event_slot, gain_in, gain_mid, slots_in,
    feats_hbm, item_weight_hbm, w_in_hbm, w_out_hbm, cot_hbm, mq_in, dkv_in,
    layer_out, d_item_out,
    feats, item_weight, w_in, w_out, cot, mq, dkv, own, part, pre, d_pre, out2, in2, out1, in1,
    load_sem, own_sem, part_send, part_recv, mq_send, mq_recv, dkv_send, dkv_recv, send2, recv2, send1, recv1,
):
    b, s, x, c, y, z = place()
    partner = x * 2 + 1 - c
    mine = y // 2
    half = y % 2
    to_batch = x * 2 + mine
    me = z + 4 * half + 8 * c
    greet(b, s, partner)
    loads = [
        pltpu.make_async_copy(src, dst, load_sem.at[k])
        for k, (src, dst) in enumerate(
            (
                (w_in_hbm, w_in),
                (w_out_hbm, w_out),
                (cot_hbm, cot),
                (feats_hbm, feats),
                (item_weight_hbm, item_weight),
            )
        )
    ]
    greeted()

    def group_order(k):
        return lax.rem(k + z, 4)

    def own_copy(g):
        return pltpu.make_async_copy(dkv_in.at[pl.ds(g * 4, 4), c], own.at[pl.ds(g * 4, 4)], own_sem.at[g])

    def part_copy(g):
        return copy_to(
            dkv_in.at[pl.ds(g * 4, 4), 1 - c], part.at[pl.ds(g * 4, 4)], part_send.at[g], part_recv.at[g], partner, s
        )

    @pl.loop(0, 4)
    def _(k):
        g = group_order(k)
        own_copy(g).start()
        part_copy(g).start()

    def is_here(source):
        return (to_batch == b) & (source == s)

    def mq_copy(source):
        return copy_to(
            mq_in.at[source], mq.at[z, :, half * 2 + c], mq_send.at[source], mq_recv.at[me], to_batch, source
        )

    def dkv_copy(source):
        return copy_to(
            own.at[source], dkv.at[z, half, c], dkv_send.at[source], dkv_recv.at[me], to_batch, source
        )

    @pl.loop(0, SEQ)
    def _(i):
        source = lax.rem(i + s, SEQ)

        @pl.when(is_here(source))
        def _():
            pltpu.make_async_copy(mq_in.at[source], mq.at[z, :, half * 2 + c], mq_recv.at[me]).start()

        @pl.when(jnp.logical_not(is_here(source)))
        def _():
            mq_copy(source).start()

    @pl.loop(0, 4)
    def _(k):
        g = group_order(k)
        own_copy(g).wait()
        arrived(part.at[pl.ds(g * 4, 4)], part_recv.at[g])

        @pl.loop(0, 4)
        def _(i):
            source = g * 4 + lax.rem(i + y, 4)
            own[source] = (own[source].astype(F32) + part[source].astype(F32)).astype(BF16)

            @pl.when(is_here(source))
            def _():
                pltpu.make_async_copy(own.at[source], dkv.at[z, half, c], dkv_recv.at[me]).start()

            @pl.when(jnp.logical_not(is_here(source)))
            def _():
                dkv_copy(source).start()

    for load in loads:
        load.start()
    onehot = slot_onehot(slot_rows(event_slot[...].reshape(1, ROWS)))
    normal, inverse = normalize(slots_in[...].astype(F32))
    normed = (normal * gain_in[...]).astype(BF16)
    loads[0].wait()
    for k in range(4):
        cols = slice(k * WIDTH, (k + 1) * WIDTH)
        pre[:, cols] = dot_nn(normed, w_in[:, cols])
    tokens = dot_tn(onehot, slots_in[...])
    gate = dot_tn(onehot, silu(pre[:, 0:WIDTH]).astype(BF16))
    loads[1].wait()
    loads[2].wait()
    d_gated = dot_nt(cot[...], w_out[...]).astype(BF16).astype(F32)
    slot_cot = dot_nn(onehot, cot[...])
    loads[3].wait()
    loads[4].wait()
    item_slope = silu_slope(dot_nn(feats[...], item_weight[...]))

    @pl.loop(0, SEQ)
    def _(w):
        arrived(mq.at[w % 4, :, ((w // 4) % 2) * 2 + w // 8], mq_recv.at[w])

    mixed = jnp.concatenate([mq[h, :, :, :, 0:HEAD].reshape(ROWS, HEAD) for h in range(HEADS)], axis=1)
    normed_mid = normalize(mixed.astype(F32))[0] * gain_mid[...]
    gated = (normed_mid * gate).astype(BF16)
    layer_out[...] = (tokens + dot_nn(gated, w_out[...])).astype(BF16)
    d_gate = dot_nn(onehot, (d_gated * normed_mid).astype(BF16))
    d_pre[...] = (d_gate * silu_slope(pre[:, 0:WIDTH])).astype(BF16)
    d_normed = dot_nt(d_pre[...], w_in[:, 0:WIDTH])
    d_query = jnp.concatenate(
        [mq[h, :, :, :, HEAD : 2 * HEAD].reshape(ROWS, HEAD) for h in range(HEADS)], axis=1
    )
    d_pre[...] = (dot_nn(onehot, d_query) * silu_slope(pre[:, 1024:1536])).astype(BF16)
    d_normed += dot_nt(d_pre[...], w_in[:, 1024:1536])
    for first_column in (512, 1536):
        cols = slice(first_column, first_column + WIDTH)
        pre[:, cols] = silu_slope(pre[:, cols])

    @pl.loop(0, SEQ)
    def _(w):
        arrived(dkv.at[w % 4, (w // 4) % 2, w // 8], dkv_recv.at[w])

    for lanes, first_column in ((0, 1536), (HEAD, 512)):
        cols = slice(first_column, first_column + WIDTH)
        grad = jnp.concatenate(
            [
                dkv[h, 0, :, :, lanes : lanes + HEAD].reshape(SLOTS, HEAD).astype(F32)
                + dkv[h, 1, :, :, lanes : lanes + HEAD].reshape(SLOTS, HEAD).astype(F32)
                for h in range(HEADS)
            ],
            axis=1,
        )
        d_pre[...] = (grad * pre[:, cols]).astype(BF16)
        d_normed += dot_nt(d_pre[...], w_in[:, cols])

    scaled = d_normed * gain_in[...]
    d_slots = slot_cot + inverse * (
        scaled
        - jnp.mean(scaled, axis=-1, keepdims=True)
        - normal * jnp.mean(scaled * normal, axis=-1, keepdims=True)
    )
    out2[...] = d_slots.astype(BF16)
    wait_all(exchange_seq(out2, in2, send2, recv2, b, s))
    out1[...] = dot_nn(by_batch(), in2[...]).astype(BF16)
    last = exchange_batch(out1, in1, send1, recv1, b, s)
    wanted = (iota((256, 256), 0) == send_rows[...]).astype(BF16)
    wait_all(last)
    d_embedded = dot_nn(wanted, in1[...])
    d_item_out[...] = (d_embedded * item_slope).astype(BF16)

    @pl.loop(0, 4)
    def _(g):
        part_copy(g).wait_send()

    @pl.loop(0, SEQ)
    def _(source):
        @pl.when(jnp.logical_not(is_here(source)))
        def _():
            mq_copy(source).wait_send()
            dkv_copy(source).wait_send()


def result_kernel(layer, d_item, item_weight, layer_out, item_grad):
    layer_out[...] = layer[...]
    item_grad[...] = dot_nt(d_item[...], item_weight[...])


def spec(space):
    return pl.BlockSpec(memory_space=space)


VMEM, SMEM, ANY = pltpu.VMEM, pltpu.SMEM, pl.ANY
DMA = pltpu.SemaphoreType.DMA


def shape(dims, dtype):
    return jax.ShapeDtypeStruct(dims, dtype)


def params(remote=None):
    return pltpu.CompilerParams(
        vmem_limit_bytes=56 << 20, has_side_effects=remote is not None, collective_id=remote
    )


def backward_call(meta, ids, kv, q, p, mixed, stats):
    return pl.pallas_call(
        backward_kernel,
        out_shape=(shape((BLOCKS, PIECE, 2 * HEAD), BF16), shape((SEQ, SLOTS, 2 * HEAD), BF16)),
        in_specs=[spec(SMEM)] + [spec(VMEM)] * 5 + [spec(ANY)],
        out_specs=(spec(ANY), spec(ANY)),
        scratch_shapes=[
            VMEM((BLOCKS, BLOCK, 2 * HEAD), BF16),
            VMEM((BLOCKS, PIECE, 2 * HEAD), BF16),
            VMEM((SEQ, SLOTS, 2 * HEAD), BF16),
            VMEM((TILES + 1, BLOCK, HEAD), BF16),
            VMEM((TILES + 1, HEAD, BLOCK), BF16),
            VMEM((TILES + 1, HEAD, BLOCK), BF16),
            VMEM((TILES + 1, BLOCK, HEAD), F32),
            VMEM((BLOCKS, 2 * HEAD, BLOCK), F32),
            DMA,
            DMA,
            DMA((SEQ,)),
        ],
        compiler_params=params(),
        name="backward",
    )(meta, ids, q, p, mixed, stats, kv)


def per_device(
    item_feats, item_weight, send_rows, event_slot, user_blocks, tail_len, block_order, gain_in, gain_mid, w_in, w_out,
    cot_out,
):
    gain_in, gain_mid = gain_in.reshape(1, WIDTH), gain_mid.reshape(1, WIDTH)
    kv, q, p, slots, ids, meta, mixed, stats = pl.pallas_call(
        send_kernel,
        out_shape=(
            shape((BLOCKS, BLOCK, 2 * HEAD), BF16),
            shape((BLOCKS, PIECE, HEAD), BF16),
            shape((BLOCKS, PIECE, HEAD), BF16),
            shape((SLOTS, WIDTH), BF16),
            shape((SEQ, 8, 128), jnp.int32),
            shape((8, 128), jnp.int32),
            shape((TILES, BLOCK, HEAD), F32),
            shape((HEADS, TILES // 2, 8, BLOCK), F32),
        ),
        in_specs=[spec(VMEM)] * 9 + [spec(ANY)] * 3,
        out_specs=(spec(ANY), spec(ANY), spec(ANY)) + (spec(VMEM),) * 5,
        scratch_shapes=[VMEM((WIDTH, 4 * WIDTH), BF16), VMEM((WIDTH, WIDTH), BF16), VMEM((ROWS, WIDTH), BF16)]
        + [VMEM((256, WIDTH), BF16)] * 4
        + [
            VMEM((HEADS, 2, HALF, 2 * HEAD), BF16),
            VMEM((HEADS, 3, 4, PIECE, HEAD), BF16),
            VMEM((HEADS, 3, 4, PIECE, HEAD), BF16),
            VMEM((8, 128), jnp.int32),
            VMEM((SEQ, 8, 128), jnp.int32),
            VMEM((SEQ, 2, HALF, 2 * HEAD), BF16),
            VMEM((BLOCKS, BLOCK, 2 * HEAD), BF16),
            VMEM((BLOCKS, PIECE, HEAD), BF16),
            VMEM((BLOCKS, PIECE, HEAD), BF16),
            SMEM((8, 128), jnp.int32),
            VMEM((MOST_PAIRS, BLOCK, HEAD), F32),
            VMEM((HEADS, TILES // 2, 8, BLOCK), F32),
            DMA((3,)),
            DMA((SEQ,)),
            DMA((2,)),
            DMA,
            DMA((GROUPS,)),
            DMA((GROUPS,)),
        ]
        + [DMA((SEQ,))] * 12
        + [DMA((HEADS,))] * 2,
        compiler_params=params(0),
        name="send",
    )(
        item_feats, item_weight, send_rows, event_slot, user_blocks, tail_len, block_order, gain_in, gain_mid, w_in,
        w_out, cot_out,
    )
    mq, dkv = backward_call(meta, ids, kv, q, p, mixed, stats)
    mq = mq.reshape(SEQ, 3, PIECE, 2 * HEAD)
    dkv = dkv.reshape(SEQ, 2, HALF, 2 * HEAD)
    layer, d_item = pl.pallas_call(
        return_kernel,
        out_shape=(shape((ROWS, WIDTH), BF16), shape((256, WIDTH), BF16)),
        in_specs=[spec(VMEM)] * 5 + [spec(ANY)] * 7,
        out_specs=(spec(VMEM), spec(VMEM)),
        scratch_shapes=[
            VMEM((256, WIDTH), BF16),
            VMEM((WIDTH, WIDTH), BF16),
            VMEM((WIDTH, 4 * WIDTH), BF16),
            VMEM((WIDTH, WIDTH), BF16),
            VMEM((ROWS, WIDTH), BF16),
            VMEM((HEADS, 3, 4, PIECE, 2 * HEAD), BF16),
            VMEM((HEADS, 2, 2, HALF, 2 * HEAD), BF16),
            VMEM((SEQ, HALF, 2 * HEAD), BF16),
            VMEM((SEQ, HALF, 2 * HEAD), BF16),
            VMEM((SLOTS, 4 * WIDTH), F32),
            VMEM((SLOTS, WIDTH), BF16),
        ]
        + [VMEM((256, WIDTH), BF16)] * 4
        + [DMA((5,))]
        + [DMA((4,))] * 3
        + [DMA((SEQ,))] * 6
        + [DMA((GROUPS,))] * 2,
        compiler_params=params(2),
        name="give_back",
    )(
        send_rows, event_slot, gain_in, gain_mid, slots, item_feats, item_weight, w_in, w_out, cot_out, mq, dkv,
    )
    return pl.pallas_call(
        result_kernel,
        out_shape=(shape((ROWS, WIDTH), BF16), shape((256, WIDTH), F32)),
        in_specs=[spec(VMEM)] * 3,
        out_specs=(spec(VMEM), spec(VMEM)),
        compiler_params=params(),
        name="results",
    )(layer, d_item, item_weight)


def solution(mesh):
    rows = P(("batch", "seq"), None)
    return jax.shard_map(
        per_device,
        mesh=mesh,
        in_specs=(
            rows,
            P(),
            rows,
            P(("batch", "seq")),
            P("batch", None),
            P("batch", None),
            P("batch", None),
            P(),
            P(),
            P(),
            P(),
            rows,
        ),
        out_specs=(rows, rows),
        check_vma=False,
    )
```

```python
import jax
import jax.numpy as jnp
from jax import lax
from jax.experimental import pallas as pl
from jax.experimental.pallas import tpu as pltpu
from jax.sharding import PartitionSpec as P

WIDTH = 512
HEAD = 128
HEADS = 4
BLOCK = 128
BLOCKS = 48
SEQ = 16
GROUPS = 8
PIECE = 32
TILES = 12
SLOTS = 256
HALF = 128
ROWS = 384
FAR = 30000
NO_BLOCK = 200
AT_ONCE = 4
MOST_PAIRS = 48
MOST_CHUNKS = 7
BACK_AT_ONCE = 4
SCALE = HEAD**-0.5
MESH = pl.DeviceIdType.MESH
F32 = jnp.float32
BF16 = jnp.bfloat16


def dot_nn(a, b):
    return jnp.dot(a, b, preferred_element_type=F32)


def dot_nt(a, b):
    return lax.dot_general(a, b, (((1,), (1,)), ((), ())), preferred_element_type=F32)


def dot_tn(a, b):
    return lax.dot_general(a, b, (((0,), (0,)), ((), ())), preferred_element_type=F32)


def silu(v):
    u = 0.5 * v
    return u + u * jnp.tanh(u)


def silu_slope(v):
    u = 0.5 * v
    t = jnp.tanh(u)
    a = 1.0 + t
    return 0.5 * (a + u * a * (1.0 - t))


def normalize(values):
    mean = jnp.mean(values, axis=-1, keepdims=True)
    centred = values - mean
    spread = jnp.mean(centred * centred, axis=-1, keepdims=True)
    inverse = lax.rsqrt(spread + 1e-05)
    return centred * inverse, inverse


def iota(shape, dim):
    return lax.broadcasted_iota(jnp.int32, shape, dim)


def place():
    b, s = lax.axis_index("batch"), lax.axis_index("seq")
    return b, s, b // 2, b % 2, s // 4, s % 4


def worker_at(w, x, c):
    head, half, core = w % 4, (w // 4) % 2, w // 8
    return head, half, core, x * 2 + core, (2 * c + half) * 4 + head


def copy_to(src, dst, send, recv, batch, seq):
    return pltpu.make_async_remote_copy(
        src_ref=src, dst_ref=dst, send_sem=send, recv_sem=recv, device_id=(batch, seq), device_id_type=MESH
    )


def arrived(ref, sem):
    pltpu.make_async_copy(ref, ref, sem).wait()


def rows_of(index, size):
    return pl.ds(pl.multiple_of(index * size, size), size)


def slot_rows(event_slot):
    e = event_slot
    return ((e >> 1) & 15) * 16 + (e >> 5) * 2 + (e & 1)


def slot_onehot(wanted):
    return (iota((SLOTS, wanted.shape[1]), 0) == wanted).astype(BF16)


def by_seq():
    i, j = iota((256, 256), 0), iota((256, 256), 1)
    return (j == ((i >> 1) & 7) * 32 + (i >> 4) * 2 + (i & 1)).astype(BF16)


def by_batch():
    i, j = iota((256, 256), 0), iota((256, 256), 1)
    return (j == ((i >> 1) & 15) * 16 + (i >> 5) * 2 + (i & 1)).astype(BF16)


def exchange_batch(src, dst, send, recv, b, s):
    copies = []
    for k in range(1, GROUPS):
        peer = lax.rem(b + k, GROUPS)
        copy = copy_to(src.at[rows_of(peer, 32)], dst.at[rows_of(b, 32)], send.at[k], recv.at[k], peer, s)
        copy.start()
        copies.append(copy)
    dst[rows_of(b, 32), :] = src[rows_of(b, 32), :]
    return copies


def exchange_seq(src, dst, send, recv, b, s):
    copies = []
    for k in range(1, SEQ):
        peer = lax.rem(s + k, SEQ)
        copy = copy_to(src.at[rows_of(peer, 16)], dst.at[rows_of(s, 16)], send.at[k], recv.at[k], b, peer)
        copy.start()
        copies.append(copy)
    dst[rows_of(s, 16), :] = src[rows_of(s, 16), :]
    return copies


def signal(barrier, batch, seq):
    pl.semaphore_signal(barrier, inc=1, device_id=(batch, seq), device_id_type=MESH)


def greet(b, s, partner):
    barrier = pltpu.get_barrier_semaphore()
    for k in range(1, GROUPS):
        signal(barrier, lax.rem(b + k, GROUPS), s)

    @pl.loop(1, SEQ)
    def _(k):
        peer = lax.rem(s + k, SEQ)
        signal(barrier, b, peer)
        signal(barrier, partner, peer)


def greeted():
    pl.semaphore_wait(pltpu.get_barrier_semaphore(), GROUPS - 1 + 2 * (SEQ - 1))


def wait_all(copies):
    for copy in copies:
        copy.wait()


def layer_kernel(
    feats, item_weight, send_rows, event_slot, user_blocks, tail_len, block_order, gain_in, gain_mid,
    w_in_hbm, w_out_hbm, cot_hbm, layer_out, d_item_out, *scratch,
):
    (
        w_in, w_out, cot, out1, in1, out2, in2, kv, q, p, ids, ids_in, kv_in, kv_events, q_in, p_in, tables_vmem, tables,
        spans, products, kv_products, stats, mixed_of, mixed_sorted, dq_sorted, mixed_slots, dq_slots, mixed_home,
        dq_home, d_mixed, d_mixed_t, query_t, own, give, part, summed, dkv_home, pre, d_pre, gate_of, d_gated_of, normal_of,
        inverse_of, back2, home2, back1, home1,
    ) = scratch[:47]
    (
        load_sem, table_sem, send1, recv1, send2, recv2, kv_send, kv_recv, pass_send, pass_recv, q_send, q_recv, p_send,
        p_recv, ids_send, ids_recv, stats_send, stats_recv, mixed_send, mixed_recv, dq_send, dq_recv, part_send,
        part_recv, dkv_send, dkv_recv, back2_send, back2_recv, back1_send, back1_recv,
    ) = scratch[47:]
    b, s, x, c, y, z = place()
    partner = x * 2 + 1 - c
    half = y % 2
    to_batch = x * 2 + y // 2
    me = z + 4 * half + 8 * c
    greet(b, s, partner)
    loads = [
        pltpu.make_async_copy(src, dst, load_sem.at[k])
        for k, (src, dst) in enumerate(((w_out_hbm, w_out), (cot_hbm, cot), (w_in_hbm, w_in)))
    ]
    for load in loads:
        load.start()

    embedded = silu(dot_nn(feats[...], item_weight[...])).astype(BF16)
    wanted = (iota((256, 256), 0) == send_rows[...]).astype(BF16)
    out1[...] = dot_tn(wanted, embedded).astype(BF16)
    slot_of_event = slot_rows(event_slot[...].reshape(1, ROWS))
    ids[...] = jnp.zeros_like(ids)
    for k in range(3):
        ids[k : k + 1, :] = slot_of_event[:, k * BLOCK : (k + 1) * BLOCK]
    ids[3:4, 0:BLOCKS] = block_order[...]
    ids[4:5, 0:4] = user_blocks[...]
    ids[5:6, 0:4] = tail_len[...]
    greeted()
    first = exchange_batch(out1, in1, send1, recv1, b, s)

    def each_worker(act):
        @pl.loop(0, SEQ)
        def _(i):
            w = lax.rem(i + s, SEQ)
            head, half, core, to_batch, to_seq = worker_at(w, x, c)
            here = (to_batch == b) & (to_seq == s)
            act(w, head, half, core, to_batch, to_seq, here)

    def start(here, src, dst, recv, remote):
        @pl.when(here)
        def _():
            pltpu.make_async_copy(src, dst, recv).start()

        @pl.when(jnp.logical_not(here))
        def _():
            remote.start()

    def ids_copy(w, to_batch, to_seq):
        return copy_to(ids, ids_in.at[s], ids_send.at[w], ids_recv.at[s], to_batch, to_seq)

    def start_ids(w, head, half, core, to_batch, to_seq, here):
        start(here, ids, ids_in.at[s], ids_recv.at[s], ids_copy(w, to_batch, to_seq))

    each_worker(start_ids)

    loads[0].wait()
    loads[1].wait()
    d_gated_of[...] = dot_nt(cot[...], w_out[...]).astype(BF16)
    wait_all(first)
    out2[...] = dot_nn(by_seq(), in1[...]).astype(BF16)
    second = exchange_seq(out2, in2, send2, recv2, b, s)
    onehot = slot_onehot(slot_of_event)
    loads[2].wait()
    wait_all(second)
    normal, inverse = normalize(in2[...].astype(F32))
    normal_of[...] = normal
    inverse_of[...] = jnp.broadcast_to(inverse, (SLOTS, 128))
    normed = (normal * gain_in[...]).astype(BF16)

    def project(first_column):
        cols = slice(first_column, first_column + WIDTH)
        made = dot_nn(normed, w_in[:, cols])
        pre[:, cols] = made
        return silu(made)

    for side, first_column in ((0, 1536), (1, 512)):
        lanes = slice(side * HEAD, side * HEAD + HEAD)
        made = project(first_column).astype(BF16)
        for h in range(HEADS):
            kv[h, 0, :, lanes] = made[:HALF, h * HEAD : (h + 1) * HEAD]
            kv[h, 1, :, lanes] = made[HALF:, h * HEAD : (h + 1) * HEAD]

    def kv_copy(w, head, core, to_batch, to_seq):
        return copy_to(kv.at[head, core], kv_in.at[s, core], kv_send.at[w], kv_recv.at[s], to_batch, to_seq)

    def start_kv(w, head, half, core, to_batch, to_seq, here):
        start(
            here, kv.at[head, core], kv_in.at[s, core], kv_recv.at[s], kv_copy(w, head, core, to_batch, to_seq)
        )

    each_worker(start_kv)

    query = (project(1024) * (0.5 * SCALE)).astype(BF16)
    query = dot_tn(onehot, query).astype(BF16)
    for h in range(HEADS):
        q[h] = query[:, h * HEAD : (h + 1) * HEAD].reshape(3, 4, PIECE, HEAD)

    def piece_copy(src, dst, send, recv, w, head, half, core, to_batch, to_seq):
        three = pl.ds(s * 3, 3)
        return copy_to(
            src.at[head, :, half * 2 + core], dst.at[three], send.at[w], recv.at[s], to_batch, to_seq
        )

    def start_piece(src, dst, send, recv):
        def act(w, head, half, core, to_batch, to_seq, here):
            start(
                here, src.at[head, :, half * 2 + core], dst.at[pl.ds(s * 3, 3)], recv.at[s],
                piece_copy(src, dst, send, recv, w, head, half, core, to_batch, to_seq),
            )

        each_worker(act)

    start_piece(q, q_in, q_send, q_recv)
    gate = dot_tn(onehot, project(0).astype(BF16))
    gate_of[...] = gate
    upstream = (d_gated_of[...].astype(F32) * gate * gain_mid[...]).astype(BF16)
    for h in range(HEADS):
        p[h] = upstream[:, h * HEAD : (h + 1) * HEAD].reshape(3, 4, PIECE, HEAD)
    start_piece(p, p_in, p_send, p_recv)

    @pl.loop(0, SEQ)
    def _(source):
        arrived(ids_in.at[source], ids_recv.at[source])

    tables_vmem[...] = tables_of(ids_in[s], half * 2 + c)
    table_copy = pltpu.make_async_copy(tables_vmem, tables, table_sem)
    table_copy.start()

    def pass_on(source):
        return copy_to(
            kv_in.at[source, c], kv_in.at[source, c], pass_send.at[source], pass_recv.at[source], partner, s
        )

    @pl.loop(0, SEQ + 2)
    def _(i):
        @pl.when(i < SEQ)
        def _():
            source = lax.rem(s - i + SEQ, SEQ)
            arrived(kv_in.at[source, c], kv_recv.at[source])
            pass_on(source).start()

        @pl.when(i >= 2)
        def _():
            source = lax.rem(s - i + 2 + SEQ, SEQ)
            arrived(kv_in.at[source, 1 - c], pass_recv.at[source])
            rows = jnp.concatenate([ids_in[source].astype(F32), jnp.zeros((120, 128), F32)], axis=0)
            columns = jnp.transpose(rows)
            lane = iota((BLOCK, SLOTS), 1).astype(F32)
            read = jnp.concatenate([(lane == columns[:, k : k + 1]).astype(BF16) for k in range(3)], axis=0)
            slots = kv_in[source].reshape(SLOTS, 2 * HEAD)
            made = dot_nn(read, slots).astype(BF16).reshape(3, BLOCK, 2 * HEAD)
            kv_events[pl.ds(source * 3, 3)] = made

    table_copy.wait()

    @pl.loop(0, SEQ)
    def _(source):
        arrived(q_in.at[pl.ds(source * 3, 3)], q_recv.at[source])

    def step(k, state):
        pairs, t, j = walk(tables, *state, AT_ONCE)
        keyvals = [four(kv_events, tables, j) for _, j in pairs]
        us = [dot_nt(four(q_in, tables, t), keyval[:, :HEAD]) for (t, _), keyval in zip(pairs, keyvals)]
        weights = []
        for (t_, j_), u in zip(pairs, us):
            w = u.astype(BF16) * (1.0 + jnp.tanh(u)).astype(BF16)
            weights.append(jnp.where(visible(tables, t_, j_), w, jnp.zeros_like(w)))
        for n, (w, keyval) in enumerate(zip(weights, keyvals)):
            products[k * AT_ONCE + n] = dot_nn(w, keyval[:, HEAD:])
        return t, j

    lax.fori_loop(0, MOST_PAIRS // AT_ONCE, step, (jnp.int32(0), jnp.int32(0)))

    @pl.loop(0, SEQ)
    def _(source):
        arrived(p_in.at[pl.ds(source * 3, 3)], p_recv.at[source])

    def sum_pairs(t, first, count):
        summed = products[jnp.minimum(first, MOST_PAIRS - 1)]
        for k in range(1, min(t + 1, MOST_CHUNKS)):
            more = products[jnp.minimum(first + k, MOST_PAIRS - 1)]
            summed = summed + jnp.where(k < count, more, jnp.zeros_like(more))
        return summed

    starts = []
    first_pair = jnp.int32(0)
    for t in range(TILES):
        count = t + 1 - tables[1, 4 * t] // 4
        starts.append((first_pair, count))
        spans[0, t] = first_pair
        spans[1, t] = tables[1, 4 * t] // 4
        mixed = sum_pairs(t, first_pair, count)
        first_pair = first_pair + count
        upstream = four(p_in, tables, t).astype(F32)
        mixed_of[t] = mixed
        mixed_sorted[4 * t : 4 * t + 4] = mixed.astype(BF16).reshape(4, PIECE, HEAD)
        mean = jnp.mean(mixed, axis=1, keepdims=True)
        centred = mixed - mean
        sums = pick4(
            iota((BLOCK, HEAD), 1) & 3,
            [
                mean,
                jnp.sum(centred * centred, axis=1, keepdims=True),
                jnp.sum(upstream, axis=1, keepdims=True),
                jnp.sum(upstream * centred, axis=1, keepdims=True),
            ],
        )
        rows = slice(4 * (t % 2), 4 * (t % 2) + 4)
        stats[z, t // 2, rows, :] = jnp.transpose(sums)[rows, :]

    copies = []
    for k in range(1, HEADS):
        peer = lax.rem(z + k, HEADS)
        copy = copy_to(stats.at[z], stats.at[z], stats_send.at[k], stats_recv.at[k], b, y * 4 + peer)
        copy.start()
        copies.append(copy)

    def is_here(source):
        return (to_batch == b) & (source == s)

    def home_copy(src, dst, send, recv, source):
        three = pl.ds(source * 3, 3)
        return copy_to(
            src.at[three], dst.at[z, :, half * 2 + c], send.at[source], recv.at[me], to_batch, source
        )

    def send_home(src, dst, send, recv):
        @pl.loop(0, SEQ)
        def _(i):
            source = lax.rem(i + s, SEQ)
            start(
                is_here(source), src.at[pl.ds(source * 3, 3)], dst.at[z, :, half * 2 + c], recv.at[me],
                home_copy(src, dst, send, recv, source),
            )

    @pl.loop(0, BLOCKS)
    def _(i):
        mixed_slots[i] = mixed_sorted[tables[4, i]]

    send_home(mixed_slots, mixed_home, mixed_send, mixed_recv)

    d_mixed[TILES] = jnp.zeros((BLOCK, HEAD), BF16)
    d_mixed_t[TILES] = jnp.zeros((HEAD, BLOCK), BF16)
    query_t[TILES] = jnp.zeros((HEAD, BLOCK), BF16)
    for t in range(TILES):
        query_t[t] = jnp.transpose(four(q_in, tables, t))
    wait_all(copies)
    for t in range(TILES):
        rows = slice(4 * (t % 2), 4 * (t % 2) + 4)
        of = [stats[h, t // 2, rows, :] for h in range(HEADS)]
        mean = sum(v[0:1] for v in of) * 0.25
        spread = sum(v[1:2] + HEAD * (v[0:1] - mean) * (v[0:1] - mean) for v in of) * (1.0 / WIDTH)
        inverse = lax.rsqrt(spread + 1e-05)
        slant = sum(v[2:3] for v in of) * (1.0 / WIDTH)
        along = sum(v[3:4] + v[2:3] * (v[0:1] - mean) for v in of) * (1.0 / WIDTH) * inverse
        columns = jnp.transpose(pick4(iota((BLOCK, HEAD), 0), [mean, inverse, slant, along]))
        mean, inverse, slant, along = (columns[:, i : i + 1] for i in range(4))
        made = (mixed_of[t] - mean) * inverse
        made = (inverse * (four(p_in, tables, t).astype(F32) - slant - made * along)).astype(BF16)
        d_mixed[t] = made
        d_mixed_t[t] = jnp.transpose(made)

    def back_step(k, state):
        pairs, t, j = walk(tables, *state, BACK_AT_ONCE)
        keyvals = [four(kv_events, tables, j) for _, j in pairs]
        us = [dot_nt(four(q_in, tables, t), keyval[:, :HEAD]) for (t, _), keyval in zip(pairs, keyvals)]
        d_weights = [dot_nt(d_mixed[t], keyval[:, HEAD:]) for (t, _), keyval in zip(pairs, keyvals)]
        made = []
        for (t_, j_), u, dw in zip(pairs, us, d_weights):
            th = jnp.tanh(u)
            a = (1.0 + th).astype(BF16)
            w = u.astype(BF16) * a
            ds = dw.astype(BF16) * (a + w * (1.0 - th).astype(BF16))
            seen = visible(tables, t_, j_)
            made.append((jnp.where(seen, w, jnp.zeros_like(w)), jnp.where(seen, ds, jnp.zeros_like(ds))))
        for n, ((t_, _), keyval, (w, ds)) in enumerate(zip(pairs, keyvals, made)):
            pair = k * BACK_AT_ONCE + n
            d_key = dot_nn(query_t[t_], ds).astype(BF16)
            d_value = dot_nn(d_mixed_t[t_], w).astype(BF16)
            for i in range(4):
                kv_products[pair, i, 0:HEAD] = d_key[:, i * BLOCK : (i + 1) * BLOCK]
                kv_products[pair, i, HEAD : 2 * HEAD] = d_value[:, i * BLOCK : (i + 1) * BLOCK]
            products[pair] = dot_nn(ds, keyval[:, :HEAD])
        return t, j

    lax.fori_loop(0, MOST_PAIRS // BACK_AT_ONCE, back_step, (jnp.int32(0), jnp.int32(0)))

    for t in range(TILES):
        dq = (sum_pairs(t, *starts[t]) * (0.5 * SCALE)).astype(BF16)
        dq_sorted[4 * t : 4 * t + 4] = dq.reshape(4, PIECE, HEAD)

    @pl.loop(0, BLOCKS)
    def _(i):
        dq_slots[i] = dq_sorted[tables[4, i]]

    send_home(dq_slots, dq_home, dq_send, dq_recv)

    def block_grad(n):
        j = n // 4
        total = jnp.zeros((2 * HEAD, BLOCK), F32)
        for k in range(MOST_CHUNKS):
            t = jnp.minimum(j + k, TILES - 1)
            since = spans[1, t]
            pair = jnp.clip(spans[0, t] + j - since, 0, MOST_PAIRS - 1)
            more = kv_products[pair, n % 4].astype(F32)
            total += jnp.where((j + k < TILES) & (since <= j), more, jnp.zeros_like(more))
        return total.astype(BF16)

    def part_copy(source):
        return copy_to(
            give.at[source], part.at[source], part_send.at[source], part_recv.at[source], partner, s
        )

    def dkv_copy(source):
        return copy_to(
            summed.at[source], dkv_home.at[z, half, c], dkv_send.at[source], dkv_recv.at[me], to_batch, source
        )

    @pl.loop(0, SEQ + 2)
    def _(i):
        @pl.when(i < SEQ)
        def _():
            source = lax.rem(s + i, SEQ)
            wanted = jnp.concatenate([ids_in[source, m : m + 1, :] for m in range(3)], axis=1)
            grads = jnp.concatenate([block_grad(tables[4, source * 3 + m]) for m in range(3)], axis=1)
            made = dot_nt(slot_onehot(wanted), grads).astype(BF16)
            own[source] = jnp.where(c == 0, made[:HALF], made[HALF:])
            give[source] = jnp.where(c == 0, made[HALF:], made[:HALF])
            part_copy(source).start()

        @pl.when(i >= 2)
        def _():
            source = lax.rem(s + i - 2, SEQ)
            arrived(part.at[source], part_recv.at[source])
            summed[source] = (own[source].astype(F32) + part[source].astype(F32)).astype(BF16)
            start(
                is_here(source), summed.at[source], dkv_home.at[z, half, c], dkv_recv.at[me], dkv_copy(source)
            )

    tokens = dot_tn(onehot, in2[...])
    slot_cot = dot_nn(onehot, cot[...])
    item_slope = silu_slope(dot_nn(feats[...], item_weight[...]))
    for first_column in range(0, 4 * WIDTH, WIDTH):
        cols = slice(first_column, first_column + WIDTH)
        pre[:, cols] = silu_slope(pre[:, cols])

    @pl.loop(0, SEQ)
    def _(w):
        arrived(mixed_home.at[w % 4, :, ((w // 4) % 2) * 2 + w // 8], mixed_recv.at[w])

    mixed = jnp.concatenate([mixed_home[h].reshape(ROWS, HEAD) for h in range(HEADS)], axis=1)
    normed_mid = normalize(mixed.astype(F32))[0] * gain_mid[...]
    gated = (normed_mid * gate_of[...]).astype(BF16)
    layer_out[...] = (tokens + dot_nn(gated, w_out[...])).astype(BF16)
    d_gate = dot_nn(onehot, (d_gated_of[...].astype(F32) * normed_mid).astype(BF16))
    d_pre[...] = (d_gate * pre[:, 0:WIDTH]).astype(BF16)
    d_normed = dot_nt(d_pre[...], w_in[:, 0:WIDTH])

    @pl.loop(0, SEQ)
    def _(w):
        arrived(dq_home.at[w % 4, :, ((w // 4) % 2) * 2 + w // 8], dq_recv.at[w])

    d_query = jnp.concatenate([dq_home[h].reshape(ROWS, HEAD) for h in range(HEADS)], axis=1)
    d_pre[...] = (dot_nn(onehot, d_query) * pre[:, 1024:1536]).astype(BF16)
    d_normed += dot_nt(d_pre[...], w_in[:, 1024:1536])

    @pl.loop(0, SEQ)
    def _(w):
        arrived(dkv_home.at[w % 4, (w // 4) % 2, w // 8], dkv_recv.at[w])

    for lanes, first_column in ((0, 1536), (HEAD, 512)):
        cols = slice(first_column, first_column + WIDTH)
        grad = jnp.concatenate(
            [
                dkv_home[h, 0, :, :, lanes : lanes + HEAD].reshape(SLOTS, HEAD).astype(F32)
                + dkv_home[h, 1, :, :, lanes : lanes + HEAD].reshape(SLOTS, HEAD).astype(F32)
                for h in range(HEADS)
            ],
            axis=1,
        )
        d_pre[...] = (grad * pre[:, cols]).astype(BF16)
        d_normed += dot_nt(d_pre[...], w_in[:, cols])

    scaled = d_normed * gain_in[...]
    normal = normal_of[...]
    d_slots = slot_cot + inverse_of[:, 0:1] * (
        scaled
        - jnp.mean(scaled, axis=-1, keepdims=True)
        - normal * jnp.mean(scaled * normal, axis=-1, keepdims=True)
    )
    back2[...] = d_slots.astype(BF16)
    wait_all(exchange_seq(back2, home2, back2_send, back2_recv, b, s))
    back1[...] = dot_nn(by_batch(), home2[...]).astype(BF16)
    last = exchange_batch(back1, home1, back1_send, back1_recv, b, s)
    wanted = (iota((256, 256), 0) == send_rows[...]).astype(BF16)
    wait_all(last)
    d_embedded = dot_nn(wanted, home1[...])
    d_item_out[...] = (d_embedded * item_slope).astype(BF16)

    def finish(w, head, half, core, to_batch, to_seq, here):
        @pl.when(jnp.logical_not(here))
        def _():
            ids_copy(w, to_batch, to_seq).wait_send()
            kv_copy(w, head, core, to_batch, to_seq).wait_send()
            piece_copy(q, q_in, q_send, q_recv, w, head, half, core, to_batch, to_seq).wait_send()
            piece_copy(p, p_in, p_send, p_recv, w, head, half, core, to_batch, to_seq).wait_send()

    each_worker(finish)

    @pl.loop(0, SEQ)
    def _(source):
        pass_on(source).wait_send()
        part_copy(source).wait_send()

        @pl.when(jnp.logical_not(is_here(source)))
        def _():
            home_copy(mixed_slots, mixed_home, mixed_send, mixed_recv, source).wait_send()
            home_copy(dq_slots, dq_home, dq_send, dq_recv, source).wait_send()
            dkv_copy(source).wait_send()


def tables_of(meta, quarter):
    slot, lane = iota((128, 128), 0), iota((1, 128), 1)
    held = jnp.transpose(jnp.broadcast_to(meta[3:4, :], (128, 128)))
    slot_of = jnp.where((held == iota((128, 128), 1)) & (slot < BLOCKS), slot, 0)
    slot_of = jnp.minimum(jnp.sum(slot_of, axis=0, keepdims=True), BLOCKS - 1)
    first = jnp.zeros((1, 1), jnp.int32)
    start_of = jnp.zeros((1, 128), jnp.int32)
    limit_of = jnp.full((1, 128), BLOCK, jnp.int32)
    for u in range(4):
        start_of = jnp.where(lane >= first, first, start_of)
        first = first + meta[4:5, u : u + 1]
        limit_of = jnp.where(lane == first - 1, meta[5:6, u : u + 1], limit_of)
    start_of = jnp.where(lane < BLOCKS, start_of, NO_BLOCK)
    row = iota((8, 128), 0)
    picked = pick4(row, [slot_of, start_of, limit_of, jnp.zeros((1, 128), jnp.int32) + quarter])
    return jnp.where(row == 4, meta[3:4, :], picked)


def pick4(index, values):
    return jnp.where(index == 0, values[0], jnp.where(index == 1, values[1], jnp.where(index == 2, values[2], values[3])))


def first_chunk(meta, t):
    return jnp.clip(meta[1, 4 * t] // 4, 0, TILES - 1)


def walk(meta, t, j, count):
    pairs = []
    for _ in range(count):
        pairs.append((t, j))
        more = j < jnp.minimum(t, TILES - 1)
        after = jnp.minimum(t + 1, TILES)
        j = jnp.where(more, j + 1, first_chunk(meta, after))
        t = jnp.where(more, t, after)
    return pairs, t, j


def pairs_in_all(meta):
    return sum(t + 1 - meta[1, 4 * t] // 4 for t in range(TILES))


def four(ref, meta, n):
    return jnp.concatenate([ref[meta[0, 4 * n + i]] for i in range(4)], axis=0)


def visible(meta, t, j):
    r, lane = iota((BLOCK, 1), 0), iota((1, BLOCK), 1)
    at = (t * 4 + (r >> 5)) * BLOCK + meta[3, 0] * PIECE + (r & 31)
    since = pick4(r >> 5, [meta[1, t * 4 + i] for i in range(4)]) * BLOCK
    where = jnp.concatenate(
        [jnp.where(lane < meta[2, j * 4 + i], (j * 4 + i) * BLOCK + lane, FAR) for i in range(4)], axis=1
    )
    where, at, since = (v.astype(jnp.int16) for v in (where, at, since))
    return (where <= at) & (where >= since)


def result_kernel(layer, d_item, item_weight, layer_out, item_grad):
    layer_out[...] = layer[...]
    item_grad[...] = dot_nt(d_item[...], item_weight[...])


def spec(space):
    return pl.BlockSpec(memory_space=space)


VMEM, SMEM, ANY = pltpu.VMEM, pltpu.SMEM, pl.ANY
DMA = pltpu.SemaphoreType.DMA


def shape(dims, dtype):
    return jax.ShapeDtypeStruct(dims, dtype)


def params(remote=None):
    return pltpu.CompilerParams(
        vmem_limit_bytes=56 << 20, has_side_effects=remote is not None, collective_id=remote
    )


def per_device(
    item_feats, item_weight, send_rows, event_slot, user_blocks, tail_len, block_order, gain_in, gain_mid, w_in, w_out,
    cot_out,
):
    gain_in, gain_mid = gain_in.reshape(1, WIDTH), gain_mid.reshape(1, WIDTH)
    wide = VMEM((256, WIDTH), BF16)
    pieces = VMEM((BLOCKS, PIECE, HEAD), BF16)
    by_head = VMEM((HEADS, 3, 4, PIECE, HEAD), BF16)
    tiles = VMEM((TILES + 1, BLOCK, HEAD), BF16)
    each, one = DMA((SEQ,)), DMA((GROUPS,))
    layer, d_item = pl.pallas_call(
        layer_kernel,
        out_shape=(shape((ROWS, WIDTH), BF16), shape((256, WIDTH), BF16)),
        in_specs=[spec(VMEM)] * 9 + [spec(ANY)] * 3,
        out_specs=(spec(VMEM), spec(VMEM)),
        scratch_shapes=[
            VMEM((WIDTH, 4 * WIDTH), BF16),
            VMEM((WIDTH, WIDTH), BF16),
            VMEM((ROWS, WIDTH), BF16),
            wide,
            wide,
            wide,
            wide,
            VMEM((HEADS, 2, HALF, 2 * HEAD), BF16),
            by_head,
            by_head,
            VMEM((8, 128), jnp.int32),
            VMEM((SEQ, 8, 128), jnp.int32),
            VMEM((SEQ, 2, HALF, 2 * HEAD), BF16),
            VMEM((BLOCKS, BLOCK, 2 * HEAD), BF16),
            pieces,
            pieces,
            VMEM((8, 128), jnp.int32),
            SMEM((8, 128), jnp.int32),
            SMEM((2, 16), jnp.int32),
            VMEM((MOST_PAIRS, BLOCK, HEAD), F32),
            VMEM((MOST_PAIRS, 4, 2 * HEAD, BLOCK), BF16),
            VMEM((HEADS, TILES // 2, 8, BLOCK), F32),
            VMEM((TILES, BLOCK, HEAD), F32),
            pieces,
            pieces,
            pieces,
            pieces,
            by_head,
            by_head,
            tiles,
            tiles,
            tiles,
            VMEM((SEQ, HALF, 2 * HEAD), BF16),
            VMEM((SEQ, HALF, 2 * HEAD), BF16),
            VMEM((SEQ, HALF, 2 * HEAD), BF16),
            VMEM((SEQ, HALF, 2 * HEAD), BF16),
            VMEM((HEADS, 2, 2, HALF, 2 * HEAD), BF16),
            VMEM((SLOTS, 4 * WIDTH), F32),
            VMEM((SLOTS, WIDTH), BF16),
            VMEM((ROWS, WIDTH), F32),
            VMEM((ROWS, WIDTH), BF16),
            VMEM((SLOTS, WIDTH), F32),
            VMEM((SLOTS, 128), F32),
            wide,
            wide,
            wide,
            wide,
            DMA((3,)),
            DMA,
            one,
            one,
            *([each] * 12),
            DMA((HEADS,)),
            DMA((HEADS,)),
            *([each] * 4),
            *([each] * 6),
            one,
            one,
        ],
        compiler_params=params(0),
        name="layer",
    )(
        item_feats, item_weight, send_rows, event_slot, user_blocks, tail_len, block_order, gain_in, gain_mid, w_in,
        w_out, cot_out,
    )
    return pl.pallas_call(
        result_kernel,
        out_shape=(shape((ROWS, WIDTH), BF16), shape((256, WIDTH), F32)),
        in_specs=[spec(VMEM)] * 3,
        out_specs=(spec(VMEM), spec(VMEM)),
        compiler_params=params(),
        name="results",
    )(layer, d_item, item_weight)


def solution(mesh):
    rows = P(("batch", "seq"), None)
    return jax.shard_map(
        per_device,
        mesh=mesh,
        in_specs=(
            rows,
            P(),
            rows,
            P(("batch", "seq")),
            P("batch", None),
            P("batch", None),
            P("batch", None),
            P(),
            P(),
            P(),
            P(),
            rows,
        ),
        out_specs=(rows, rows),
        check_vma=False,
    )
```

```python
import jax
import jax.numpy as jnp
from jax import lax
from jax.experimental import pallas as pl
from jax.experimental.pallas import tpu as pltpu
from jax.sharding import PartitionSpec as P

WIDTH = 512
HEAD = 128
HEADS = 4
BLOCK = 128
BLOCKS = 48
SEQ = 16
GROUPS = 8
PIECE = 32
TILES = 12
SLOTS = 256
HALF = 128
ROWS = 384
FAR = 30000
NO_BLOCK = 200
AT_ONCE = 6
MOST_PAIRS = 48
MOST_CHUNKS = 7
BACK_AT_ONCE = 6
SCALE = HEAD**-0.5
MESH = pl.DeviceIdType.MESH
F32 = jnp.float32
BF16 = jnp.bfloat16


def dot_nn(a, b):
    return jnp.dot(a, b, preferred_element_type=F32)


def dot_nt(a, b):
    return lax.dot_general(a, b, (((1,), (1,)), ((), ())), preferred_element_type=F32)


def dot_tn(a, b):
    return lax.dot_general(a, b, (((0,), (0,)), ((), ())), preferred_element_type=F32)


def silu(v):
    u = 0.5 * v
    return u + u * jnp.tanh(u)


def silu_slope(v):
    u = 0.5 * v
    t = jnp.tanh(u)
    a = 1.0 + t
    return 0.5 * (a + u * a * (1.0 - t))


def normalize(values):
    mean = jnp.mean(values, axis=-1, keepdims=True)
    centred = values - mean
    spread = jnp.mean(centred * centred, axis=-1, keepdims=True)
    inverse = lax.rsqrt(spread + 1e-05)
    return centred * inverse, inverse


def iota(shape, dim):
    return lax.broadcasted_iota(jnp.int32, shape, dim)


def place():
    b, s = lax.axis_index("batch"), lax.axis_index("seq")
    return b, s, b // 2, b % 2, s // 4, s % 4


def worker_at(w, x, c):
    head, half, core = w % 4, (w // 4) % 2, w // 8
    return head, half, core, x * 2 + core, (2 * c + half) * 4 + head


def copy_to(src, dst, send, recv, batch, seq):
    return pltpu.make_async_remote_copy(
        src_ref=src, dst_ref=dst, send_sem=send, recv_sem=recv, device_id=(batch, seq), device_id_type=MESH
    )


def arrived(ref, sem):
    pltpu.make_async_copy(ref, ref, sem).wait()


def rows_of(index, size):
    return pl.ds(pl.multiple_of(index * size, size), size)


def slot_rows(event_slot):
    e = event_slot
    return ((e >> 1) & 15) * 16 + (e >> 5) * 2 + (e & 1)


def slot_onehot(wanted):
    return (iota((SLOTS, wanted.shape[1]), 0) == wanted).astype(BF16)


def by_seq():
    i, j = iota((256, 256), 0), iota((256, 256), 1)
    return (j == ((i >> 1) & 7) * 32 + (i >> 4) * 2 + (i & 1)).astype(BF16)


def by_batch():
    i, j = iota((256, 256), 0), iota((256, 256), 1)
    return (j == ((i >> 1) & 15) * 16 + (i >> 5) * 2 + (i & 1)).astype(BF16)


def exchange_batch(src, dst, send, recv, b, s):
    copies = []
    for k in range(1, GROUPS):
        peer = lax.rem(b + k, GROUPS)
        copy = copy_to(src.at[rows_of(peer, 32)], dst.at[rows_of(b, 32)], send.at[k], recv.at[k], peer, s)
        copy.start()
        copies.append(copy)
    dst[rows_of(b, 32), :] = src[rows_of(b, 32), :]
    return copies


def exchange_seq(src, dst, send, recv, b, s):
    copies = []
    for k in range(1, SEQ):
        peer = lax.rem(s + k, SEQ)
        copy = copy_to(src.at[rows_of(peer, 16)], dst.at[rows_of(s, 16)], send.at[k], recv.at[k], b, peer)
        copy.start()
        copies.append(copy)
    dst[rows_of(s, 16), :] = src[rows_of(s, 16), :]
    return copies


def signal(barrier, batch, seq):
    pl.semaphore_signal(barrier, inc=1, device_id=(batch, seq), device_id_type=MESH)


def greet(b, s, partner):
    barrier = pltpu.get_barrier_semaphore()
    for k in range(1, GROUPS):
        signal(barrier, lax.rem(b + k, GROUPS), s)

    @pl.loop(1, SEQ)
    def _(k):
        peer = lax.rem(s + k, SEQ)
        signal(barrier, b, peer)
        signal(barrier, partner, peer)


def greeted():
    pl.semaphore_wait(pltpu.get_barrier_semaphore(), GROUPS - 1 + 2 * (SEQ - 1))


def wait_all(copies):
    for copy in copies:
        copy.wait()


def layer_kernel(
    feats, item_weight, send_rows, event_slot, user_blocks, tail_len, block_order, gain_in, gain_mid,
    w_in_hbm, w_out_hbm, cot_hbm, layer_out, d_item_out, *scratch,
):
    (
        w_in, w_out, cot, out1, in1, out2, in2, kv, q, p, ids, ids_in, kv_in, kv_events, q_in, p_in, tables_vmem, tables,
        spans, products, kv_products, stats, mixed_of, mixed_sorted, dq_sorted, mixed_slots, dq_slots, mixed_home,
        dq_home, d_mixed, d_mixed_t, query_t, own, give, part, summed, dkv_home, pre, d_pre, gate_of, d_gated_of, normal_of,
        inverse_of, back2, home2, back1, home1,
    ) = scratch[:47]
    (
        load_sem, table_sem, send1, recv1, send2, recv2, kv_send, kv_recv, pass_send, pass_recv, q_send, q_recv, p_send,
        p_recv, ids_send, ids_recv, stats_send, stats_recv, mixed_send, mixed_recv, dq_send, dq_recv, part_send,
        part_recv, dkv_send, dkv_recv, back2_send, back2_recv, back1_send, back1_recv,
    ) = scratch[47:]
    b, s, x, c, y, z = place()
    partner = x * 2 + 1 - c
    half = y % 2
    to_batch = x * 2 + y // 2
    me = z + 4 * half + 8 * c
    greet(b, s, partner)
    loads = [
        pltpu.make_async_copy(src, dst, load_sem.at[k])
        for k, (src, dst) in enumerate(((w_out_hbm, w_out), (cot_hbm, cot), (w_in_hbm, w_in)))
    ]
    for load in loads:
        load.start()

    embedded = silu(dot_nn(feats[...], item_weight[...])).astype(BF16)
    wanted = (iota((256, 256), 0) == send_rows[...]).astype(BF16)
    out1[...] = dot_tn(wanted, embedded).astype(BF16)
    slot_of_event = slot_rows(event_slot[...].reshape(1, ROWS))
    ids[...] = jnp.zeros_like(ids)
    for k in range(3):
        ids[k : k + 1, :] = slot_of_event[:, k * BLOCK : (k + 1) * BLOCK]
    ids[3:4, 0:BLOCKS] = block_order[...]
    ids[4:5, 0:4] = user_blocks[...]
    ids[5:6, 0:4] = tail_len[...]
    greeted()
    first = exchange_batch(out1, in1, send1, recv1, b, s)

    def each_worker(act):
        @pl.loop(0, SEQ)
        def _(i):
            w = lax.rem(i + s, SEQ)
            head, half, core, to_batch, to_seq = worker_at(w, x, c)
            here = (to_batch == b) & (to_seq == s)
            act(w, head, half, core, to_batch, to_seq, here)

    def start(here, src, dst, recv, remote):
        @pl.when(here)
        def _():
            pltpu.make_async_copy(src, dst, recv).start()

        @pl.when(jnp.logical_not(here))
        def _():
            remote.start()

    def ids_copy(w, to_batch, to_seq):
        return copy_to(ids, ids_in.at[s], ids_send.at[w], ids_recv.at[s], to_batch, to_seq)

    def start_ids(w, head, half, core, to_batch, to_seq, here):
        start(here, ids, ids_in.at[s], ids_recv.at[s], ids_copy(w, to_batch, to_seq))

    each_worker(start_ids)

    loads[0].wait()
    loads[1].wait()
    d_gated_of[...] = dot_nt(cot[...], w_out[...]).astype(BF16)
    wait_all(first)
    out2[...] = dot_nn(by_seq(), in1[...]).astype(BF16)
    second = exchange_seq(out2, in2, send2, recv2, b, s)
    onehot = slot_onehot(slot_of_event)
    loads[2].wait()
    wait_all(second)
    normal, inverse = normalize(in2[...].astype(F32))
    normal_of[...] = normal
    inverse_of[...] = jnp.broadcast_to(inverse, (SLOTS, 128))
    normed = (normal * gain_in[...]).astype(BF16)

    def project(first_column):
        cols = slice(first_column, first_column + WIDTH)
        made = dot_nn(normed, w_in[:, cols])
        pre[:, cols] = made
        return silu(made)

    for side, first_column in ((0, 1536), (1, 512)):
        lanes = slice(side * HEAD, side * HEAD + HEAD)
        made = project(first_column).astype(BF16)
        for h in range(HEADS):
            kv[h, 0, :, lanes] = made[:HALF, h * HEAD : (h + 1) * HEAD]
            kv[h, 1, :, lanes] = made[HALF:, h * HEAD : (h + 1) * HEAD]

    def kv_copy(w, head, core, to_batch, to_seq):
        return copy_to(kv.at[head, core], kv_in.at[s, core], kv_send.at[w], kv_recv.at[s], to_batch, to_seq)

    def start_kv(w, head, half, core, to_batch, to_seq, here):
        start(
            here, kv.at[head, core], kv_in.at[s, core], kv_recv.at[s], kv_copy(w, head, core, to_batch, to_seq)
        )

    each_worker(start_kv)

    query = (project(1024) * (0.5 * SCALE)).astype(BF16)
    query = dot_tn(onehot, query).astype(BF16)
    for h in range(HEADS):
        q[h] = query[:, h * HEAD : (h + 1) * HEAD].reshape(3, 4, PIECE, HEAD)

    def piece_copy(src, dst, send, recv, w, head, half, core, to_batch, to_seq):
        three = pl.ds(s * 3, 3)
        return copy_to(
            src.at[head, :, half * 2 + core], dst.at[three], send.at[w], recv.at[s], to_batch, to_seq
        )

    def start_piece(src, dst, send, recv):
        def act(w, head, half, core, to_batch, to_seq, here):
            start(
                here, src.at[head, :, half * 2 + core], dst.at[pl.ds(s * 3, 3)], recv.at[s],
                piece_copy(src, dst, send, recv, w, head, half, core, to_batch, to_seq),
            )

        each_worker(act)

    start_piece(q, q_in, q_send, q_recv)
    gate = dot_tn(onehot, project(0).astype(BF16))
    gate_of[...] = gate
    upstream = (d_gated_of[...].astype(F32) * gate * gain_mid[...]).astype(BF16)
    for h in range(HEADS):
        p[h] = upstream[:, h * HEAD : (h + 1) * HEAD].reshape(3, 4, PIECE, HEAD)
    start_piece(p, p_in, p_send, p_recv)

    @pl.loop(0, SEQ)
    def _(source):
        arrived(ids_in.at[source], ids_recv.at[source])

    tables_vmem[...] = tables_of(ids_in[s], half * 2 + c)
    table_copy = pltpu.make_async_copy(tables_vmem, tables, table_sem)
    table_copy.start()

    def pass_on(source):
        return copy_to(
            kv_in.at[source, c], kv_in.at[source, c], pass_send.at[source], pass_recv.at[source], partner, s
        )

    @pl.loop(0, SEQ + 2)
    def _(i):
        @pl.when(i < SEQ)
        def _():
            source = lax.rem(s - i + SEQ, SEQ)
            arrived(kv_in.at[source, c], kv_recv.at[source])
            pass_on(source).start()

        @pl.when(i >= 2)
        def _():
            source = lax.rem(s - i + 2 + SEQ, SEQ)
            arrived(kv_in.at[source, 1 - c], pass_recv.at[source])
            rows = jnp.concatenate([ids_in[source].astype(F32), jnp.zeros((120, 128), F32)], axis=0)
            columns = jnp.transpose(rows)
            lane = iota((BLOCK, SLOTS), 1).astype(F32)
            read = jnp.concatenate([(lane == columns[:, k : k + 1]).astype(BF16) for k in range(3)], axis=0)
            slots = kv_in[source].reshape(SLOTS, 2 * HEAD)
            made = dot_nn(read, slots).astype(BF16).reshape(3, BLOCK, 2 * HEAD)
            kv_events[pl.ds(source * 3, 3)] = made

    table_copy.wait()

    @pl.loop(0, SEQ)
    def _(source):
        arrived(q_in.at[pl.ds(source * 3, 3)], q_recv.at[source])

    def step(k, state):
        pairs, t, j = walk(tables, *state, AT_ONCE)
        keyvals = [four(kv_events, tables, j) for _, j in pairs]
        us = [dot_nt(four(q_in, tables, t), keyval[:, :HEAD]) for (t, _), keyval in zip(pairs, keyvals)]
        weights = []
        for (t_, j_), u in zip(pairs, us):
            w = u.astype(BF16) * (1.0 + jnp.tanh(u)).astype(BF16)
            weights.append(jnp.where(visible(tables, t_, j_), w, jnp.zeros_like(w)))
        for n, (w, keyval) in enumerate(zip(weights, keyvals)):
            products[k * AT_ONCE + n] = dot_nn(w, keyval[:, HEAD:])
        return t, j

    lax.fori_loop(0, MOST_PAIRS // AT_ONCE, step, (jnp.int32(0), jnp.int32(0)))

    @pl.loop(0, SEQ)
    def _(source):
        arrived(p_in.at[pl.ds(source * 3, 3)], p_recv.at[source])

    def sum_pairs(t, first, count):
        summed = products[jnp.minimum(first, MOST_PAIRS - 1)]
        for k in range(1, min(t + 1, MOST_CHUNKS)):
            more = products[jnp.minimum(first + k, MOST_PAIRS - 1)]
            summed = summed + jnp.where(k < count, more, jnp.zeros_like(more))
        return summed

    starts = []
    first_pair = jnp.int32(0)
    for t in range(TILES):
        count = t + 1 - tables[1, 4 * t] // 4
        starts.append((first_pair, count))
        spans[0, t] = first_pair
        spans[1, t] = tables[1, 4 * t] // 4
        mixed = sum_pairs(t, first_pair, count)
        first_pair = first_pair + count
        upstream = four(p_in, tables, t).astype(F32)
        mixed_of[t] = mixed
        mixed_sorted[4 * t : 4 * t + 4] = mixed.astype(BF16).reshape(4, PIECE, HEAD)
        mean = jnp.mean(mixed, axis=1, keepdims=True)
        centred = mixed - mean
        sums = pick4(
            iota((BLOCK, HEAD), 1) & 3,
            [
                mean,
                jnp.sum(centred * centred, axis=1, keepdims=True),
                jnp.sum(upstream, axis=1, keepdims=True),
                jnp.sum(upstream * centred, axis=1, keepdims=True),
            ],
        )
        rows = slice(4 * (t % 2), 4 * (t % 2) + 4)
        stats[z, t // 2, rows, :] = jnp.transpose(sums)[rows, :]

    copies = []
    for k in range(1, HEADS):
        peer = lax.rem(z + k, HEADS)
        copy = copy_to(stats.at[z], stats.at[z], stats_send.at[k], stats_recv.at[k], b, y * 4 + peer)
        copy.start()
        copies.append(copy)

    def is_here(source):
        return (to_batch == b) & (source == s)

    def home_copy(src, dst, send, recv, source):
        three = pl.ds(source * 3, 3)
        return copy_to(
            src.at[three], dst.at[z, :, half * 2 + c], send.at[source], recv.at[me], to_batch, source
        )

    def send_home(src, dst, send, recv):
        @pl.loop(0, SEQ)
        def _(i):
            source = lax.rem(i + s, SEQ)
            start(
                is_here(source), src.at[pl.ds(source * 3, 3)], dst.at[z, :, half * 2 + c], recv.at[me],
                home_copy(src, dst, send, recv, source),
            )

    @pl.loop(0, BLOCKS, unroll=4)
    def _(i):
        mixed_slots[i] = mixed_sorted[tables[4, i]]

    send_home(mixed_slots, mixed_home, mixed_send, mixed_recv)

    d_mixed[TILES] = jnp.zeros((BLOCK, HEAD), BF16)
    d_mixed_t[TILES] = jnp.zeros((HEAD, BLOCK), BF16)
    query_t[TILES] = jnp.zeros((HEAD, BLOCK), BF16)
    for t in range(TILES):
        query_t[t] = jnp.transpose(four(q_in, tables, t))
    wait_all(copies)
    for t in range(TILES):
        rows = slice(4 * (t % 2), 4 * (t % 2) + 4)
        of = [stats[h, t // 2, rows, :] for h in range(HEADS)]
        mean = sum(v[0:1] for v in of) * 0.25
        spread = sum(v[1:2] + HEAD * (v[0:1] - mean) * (v[0:1] - mean) for v in of) * (1.0 / WIDTH)
        inverse = lax.rsqrt(spread + 1e-05)
        slant = sum(v[2:3] for v in of) * (1.0 / WIDTH)
        along = sum(v[3:4] + v[2:3] * (v[0:1] - mean) for v in of) * (1.0 / WIDTH) * inverse
        columns = jnp.transpose(pick4(iota((BLOCK, HEAD), 0), [mean, inverse, slant, along]))
        mean, inverse, slant, along = (columns[:, i : i + 1] for i in range(4))
        made = (mixed_of[t] - mean) * inverse
        made = (inverse * (four(p_in, tables, t).astype(F32) - slant - made * along)).astype(BF16)
        d_mixed[t] = made
        d_mixed_t[t] = jnp.transpose(made)

    def back_step(k, state):
        pairs, t, j = walk(tables, *state, BACK_AT_ONCE)
        keyvals = [four(kv_events, tables, j) for _, j in pairs]
        us = [dot_nt(four(q_in, tables, t), keyval[:, :HEAD]) for (t, _), keyval in zip(pairs, keyvals)]
        d_weights = [dot_nt(d_mixed[t], keyval[:, HEAD:]) for (t, _), keyval in zip(pairs, keyvals)]
        made = []
        for (t_, j_), u, dw in zip(pairs, us, d_weights):
            th = jnp.tanh(u)
            a = (1.0 + th).astype(BF16)
            w = u.astype(BF16) * a
            ds = dw.astype(BF16) * (a + w * (1.0 - th).astype(BF16))
            seen = visible(tables, t_, j_)
            made.append((jnp.where(seen, w, jnp.zeros_like(w)), jnp.where(seen, ds, jnp.zeros_like(ds))))
        for n, ((t_, _), keyval, (w, ds)) in enumerate(zip(pairs, keyvals, made)):
            pair = k * BACK_AT_ONCE + n
            d_key = dot_nn(query_t[t_], ds).astype(BF16)
            d_value = dot_nn(d_mixed_t[t_], w).astype(BF16)
            for i in range(4):
                kv_products[pair, i, 0:HEAD] = d_key[:, i * BLOCK : (i + 1) * BLOCK]
                kv_products[pair, i, HEAD : 2 * HEAD] = d_value[:, i * BLOCK : (i + 1) * BLOCK]
            products[pair] = dot_nn(ds, keyval[:, :HEAD])
        return t, j

    lax.fori_loop(0, MOST_PAIRS // BACK_AT_ONCE, back_step, (jnp.int32(0), jnp.int32(0)))

    for t in range(TILES):
        dq = (sum_pairs(t, *starts[t]) * (0.5 * SCALE)).astype(BF16)
        dq_sorted[4 * t : 4 * t + 4] = dq.reshape(4, PIECE, HEAD)

    @pl.loop(0, BLOCKS, unroll=4)
    def _(i):
        dq_slots[i] = dq_sorted[tables[4, i]]

    send_home(dq_slots, dq_home, dq_send, dq_recv)

    def block_grad(n):
        j = n // 4
        total = jnp.zeros((2 * HEAD, BLOCK), F32)
        for k in range(MOST_CHUNKS):
            t = jnp.minimum(j + k, TILES - 1)
            since = spans[1, t]
            pair = jnp.clip(spans[0, t] + j - since, 0, MOST_PAIRS - 1)
            more = kv_products[pair, n % 4].astype(F32)
            total += jnp.where((j + k < TILES) & (since <= j), more, jnp.zeros_like(more))
        return total.astype(BF16)

    def part_copy(source):
        return copy_to(
            give.at[source], part.at[source], part_send.at[source], part_recv.at[source], partner, s
        )

    def dkv_copy(source):
        return copy_to(
            summed.at[source], dkv_home.at[z, half, c], dkv_send.at[source], dkv_recv.at[me], to_batch, source
        )

    @pl.loop(0, SEQ + 2)
    def _(i):
        @pl.when(i < SEQ)
        def _():
            source = lax.rem(s + i, SEQ)
            wanted = jnp.concatenate([ids_in[source, m : m + 1, :] for m in range(3)], axis=1)
            grads = jnp.concatenate([block_grad(tables[4, source * 3 + m]) for m in range(3)], axis=1)
            made = dot_nt(slot_onehot(wanted), grads).astype(BF16)
            own[source] = jnp.where(c == 0, made[:HALF], made[HALF:])
            give[source] = jnp.where(c == 0, made[HALF:], made[:HALF])
            part_copy(source).start()

        @pl.when(i >= 2)
        def _():
            source = lax.rem(s + i - 2, SEQ)
            arrived(part.at[source], part_recv.at[source])
            summed[source] = (own[source].astype(F32) + part[source].astype(F32)).astype(BF16)
            start(
                is_here(source), summed.at[source], dkv_home.at[z, half, c], dkv_recv.at[me], dkv_copy(source)
            )

    tokens = dot_tn(onehot, in2[...])
    slot_cot = dot_nn(onehot, cot[...])
    item_slope = silu_slope(dot_nn(feats[...], item_weight[...]))
    for first_column in range(0, 4 * WIDTH, WIDTH):
        cols = slice(first_column, first_column + WIDTH)
        pre[:, cols] = silu_slope(pre[:, cols])

    @pl.loop(0, SEQ)
    def _(w):
        arrived(mixed_home.at[w % 4, :, ((w // 4) % 2) * 2 + w // 8], mixed_recv.at[w])

    mixed = jnp.concatenate([mixed_home[h].reshape(ROWS, HEAD) for h in range(HEADS)], axis=1)
    normed_mid = normalize(mixed.astype(F32))[0] * gain_mid[...]
    gated = (normed_mid * gate_of[...]).astype(BF16)
    layer_out[...] = (tokens + dot_nn(gated, w_out[...])).astype(BF16)
    d_gate = dot_nn(onehot, (d_gated_of[...].astype(F32) * normed_mid).astype(BF16))
    d_pre[...] = (d_gate * pre[:, 0:WIDTH]).astype(BF16)
    d_normed = dot_nt(d_pre[...], w_in[:, 0:WIDTH])

    @pl.loop(0, SEQ)
    def _(w):
        arrived(dq_home.at[w % 4, :, ((w // 4) % 2) * 2 + w // 8], dq_recv.at[w])

    d_query = jnp.concatenate([dq_home[h].reshape(ROWS, HEAD) for h in range(HEADS)], axis=1)
    d_pre[...] = (dot_nn(onehot, d_query) * pre[:, 1024:1536]).astype(BF16)
    d_normed += dot_nt(d_pre[...], w_in[:, 1024:1536])

    @pl.loop(0, SEQ)
    def _(w):
        arrived(dkv_home.at[w % 4, (w // 4) % 2, w // 8], dkv_recv.at[w])

    for lanes, first_column in ((0, 1536), (HEAD, 512)):
        cols = slice(first_column, first_column + WIDTH)
        grad = jnp.concatenate(
            [
                dkv_home[h, 0, :, :, lanes : lanes + HEAD].reshape(SLOTS, HEAD).astype(F32)
                + dkv_home[h, 1, :, :, lanes : lanes + HEAD].reshape(SLOTS, HEAD).astype(F32)
                for h in range(HEADS)
            ],
            axis=1,
        )
        d_pre[...] = (grad * pre[:, cols]).astype(BF16)
        d_normed += dot_nt(d_pre[...], w_in[:, cols])

    scaled = d_normed * gain_in[...]
    normal = normal_of[...]
    d_slots = slot_cot + inverse_of[:, 0:1] * (
        scaled
        - jnp.mean(scaled, axis=-1, keepdims=True)
        - normal * jnp.mean(scaled * normal, axis=-1, keepdims=True)
    )
    back2[...] = d_slots.astype(BF16)
    wait_all(exchange_seq(back2, home2, back2_send, back2_recv, b, s))
    back1[...] = dot_nn(by_batch(), home2[...]).astype(BF16)
    last = exchange_batch(back1, home1, back1_send, back1_recv, b, s)
    wanted = (iota((256, 256), 0) == send_rows[...]).astype(BF16)
    wait_all(last)
    d_embedded = dot_nn(wanted, home1[...])
    d_item_out[...] = (d_embedded * item_slope).astype(BF16)

    def finish(w, head, half, core, to_batch, to_seq, here):
        @pl.when(jnp.logical_not(here))
        def _():
            ids_copy(w, to_batch, to_seq).wait_send()
            kv_copy(w, head, core, to_batch, to_seq).wait_send()
            piece_copy(q, q_in, q_send, q_recv, w, head, half, core, to_batch, to_seq).wait_send()
            piece_copy(p, p_in, p_send, p_recv, w, head, half, core, to_batch, to_seq).wait_send()

    each_worker(finish)

    @pl.loop(0, SEQ)
    def _(source):
        pass_on(source).wait_send()
        part_copy(source).wait_send()

        @pl.when(jnp.logical_not(is_here(source)))
        def _():
            home_copy(mixed_slots, mixed_home, mixed_send, mixed_recv, source).wait_send()
            home_copy(dq_slots, dq_home, dq_send, dq_recv, source).wait_send()
            dkv_copy(source).wait_send()


def tables_of(meta, quarter):
    slot, lane = iota((128, 128), 0), iota((1, 128), 1)
    held = jnp.transpose(jnp.broadcast_to(meta[3:4, :], (128, 128)))
    slot_of = jnp.where((held == iota((128, 128), 1)) & (slot < BLOCKS), slot, 0)
    slot_of = jnp.minimum(jnp.sum(slot_of, axis=0, keepdims=True), BLOCKS - 1)
    first = jnp.zeros((1, 1), jnp.int32)
    start_of = jnp.zeros((1, 128), jnp.int32)
    limit_of = jnp.full((1, 128), BLOCK, jnp.int32)
    for u in range(4):
        start_of = jnp.where(lane >= first, first, start_of)
        first = first + meta[4:5, u : u + 1]
        limit_of = jnp.where(lane == first - 1, meta[5:6, u : u + 1], limit_of)
    start_of = jnp.where(lane < BLOCKS, start_of, NO_BLOCK)
    row = iota((8, 128), 0)
    picked = pick4(row, [slot_of, start_of, limit_of, jnp.zeros((1, 128), jnp.int32) + quarter])
    return jnp.where(row == 4, meta[3:4, :], picked)


def pick4(index, values):
    return jnp.where(index == 0, values[0], jnp.where(index == 1, values[1], jnp.where(index == 2, values[2], values[3])))


def first_chunk(meta, t):
    return jnp.clip(meta[1, 4 * t] // 4, 0, TILES - 1)


def walk(meta, t, j, count):
    pairs = []
    for _ in range(count):
        pairs.append((t, j))
        more = j < jnp.minimum(t, TILES - 1)
        after = jnp.minimum(t + 1, TILES)
        j = jnp.where(more, j + 1, first_chunk(meta, after))
        t = jnp.where(more, t, after)
    return pairs, t, j


def pairs_in_all(meta):
    return sum(t + 1 - meta[1, 4 * t] // 4 for t in range(TILES))


def four(ref, meta, n):
    return jnp.concatenate([ref[meta[0, 4 * n + i]] for i in range(4)], axis=0)


def visible(meta, t, j):
    r, lane = iota((BLOCK, 1), 0), iota((1, BLOCK), 1)
    at = (t * 4 + (r >> 5)) * BLOCK + meta[3, 0] * PIECE + (r & 31)
    since = pick4(r >> 5, [meta[1, t * 4 + i] for i in range(4)]) * BLOCK
    where = jnp.concatenate(
        [jnp.where(lane < meta[2, j * 4 + i], (j * 4 + i) * BLOCK + lane, FAR) for i in range(4)], axis=1
    )
    where, at, since = (v.astype(jnp.int16) for v in (where, at, since))
    return (where <= at) & (where >= since)


def result_kernel(layer, d_item, item_weight, layer_out, item_grad):
    layer_out[...] = layer[...]
    item_grad[...] = dot_nt(d_item[...], item_weight[...])


def spec(space):
    return pl.BlockSpec(memory_space=space)


VMEM, SMEM, ANY = pltpu.VMEM, pltpu.SMEM, pl.ANY
DMA = pltpu.SemaphoreType.DMA


def shape(dims, dtype):
    return jax.ShapeDtypeStruct(dims, dtype)


def params(remote=None):
    return pltpu.CompilerParams(
        vmem_limit_bytes=56 << 20, has_side_effects=remote is not None, collective_id=remote
    )


def per_device(
    item_feats, item_weight, send_rows, event_slot, user_blocks, tail_len, block_order, gain_in, gain_mid, w_in, w_out,
    cot_out,
):
    gain_in, gain_mid = gain_in.reshape(1, WIDTH), gain_mid.reshape(1, WIDTH)
    wide = VMEM((256, WIDTH), BF16)
    pieces = VMEM((BLOCKS, PIECE, HEAD), BF16)
    by_head = VMEM((HEADS, 3, 4, PIECE, HEAD), BF16)
    tiles = VMEM((TILES + 1, BLOCK, HEAD), BF16)
    each, one = DMA((SEQ,)), DMA((GROUPS,))
    layer, d_item = pl.pallas_call(
        layer_kernel,
        out_shape=(shape((ROWS, WIDTH), BF16), shape((256, WIDTH), BF16)),
        in_specs=[spec(VMEM)] * 9 + [spec(ANY)] * 3,
        out_specs=(spec(VMEM), spec(VMEM)),
        scratch_shapes=[
            VMEM((WIDTH, 4 * WIDTH), BF16),
            VMEM((WIDTH, WIDTH), BF16),
            VMEM((ROWS, WIDTH), BF16),
            wide,
            wide,
            wide,
            wide,
            VMEM((HEADS, 2, HALF, 2 * HEAD), BF16),
            by_head,
            by_head,
            VMEM((8, 128), jnp.int32),
            VMEM((SEQ, 8, 128), jnp.int32),
            VMEM((SEQ, 2, HALF, 2 * HEAD), BF16),
            VMEM((BLOCKS, BLOCK, 2 * HEAD), BF16),
            pieces,
            pieces,
            VMEM((8, 128), jnp.int32),
            SMEM((8, 128), jnp.int32),
            SMEM((2, 16), jnp.int32),
            VMEM((MOST_PAIRS, BLOCK, HEAD), F32),
            VMEM((MOST_PAIRS, 4, 2 * HEAD, BLOCK), BF16),
            VMEM((HEADS, TILES // 2, 8, BLOCK), F32),
            VMEM((TILES, BLOCK, HEAD), F32),
            pieces,
            pieces,
            pieces,
            pieces,
            by_head,
            by_head,
            tiles,
            tiles,
            tiles,
            VMEM((SEQ, HALF, 2 * HEAD), BF16),
            VMEM((SEQ, HALF, 2 * HEAD), BF16),
            VMEM((SEQ, HALF, 2 * HEAD), BF16),
            VMEM((SEQ, HALF, 2 * HEAD), BF16),
            VMEM((HEADS, 2, 2, HALF, 2 * HEAD), BF16),
            VMEM((SLOTS, 4 * WIDTH), F32),
            VMEM((SLOTS, WIDTH), BF16),
            VMEM((ROWS, WIDTH), F32),
            VMEM((ROWS, WIDTH), BF16),
            VMEM((SLOTS, WIDTH), F32),
            VMEM((SLOTS, 128), F32),
            wide,
            wide,
            wide,
            wide,
            DMA((3,)),
            DMA,
            one,
            one,
            *([each] * 12),
            DMA((HEADS,)),
            DMA((HEADS,)),
            *([each] * 4),
            *([each] * 6),
            one,
            one,
        ],
        compiler_params=params(0),
        name="layer",
    )(
        item_feats, item_weight, send_rows, event_slot, user_blocks, tail_len, block_order, gain_in, gain_mid, w_in,
        w_out, cot_out,
    )
    return pl.pallas_call(
        result_kernel,
        out_shape=(shape((ROWS, WIDTH), BF16), shape((256, WIDTH), F32)),
        in_specs=[spec(VMEM)] * 3,
        out_specs=(spec(VMEM), spec(VMEM)),
        compiler_params=params(),
        name="results",
    )(layer, d_item, item_weight)


def solution(mesh):
    rows = P(("batch", "seq"), None)
    return jax.shard_map(
        per_device,
        mesh=mesh,
        in_specs=(
            rows,
            P(),
            rows,
            P(("batch", "seq")),
            P("batch", None),
            P("batch", None),
            P("batch", None),
            P(),
            P(),
            P(),
            P(),
            rows,
        ),
        out_specs=(rows, rows),
        check_vma=False,
    )
```

```python
import jax
import jax.numpy as jnp
from jax import lax
from jax.experimental import pallas as pl
from jax.experimental.pallas import tpu as pltpu
from jax.sharding import PartitionSpec as P

WIDTH = 512
HEAD = 128
HEADS = 4
BLOCK = 128
BLOCKS = 48
SEQ = 16
GROUPS = 8
PIECE = 32
TILES = 12
SLOTS = 256
HALF = 128
ROWS = 384
FAR = 30000
NO_BLOCK = 200
AT_ONCE = 6
MOST_PAIRS = 48
MOST_CHUNKS = 7
BACK_AT_ONCE = 6
SCALE = HEAD**-0.5
MESH = pl.DeviceIdType.MESH
F32 = jnp.float32
BF16 = jnp.bfloat16


def dot_nn(a, b):
    return jnp.dot(a, b, preferred_element_type=F32)


def dot_nt(a, b):
    return lax.dot_general(a, b, (((1,), (1,)), ((), ())), preferred_element_type=F32)


def dot_tn(a, b):
    return lax.dot_general(a, b, (((0,), (0,)), ((), ())), preferred_element_type=F32)


def silu(v):
    u = 0.5 * v
    return u + u * jnp.tanh(u)


def silu_slope(v):
    u = 0.5 * v
    t = jnp.tanh(u)
    a = 1.0 + t
    return 0.5 * (a + u * a * (1.0 - t))


def normalize(values):
    mean = jnp.mean(values, axis=-1, keepdims=True)
    centred = values - mean
    spread = jnp.mean(centred * centred, axis=-1, keepdims=True)
    inverse = lax.rsqrt(spread + 1e-05)
    return centred * inverse, inverse


def iota(shape, dim):
    return lax.broadcasted_iota(jnp.int32, shape, dim)


def place():
    b, s = lax.axis_index("batch"), lax.axis_index("seq")
    return b, s, b // 2, b % 2, s // 4, s % 4


def worker_at(w, x, c):
    head, half, core = w % 4, (w // 4) % 2, w // 8
    return head, half, core, x * 2 + core, (2 * c + half) * 4 + head


def copy_to(src, dst, send, recv, batch, seq):
    return pltpu.make_async_remote_copy(
        src_ref=src, dst_ref=dst, send_sem=send, recv_sem=recv, device_id=(batch, seq), device_id_type=MESH
    )


def arrived(ref, sem):
    pltpu.make_async_copy(ref, ref, sem).wait()


def rows_of(index, size):
    return pl.ds(pl.multiple_of(index * size, size), size)


def slot_rows(event_slot):
    e = event_slot
    return ((e >> 1) & 15) * 16 + (e >> 5) * 2 + (e & 1)


def slot_onehot(wanted):
    return (iota((SLOTS, wanted.shape[1]), 0) == wanted).astype(BF16)


def by_seq():
    i, j = iota((256, 256), 0), iota((256, 256), 1)
    return (j == ((i >> 1) & 7) * 32 + (i >> 4) * 2 + (i & 1)).astype(BF16)


def by_batch():
    i, j = iota((256, 256), 0), iota((256, 256), 1)
    return (j == ((i >> 1) & 15) * 16 + (i >> 5) * 2 + (i & 1)).astype(BF16)


def exchange_batch(src, dst, send, recv, b, s):
    copies = []
    for k in range(1, GROUPS):
        peer = lax.rem(b + k, GROUPS)
        copy = copy_to(src.at[rows_of(peer, 32)], dst.at[rows_of(b, 32)], send.at[k], recv.at[k], peer, s)
        copy.start()
        copies.append(copy)
    dst[rows_of(b, 32), :] = src[rows_of(b, 32), :]
    return copies


def exchange_seq(src, dst, send, recv, b, s):
    copies = []
    for k in range(1, SEQ):
        peer = lax.rem(s + k, SEQ)
        copy = copy_to(src.at[rows_of(peer, 16)], dst.at[rows_of(s, 16)], send.at[k], recv.at[k], b, peer)
        copy.start()
        copies.append(copy)
    dst[rows_of(s, 16), :] = src[rows_of(s, 16), :]
    return copies


def signal(barrier, batch, seq):
    pl.semaphore_signal(barrier, inc=1, device_id=(batch, seq), device_id_type=MESH)


def greet(b, s, partner):
    barrier = pltpu.get_barrier_semaphore()
    for k in range(1, GROUPS):
        signal(barrier, lax.rem(b + k, GROUPS), s)

    @pl.loop(1, SEQ)
    def _(k):
        peer = lax.rem(s + k, SEQ)
        signal(barrier, b, peer)
        signal(barrier, partner, peer)


def greeted():
    pl.semaphore_wait(pltpu.get_barrier_semaphore(), GROUPS - 1 + 2 * (SEQ - 1))


def wait_all(copies):
    for copy in copies:
        copy.wait()


def layer_kernel(
    feats, item_weight, send_rows, event_slot, user_blocks, tail_len, block_order, gain_in, gain_mid,
    w_in_hbm, w_out_hbm, cot_hbm, layer_out, d_item_out, *scratch,
):
    (
        w_in, w_out, cot, out1, in1, out2, in2, kv, q, p, ids, ids_in, kv_in, kv_events, q_in, p_in, tables_vmem, tables,
        spans, products, kv_products, stats, mixed_of, mixed_sorted, dq_sorted, mixed_slots, dq_slots, mixed_home,
        dq_home, d_mixed, d_mixed_t, query_t, own, give, part, summed, dkv_home, pre, d_pre, gate_of, d_gated_of, normal_of,
        inverse_of, back2, home2, back1, home1,
    ) = scratch[:47]
    (
        load_sem, table_sem, send1, recv1, send2, recv2, kv_send, kv_recv, pass_send, pass_recv, q_send, q_recv, p_send,
        p_recv, ids_send, ids_recv, stats_send, stats_recv, mixed_send, mixed_recv, dq_send, dq_recv, part_send,
        part_recv, dkv_send, dkv_recv, back2_send, back2_recv, back1_send, back1_recv,
    ) = scratch[47:]
    b, s, x, c, y, z = place()
    partner = x * 2 + 1 - c
    half = y % 2
    to_batch = x * 2 + y // 2
    me = z + 4 * half + 8 * c
    greet(b, s, partner)
    loads = [
        pltpu.make_async_copy(src, dst, load_sem.at[k])
        for k, (src, dst) in enumerate(((w_out_hbm, w_out), (cot_hbm, cot), (w_in_hbm, w_in)))
    ]
    for load in loads:
        load.start()

    embedded = silu(dot_nn(feats[...], item_weight[...])).astype(BF16)
    wanted = (iota((256, 256), 0) == send_rows[...]).astype(BF16)
    out1[...] = dot_tn(wanted, embedded).astype(BF16)
    slot_of_event = slot_rows(event_slot[...].reshape(1, ROWS))
    ids[...] = jnp.zeros_like(ids)
    for k in range(3):
        ids[k : k + 1, :] = slot_of_event[:, k * BLOCK : (k + 1) * BLOCK]
    ids[3:4, 0:BLOCKS] = block_order[...]
    ids[4:5, 0:4] = user_blocks[...]
    ids[5:6, 0:4] = tail_len[...]
    greeted()
    first = exchange_batch(out1, in1, send1, recv1, b, s)

    def each_worker(act):
        @pl.loop(0, SEQ)
        def _(i):
            w = lax.rem(i + s, SEQ)
            head, half, core, to_batch, to_seq = worker_at(w, x, c)
            here = (to_batch == b) & (to_seq == s)
            act(w, head, half, core, to_batch, to_seq, here)

    def start(here, src, dst, recv, remote):
        @pl.when(here)
        def _():
            pltpu.make_async_copy(src, dst, recv).start()

        @pl.when(jnp.logical_not(here))
        def _():
            remote.start()

    def ids_copy(w, to_batch, to_seq):
        return copy_to(ids, ids_in.at[s], ids_send.at[w], ids_recv.at[s], to_batch, to_seq)

    def start_ids(w, head, half, core, to_batch, to_seq, here):
        start(here, ids, ids_in.at[s], ids_recv.at[s], ids_copy(w, to_batch, to_seq))

    each_worker(start_ids)

    loads[0].wait()
    loads[1].wait()
    d_gated_of[...] = dot_nt(cot[...], w_out[...]).astype(BF16)
    wait_all(first)
    out2[...] = dot_nn(by_seq(), in1[...]).astype(BF16)
    second = exchange_seq(out2, in2, send2, recv2, b, s)
    onehot = slot_onehot(slot_of_event)
    loads[2].wait()
    wait_all(second)
    normal, inverse = normalize(in2[...].astype(F32))
    normal_of[...] = normal
    inverse_of[...] = jnp.broadcast_to(inverse, (SLOTS, 128))
    normed = (normal * gain_in[...]).astype(BF16)

    def project(first_column):
        cols = slice(first_column, first_column + WIDTH)
        made = dot_nn(normed, w_in[:, cols])
        pre[:, cols] = made
        return silu(made)

    for side, first_column in ((0, 1536), (1, 512)):
        lanes = slice(side * HEAD, side * HEAD + HEAD)
        made = project(first_column).astype(BF16)
        for h in range(HEADS):
            kv[h, 0, :, lanes] = made[:HALF, h * HEAD : (h + 1) * HEAD]
            kv[h, 1, :, lanes] = made[HALF:, h * HEAD : (h + 1) * HEAD]

    def kv_copy(w, head, core, to_batch, to_seq):
        return copy_to(kv.at[head, core], kv_in.at[s, core], kv_send.at[w], kv_recv.at[s], to_batch, to_seq)

    def start_kv(w, head, half, core, to_batch, to_seq, here):
        start(
            here, kv.at[head, core], kv_in.at[s, core], kv_recv.at[s], kv_copy(w, head, core, to_batch, to_seq)
        )

    each_worker(start_kv)

    query = (project(1024) * (0.5 * SCALE)).astype(BF16)
    query = dot_tn(onehot, query).astype(BF16)
    for h in range(HEADS):
        q[h] = query[:, h * HEAD : (h + 1) * HEAD].reshape(3, 4, PIECE, HEAD)

    def piece_copy(src, dst, send, recv, w, head, half, core, to_batch, to_seq):
        three = pl.ds(s * 3, 3)
        return copy_to(
            src.at[head, :, half * 2 + core], dst.at[three], send.at[w], recv.at[s], to_batch, to_seq
        )

    def start_piece(src, dst, send, recv):
        def act(w, head, half, core, to_batch, to_seq, here):
            start(
                here, src.at[head, :, half * 2 + core], dst.at[pl.ds(s * 3, 3)], recv.at[s],
                piece_copy(src, dst, send, recv, w, head, half, core, to_batch, to_seq),
            )

        each_worker(act)

    start_piece(q, q_in, q_send, q_recv)
    gate = dot_tn(onehot, project(0).astype(BF16))
    gate_of[...] = gate
    upstream = (d_gated_of[...].astype(F32) * gate * gain_mid[...]).astype(BF16)
    for h in range(HEADS):
        p[h] = upstream[:, h * HEAD : (h + 1) * HEAD].reshape(3, 4, PIECE, HEAD)
    start_piece(p, p_in, p_send, p_recv)

    @pl.loop(0, SEQ)
    def _(source):
        arrived(ids_in.at[source], ids_recv.at[source])

    tables_vmem[...] = tables_of(ids_in[s], half * 2 + c)
    table_copy = pltpu.make_async_copy(tables_vmem, tables, table_sem)
    table_copy.start()

    def pass_on(source):
        return copy_to(
            kv_in.at[source, c], kv_in.at[source, c], pass_send.at[source], pass_recv.at[source], partner, s
        )

    @pl.loop(0, SEQ + 2)
    def _(i):
        @pl.when(i < SEQ)
        def _():
            source = lax.rem(s - i + SEQ, SEQ)
            arrived(kv_in.at[source, c], kv_recv.at[source])
            pass_on(source).start()

        @pl.when(i >= 2)
        def _():
            source = lax.rem(s - i + 2 + SEQ, SEQ)
            arrived(kv_in.at[source, 1 - c], pass_recv.at[source])
            rows = jnp.concatenate([ids_in[source].astype(F32), jnp.zeros((120, 128), F32)], axis=0)
            columns = jnp.transpose(rows)
            lane = iota((BLOCK, SLOTS), 1).astype(F32)
            read = jnp.concatenate([(lane == columns[:, k : k + 1]).astype(BF16) for k in range(3)], axis=0)
            slots = kv_in[source].reshape(SLOTS, 2 * HEAD)
            made = dot_nn(read, slots).astype(BF16).reshape(3, BLOCK, 2 * HEAD)
            kv_events[pl.ds(source * 3, 3)] = made

    table_copy.wait()

    @pl.loop(0, SEQ)
    def _(source):
        arrived(q_in.at[pl.ds(source * 3, 3)], q_recv.at[source])

    def step(k, state):
        pairs, t, j = walk(tables, *state, AT_ONCE)
        keyvals = [four(kv_events, tables, j) for _, j in pairs]
        us = [dot_nt(four(q_in, tables, t), keyval[:, :HEAD]) for (t, _), keyval in zip(pairs, keyvals)]
        weights = []
        for (t_, j_), u in zip(pairs, us):
            w = u.astype(BF16) * (1.0 + jnp.tanh(u)).astype(BF16)
            weights.append(jnp.where(visible(tables, t_, j_), w, jnp.zeros_like(w)))
        for n, (w, keyval) in enumerate(zip(weights, keyvals)):
            products[k * AT_ONCE + n] = dot_nn(w, keyval[:, HEAD:])
        return t, j

    lax.fori_loop(0, MOST_PAIRS // AT_ONCE, step, (jnp.int32(0), jnp.int32(0)))

    @pl.loop(0, SEQ)
    def _(source):
        arrived(p_in.at[pl.ds(source * 3, 3)], p_recv.at[source])

    def sum_pairs(t, first, count):
        summed = products[jnp.minimum(first, MOST_PAIRS - 1)]
        for k in range(1, min(t + 1, MOST_CHUNKS)):
            more = products[jnp.minimum(first + k, MOST_PAIRS - 1)]
            summed = summed + jnp.where(k < count, more, jnp.zeros_like(more))
        return summed

    starts = []
    first_pair = jnp.int32(0)
    for t in range(TILES):
        count = t + 1 - tables[1, 4 * t] // 4
        starts.append((first_pair, count))
        spans[0, t] = first_pair
        spans[1, t] = tables[1, 4 * t] // 4
        mixed = sum_pairs(t, first_pair, count)
        first_pair = first_pair + count
        upstream = four(p_in, tables, t).astype(F32)
        mixed_of[t] = mixed
        mixed_sorted[4 * t : 4 * t + 4] = mixed.astype(BF16).reshape(4, PIECE, HEAD)
        mean = jnp.mean(mixed, axis=1, keepdims=True)
        centred = mixed - mean
        sums = pick4(
            iota((BLOCK, HEAD), 1) & 3,
            [
                mean,
                jnp.sum(centred * centred, axis=1, keepdims=True),
                jnp.sum(upstream, axis=1, keepdims=True),
                jnp.sum(upstream * centred, axis=1, keepdims=True),
            ],
        )
        rows = slice(4 * (t % 2), 4 * (t % 2) + 4)
        stats[z, t // 2, rows, :] = jnp.transpose(sums)[rows, :]

    copies = []
    for k in range(1, HEADS):
        peer = lax.rem(z + k, HEADS)
        copy = copy_to(stats.at[z], stats.at[z], stats_send.at[k], stats_recv.at[k], b, y * 4 + peer)
        copy.start()
        copies.append(copy)

    def is_here(source):
        return (to_batch == b) & (source == s)

    def home_copy(src, dst, send, recv, source):
        three = pl.ds(source * 3, 3)
        return copy_to(
            src.at[three], dst.at[z, :, half * 2 + c], send.at[source], recv.at[me], to_batch, source
        )

    def send_home(src, dst, send, recv):
        @pl.loop(0, SEQ)
        def _(i):
            source = lax.rem(i + s, SEQ)
            start(
                is_here(source), src.at[pl.ds(source * 3, 3)], dst.at[z, :, half * 2 + c], recv.at[me],
                home_copy(src, dst, send, recv, source),
            )

    @pl.loop(0, BLOCKS, unroll=4)
    def _(i):
        mixed_slots[i] = mixed_sorted[tables[4, i]]

    d_mixed[TILES] = jnp.zeros((BLOCK, HEAD), BF16)
    d_mixed_t[TILES] = jnp.zeros((HEAD, BLOCK), BF16)
    query_t[TILES] = jnp.zeros((HEAD, BLOCK), BF16)
    for t in range(TILES):
        query_t[t] = jnp.transpose(four(q_in, tables, t))
    wait_all(copies)
    send_home(mixed_slots, mixed_home, mixed_send, mixed_recv)
    for t in range(TILES):
        rows = slice(4 * (t % 2), 4 * (t % 2) + 4)
        of = [stats[h, t // 2, rows, :] for h in range(HEADS)]
        mean = sum(v[0:1] for v in of) * 0.25
        spread = sum(v[1:2] + HEAD * (v[0:1] - mean) * (v[0:1] - mean) for v in of) * (1.0 / WIDTH)
        inverse = lax.rsqrt(spread + 1e-05)
        slant = sum(v[2:3] for v in of) * (1.0 / WIDTH)
        along = sum(v[3:4] + v[2:3] * (v[0:1] - mean) for v in of) * (1.0 / WIDTH) * inverse
        columns = jnp.transpose(pick4(iota((BLOCK, HEAD), 0), [mean, inverse, slant, along]))
        mean, inverse, slant, along = (columns[:, i : i + 1] for i in range(4))
        made = (mixed_of[t] - mean) * inverse
        made = (inverse * (four(p_in, tables, t).astype(F32) - slant - made * along)).astype(BF16)
        d_mixed[t] = made
        d_mixed_t[t] = jnp.transpose(made)

    def back_step(k, state):
        pairs, t, j = walk(tables, *state, BACK_AT_ONCE)
        keyvals = [four(kv_events, tables, j) for _, j in pairs]
        us = [dot_nt(four(q_in, tables, t), keyval[:, :HEAD]) for (t, _), keyval in zip(pairs, keyvals)]
        d_weights = [dot_nt(d_mixed[t], keyval[:, HEAD:]) for (t, _), keyval in zip(pairs, keyvals)]
        made = []
        for (t_, j_), u, dw in zip(pairs, us, d_weights):
            th = jnp.tanh(u)
            a = (1.0 + th).astype(BF16)
            w = u.astype(BF16) * a
            ds = dw.astype(BF16) * (a + w * (1.0 - th).astype(BF16))
            seen = visible(tables, t_, j_)
            made.append((jnp.where(seen, w, jnp.zeros_like(w)), jnp.where(seen, ds, jnp.zeros_like(ds))))
        for n, ((t_, _), keyval, (w, ds)) in enumerate(zip(pairs, keyvals, made)):
            pair = k * BACK_AT_ONCE + n
            d_key = dot_nn(query_t[t_], ds).astype(BF16)
            d_value = dot_nn(d_mixed_t[t_], w).astype(BF16)
            for i in range(4):
                kv_products[pair, i, 0:HEAD] = d_key[:, i * BLOCK : (i + 1) * BLOCK]
                kv_products[pair, i, HEAD : 2 * HEAD] = d_value[:, i * BLOCK : (i + 1) * BLOCK]
            products[pair] = dot_nn(ds, keyval[:, :HEAD])
        return t, j

    lax.fori_loop(0, MOST_PAIRS // BACK_AT_ONCE, back_step, (jnp.int32(0), jnp.int32(0)))

    for t in range(TILES):
        dq = (sum_pairs(t, *starts[t]) * (0.5 * SCALE)).astype(BF16)
        dq_sorted[4 * t : 4 * t + 4] = dq.reshape(4, PIECE, HEAD)

    @pl.loop(0, BLOCKS, unroll=4)
    def _(i):
        dq_slots[i] = dq_sorted[tables[4, i]]

    send_home(dq_slots, dq_home, dq_send, dq_recv)

    def block_grad(n):
        j = n // 4
        total = jnp.zeros((2 * HEAD, BLOCK), F32)
        for k in range(MOST_CHUNKS):
            t = jnp.minimum(j + k, TILES - 1)
            since = spans[1, t]
            pair = jnp.clip(spans[0, t] + j - since, 0, MOST_PAIRS - 1)
            more = kv_products[pair, n % 4].astype(F32)
            total += jnp.where((j + k < TILES) & (since <= j), more, jnp.zeros_like(more))
        return total.astype(BF16)

    def part_copy(source):
        return copy_to(
            give.at[source], part.at[source], part_send.at[source], part_recv.at[source], partner, s
        )

    def dkv_copy(source):
        return copy_to(
            summed.at[source], dkv_home.at[z, half, c], dkv_send.at[source], dkv_recv.at[me], to_batch, source
        )

    @pl.loop(0, SEQ + 2)
    def _(i):
        @pl.when(i < SEQ)
        def _():
            source = lax.rem(s + i, SEQ)
            wanted = jnp.concatenate([ids_in[source, m : m + 1, :] for m in range(3)], axis=1)
            grads = jnp.concatenate([block_grad(tables[4, source * 3 + m]) for m in range(3)], axis=1)
            made = dot_nt(slot_onehot(wanted), grads).astype(BF16)
            own[source] = jnp.where(c == 0, made[:HALF], made[HALF:])
            give[source] = jnp.where(c == 0, made[HALF:], made[:HALF])
            part_copy(source).start()

        @pl.when(i >= 2)
        def _():
            source = lax.rem(s + i - 2, SEQ)
            arrived(part.at[source], part_recv.at[source])
            summed[source] = (own[source].astype(F32) + part[source].astype(F32)).astype(BF16)
            start(
                is_here(source), summed.at[source], dkv_home.at[z, half, c], dkv_recv.at[me], dkv_copy(source)
            )

    tokens = dot_tn(onehot, in2[...])
    slot_cot = dot_nn(onehot, cot[...])
    item_slope = silu_slope(dot_nn(feats[...], item_weight[...]))
    for first_column in range(0, 4 * WIDTH, WIDTH):
        cols = slice(first_column, first_column + WIDTH)
        pre[:, cols] = silu_slope(pre[:, cols])

    @pl.loop(0, SEQ)
    def _(w):
        arrived(mixed_home.at[w % 4, :, ((w // 4) % 2) * 2 + w // 8], mixed_recv.at[w])

    mixed = jnp.concatenate([mixed_home[h].reshape(ROWS, HEAD) for h in range(HEADS)], axis=1)
    normed_mid = normalize(mixed.astype(F32))[0] * gain_mid[...]
    gated = (normed_mid * gate_of[...]).astype(BF16)
    layer_out[...] = (tokens + dot_nn(gated, w_out[...])).astype(BF16)
    d_gate = dot_nn(onehot, (d_gated_of[...].astype(F32) * normed_mid).astype(BF16))
    d_pre[...] = (d_gate * pre[:, 0:WIDTH]).astype(BF16)
    d_normed = dot_nt(d_pre[...], w_in[:, 0:WIDTH])

    @pl.loop(0, SEQ)
    def _(w):
        arrived(dq_home.at[w % 4, :, ((w // 4) % 2) * 2 + w // 8], dq_recv.at[w])

    d_query = jnp.concatenate([dq_home[h].reshape(ROWS, HEAD) for h in range(HEADS)], axis=1)
    d_pre[...] = (dot_nn(onehot, d_query) * pre[:, 1024:1536]).astype(BF16)
    d_normed += dot_nt(d_pre[...], w_in[:, 1024:1536])

    @pl.loop(0, SEQ)
    def _(w):
        arrived(dkv_home.at[w % 4, (w // 4) % 2, w // 8], dkv_recv.at[w])

    for lanes, first_column in ((0, 1536), (HEAD, 512)):
        cols = slice(first_column, first_column + WIDTH)
        grad = jnp.concatenate(
            [
                dkv_home[h, 0, :, :, lanes : lanes + HEAD].reshape(SLOTS, HEAD).astype(F32)
                + dkv_home[h, 1, :, :, lanes : lanes + HEAD].reshape(SLOTS, HEAD).astype(F32)
                for h in range(HEADS)
            ],
            axis=1,
        )
        d_pre[...] = (grad * pre[:, cols]).astype(BF16)
        d_normed += dot_nt(d_pre[...], w_in[:, cols])

    scaled = d_normed * gain_in[...]
    normal = normal_of[...]
    d_slots = slot_cot + inverse_of[:, 0:1] * (
        scaled
        - jnp.mean(scaled, axis=-1, keepdims=True)
        - normal * jnp.mean(scaled * normal, axis=-1, keepdims=True)
    )
    back2[...] = d_slots.astype(BF16)
    wait_all(exchange_seq(back2, home2, back2_send, back2_recv, b, s))
    back1[...] = dot_nn(by_batch(), home2[...]).astype(BF16)
    last = exchange_batch(back1, home1, back1_send, back1_recv, b, s)
    wanted = (iota((256, 256), 0) == send_rows[...]).astype(BF16)
    wait_all(last)
    d_embedded = dot_nn(wanted, home1[...])
    d_item_out[...] = (d_embedded * item_slope).astype(BF16)

    def finish(w, head, half, core, to_batch, to_seq, here):
        @pl.when(jnp.logical_not(here))
        def _():
            ids_copy(w, to_batch, to_seq).wait_send()
            kv_copy(w, head, core, to_batch, to_seq).wait_send()
            piece_copy(q, q_in, q_send, q_recv, w, head, half, core, to_batch, to_seq).wait_send()
            piece_copy(p, p_in, p_send, p_recv, w, head, half, core, to_batch, to_seq).wait_send()

    each_worker(finish)

    @pl.loop(0, SEQ)
    def _(source):
        pass_on(source).wait_send()
        part_copy(source).wait_send()

        @pl.when(jnp.logical_not(is_here(source)))
        def _():
            home_copy(mixed_slots, mixed_home, mixed_send, mixed_recv, source).wait_send()
            home_copy(dq_slots, dq_home, dq_send, dq_recv, source).wait_send()
            dkv_copy(source).wait_send()


def tables_of(meta, quarter):
    slot, lane = iota((128, 128), 0), iota((1, 128), 1)
    held = jnp.transpose(jnp.broadcast_to(meta[3:4, :], (128, 128)))
    slot_of = jnp.where((held == iota((128, 128), 1)) & (slot < BLOCKS), slot, 0)
    slot_of = jnp.minimum(jnp.sum(slot_of, axis=0, keepdims=True), BLOCKS - 1)
    first = jnp.zeros((1, 1), jnp.int32)
    start_of = jnp.zeros((1, 128), jnp.int32)
    limit_of = jnp.full((1, 128), BLOCK, jnp.int32)
    for u in range(4):
        start_of = jnp.where(lane >= first, first, start_of)
        first = first + meta[4:5, u : u + 1]
        limit_of = jnp.where(lane == first - 1, meta[5:6, u : u + 1], limit_of)
    start_of = jnp.where(lane < BLOCKS, start_of, NO_BLOCK)
    row = iota((8, 128), 0)
    picked = pick4(row, [slot_of, start_of, limit_of, jnp.zeros((1, 128), jnp.int32) + quarter])
    return jnp.where(row == 4, meta[3:4, :], picked)


def pick4(index, values):
    return jnp.where(index == 0, values[0], jnp.where(index == 1, values[1], jnp.where(index == 2, values[2], values[3])))


def first_chunk(meta, t):
    return jnp.clip(meta[1, 4 * t] // 4, 0, TILES - 1)


def walk(meta, t, j, count):
    pairs = []
    for _ in range(count):
        pairs.append((t, j))
        more = j < jnp.minimum(t, TILES - 1)
        after = jnp.minimum(t + 1, TILES)
        j = jnp.where(more, j + 1, first_chunk(meta, after))
        t = jnp.where(more, t, after)
    return pairs, t, j


def pairs_in_all(meta):
    return sum(t + 1 - meta[1, 4 * t] // 4 for t in range(TILES))


def four(ref, meta, n):
    return jnp.concatenate([ref[meta[0, 4 * n + i]] for i in range(4)], axis=0)


def visible(meta, t, j):
    r, lane = iota((BLOCK, 1), 0), iota((1, BLOCK), 1)
    at = (t * 4 + (r >> 5)) * BLOCK + meta[3, 0] * PIECE + (r & 31)
    since = pick4(r >> 5, [meta[1, t * 4 + i] for i in range(4)]) * BLOCK
    where = jnp.concatenate(
        [jnp.where(lane < meta[2, j * 4 + i], (j * 4 + i) * BLOCK + lane, FAR) for i in range(4)], axis=1
    )
    where, at, since = (v.astype(jnp.int16) for v in (where, at, since))
    return (where <= at) & (where >= since)


def result_kernel(layer, d_item, item_weight, layer_out, item_grad):
    layer_out[...] = layer[...]
    item_grad[...] = dot_nt(d_item[...], item_weight[...])


def spec(space):
    return pl.BlockSpec(memory_space=space)


VMEM, SMEM, ANY = pltpu.VMEM, pltpu.SMEM, pl.ANY
DMA = pltpu.SemaphoreType.DMA


def shape(dims, dtype):
    return jax.ShapeDtypeStruct(dims, dtype)


def params(remote=None):
    return pltpu.CompilerParams(
        vmem_limit_bytes=56 << 20, has_side_effects=remote is not None, collective_id=remote
    )


def per_device(
    item_feats, item_weight, send_rows, event_slot, user_blocks, tail_len, block_order, gain_in, gain_mid, w_in, w_out,
    cot_out,
):
    gain_in, gain_mid = gain_in.reshape(1, WIDTH), gain_mid.reshape(1, WIDTH)
    wide = VMEM((256, WIDTH), BF16)
    pieces = VMEM((BLOCKS, PIECE, HEAD), BF16)
    by_head = VMEM((HEADS, 3, 4, PIECE, HEAD), BF16)
    tiles = VMEM((TILES + 1, BLOCK, HEAD), BF16)
    each, one = DMA((SEQ,)), DMA((GROUPS,))
    layer, d_item = pl.pallas_call(
        layer_kernel,
        out_shape=(shape((ROWS, WIDTH), BF16), shape((256, WIDTH), BF16)),
        in_specs=[spec(VMEM)] * 9 + [spec(ANY)] * 3,
        out_specs=(spec(VMEM), spec(VMEM)),
        scratch_shapes=[
            VMEM((WIDTH, 4 * WIDTH), BF16),
            VMEM((WIDTH, WIDTH), BF16),
            VMEM((ROWS, WIDTH), BF16),
            wide,
            wide,
            wide,
            wide,
            VMEM((HEADS, 2, HALF, 2 * HEAD), BF16),
            by_head,
            by_head,
            VMEM((8, 128), jnp.int32),
            VMEM((SEQ, 8, 128), jnp.int32),
            VMEM((SEQ, 2, HALF, 2 * HEAD), BF16),
            VMEM((BLOCKS, BLOCK, 2 * HEAD), BF16),
            pieces,
            pieces,
            VMEM((8, 128), jnp.int32),
            SMEM((8, 128), jnp.int32),
            SMEM((2, 16), jnp.int32),
            VMEM((MOST_PAIRS, BLOCK, HEAD), F32),
            VMEM((MOST_PAIRS, 4, 2 * HEAD, BLOCK), BF16),
            VMEM((HEADS, TILES // 2, 8, BLOCK), F32),
            VMEM((TILES, BLOCK, HEAD), F32),
            pieces,
            pieces,
            pieces,
            pieces,
            by_head,
            by_head,
            tiles,
            tiles,
            tiles,
            VMEM((SEQ, HALF, 2 * HEAD), BF16),
            VMEM((SEQ, HALF, 2 * HEAD), BF16),
            VMEM((SEQ, HALF, 2 * HEAD), BF16),
            VMEM((SEQ, HALF, 2 * HEAD), BF16),
            VMEM((HEADS, 2, 2, HALF, 2 * HEAD), BF16),
            VMEM((SLOTS, 4 * WIDTH), F32),
            VMEM((SLOTS, WIDTH), BF16),
            VMEM((ROWS, WIDTH), F32),
            VMEM((ROWS, WIDTH), BF16),
            VMEM((SLOTS, WIDTH), F32),
            VMEM((SLOTS, 128), F32),
            wide,
            wide,
            wide,
            wide,
            DMA((3,)),
            DMA,
            one,
            one,
            *([each] * 12),
            DMA((HEADS,)),
            DMA((HEADS,)),
            *([each] * 4),
            *([each] * 6),
            one,
            one,
        ],
        compiler_params=params(0),
        name="layer",
    )(
        item_feats, item_weight, send_rows, event_slot, user_blocks, tail_len, block_order, gain_in, gain_mid, w_in,
        w_out, cot_out,
    )
    return pl.pallas_call(
        result_kernel,
        out_shape=(shape((ROWS, WIDTH), BF16), shape((256, WIDTH), F32)),
        in_specs=[spec(VMEM)] * 3,
        out_specs=(spec(VMEM), spec(VMEM)),
        compiler_params=params(),
        name="results",
    )(layer, d_item, item_weight)


def solution(mesh):
    rows = P(("batch", "seq"), None)
    return jax.shard_map(
        per_device,
        mesh=mesh,
        in_specs=(
            rows,
            P(),
            rows,
            P(("batch", "seq")),
            P("batch", None),
            P("batch", None),
            P("batch", None),
            P(),
            P(),
            P(),
            P(),
            rows,
        ),
        out_specs=(rows, rows),
        check_vma=False,
    )
```
